32 devices in a mesh: section: 2 (over core), expert: 16 (over z, y, x).
Axes of the slice: x: 2, y: 2, z: 4, core: 2. Of those that a mesh axis runs over, the one named last changes fastest.
Arguments:
- inputs: bfloat16 [2, 2, 2048, 512], P('section', None, 'expert'), may hold values from -6 to 6
- cotangent: bfloat16 [2, 2, 2048, 512], P('section', None, 'expert'), may hold values from -6 to 6
- segments: int32 [2, 2, 2048], P('section', None, 'expert'), may hold values from 0 to 63, never falling along the last dimension, each value on 1 to 128 neighbouring positions
- tasks: int32 [2, 2, 2048, 1], P('section', None, 'expert'), may hold values from 0 to 7; in each aligned block of 128 rows (0 to 127, 128 to 255, ..., all dimensions but the last counted through in order) at most 48 rows name the same one
- table: int32 [2, 8, 2], P('section'), may hold values from 0 to 15, as said below
- capacity: int32 [2], P('section'), may hold values from 192 to 256, as said below
- gains: float32 [2, 3, 512], P('section'), may hold values from 0.1 to 1.9
- w_qkv: bfloat16 [2, 512, 1536], P('section'), may hold values from -0.25 to 0.25
- w_out: bfloat16 [2, 512, 512], P('section'), may hold values from -0.75 to 0.75
- w_cross: bfloat16 [2, 512, 1024], P('section')
- w_router: bfloat16 [2, 512, 16], P('section'), may hold values from -0.1875 to 0.1875
- w_up: bfloat16 [2, 16, 512, 2048], P('section', 'expert'), may hold values from -0.25 to 0.25
- w_down: bfloat16 [2, 16, 2048, 512], P('section', 'expert'), may hold values from -0.125 to 0.125
Outputs:
- layer_out: bfloat16 [2, 2, 2048, 512], P('section', None, 'expert')
- inputs_grad: float32 [2, 2, 2048, 512], P('section', None, 'expert')
- gains_grad: float32 [2, 3, 512], P('section')
- w_qkv_grad: float32 [2, 512, 1536], P('section')
- w_out_grad: float32 [2, 512, 512], P('section')
- w_cross_grad: float32 [2, 512, 1024], P('section')
- w_router_grad: float32 [2, 512, 16], P('section')
- w_up_grad: float32 [2, 16, 512, 2048], P('section', 'expert')
- w_down_grad: float32 [2, 16, 2048, 512], P('section', 'expert')
The draws below stay inside these ranges and needn't reach their ends.
Inputs may be any that keep to these rules, and one draw needn't show every extreme that they name: `tasks`: in each device's rows of one micro-batch (aligned blocks of 128 tokens) no task occurs more than 48 times, and some task occurs exactly that often. `table`: for each layer every expert belongs to exactly one task, and a task's two experts differ. One of the two layers has capacity 256.
All inputs are finite; a program needn't handle non-finite values.
Results may differ from the reference program's by a relative error of at most 0.015.
Values may be sent and summed in bfloat16 or wider, within the bound.
A program may use at most 192 MiB of HBM per device.

```python
import math
import jax
import jax.numpy as jnp
import numpy as np
from jax import lax

D = 512
HEADS = 8
F = 2048
TOK_DEV = 128
MICRO = 2
EXPERTS = 16
TASKS = 8
SEND = 48
CAP = 256
TOKENS = 2048


def draw_table(key, part):
    key = jax.random.fold_in(key, 7)
    first_layer = jax.random.permutation(jax.random.fold_in(key, 1), EXPERTS).reshape(TASKS, 2)
    second_layer = jax.random.permutation(jax.random.fold_in(key, 2), EXPERTS).reshape(TASKS, 2)
    return jnp.stack([first_layer, second_layer]).astype(jnp.int32)


def draw_capacity(key, part):
    key = jax.random.fold_in(key, 11)
    chosen_layer = jax.random.randint(jax.random.fold_in(key, 1), (), 0, 2)
    other_values = jax.random.randint(jax.random.fold_in(key, 2), (2,), 3 * CAP // 4, CAP + 1)
    return jnp.where(jnp.arange(2) == chosen_layer, CAP, other_values).astype(jnp.int32)


def draw_w_cross(key, part):
    key = jax.random.fold_in(key, 5)
    entries = jax.random.normal(key, (2, D, 2 * D), jnp.float32)
    layer_ids = jnp.arange(2)[:, None, None]
    columns = jnp.arange(2 * D)[None, None, :]
    boost = jnp.where((layer_ids == 1) & (columns >= D), 8.0 ** 0.5, 1.0)
    return (entries * boost * D ** (-0.5)).astype(jnp.bfloat16)


def steps_of(own_key, shape, pieces, low, high):
    def one(axis_at, blocks):
        steps = jax.random.uniform(jax.random.fold_in(jax.random.fold_in(own_key, 6), axis_at), (blocks,), jnp.float32, low / len(pieces), high / len(pieces))
        return jnp.repeat(jnp.exp(steps), shape[axis_at] // blocks).reshape((-1,) + (1,) * (len(shape) - axis_at - 1))

    loudness = one(*pieces[0])
    for cut in pieces[1:]:
        loudness = loudness * one(*cut)
    return loudness


def length_profile(count, total, reach, skew):
    portions = [(1 << 20) // math.isqrt(grade ** skew) + 1 for grade in range(2, count + 1)]
    surplus, counts = total - reach - (count - 1), [1] * (count - 1)
    while surplus > 0:
        candidates = [i for i in range(count - 1) if counts[i] < reach]
        whole, left = sum([portions[i] for i in candidates]), surplus
        for i in candidates:
            more = min(reach - counts[i], max(1, left * portions[i] // whole), surplus)
            counts[i] = counts[i] + more
            surplus = surplus - more
    return np.array([reach] + counts)


def uneven_parts(stream_key, number_of, total, most, slope):
    if number_of == 2:
        one = jax.random.randint(stream_key, (), max(1, total - most), min(most, total - 1) + 1)
        return jnp.stack([one, total - one])
    lengths = jnp.asarray(length_profile(number_of, total, most, slope), jnp.int32)
    twos = (number_of - 1) // 2
    source_of, sink = lengths[1:1 + 2 * twos:2], lengths[2:2 + 2 * twos:2]
    slack = jnp.minimum(source_of - 1, most - sink)
    shifted = jax.random.randint(jax.random.fold_in(stream_key, 1), (twos,), 0, 1 << 20) % (slack + 1)
    lengths = lengths.at[1:1 + 2 * twos:2].set(source_of - shifted).at[2:2 + 2 * twos:2].set(sink + shifted)
    return lengths[jax.random.permutation(jax.random.fold_in(stream_key, 2), number_of)]


def shared_out(own_key, own, number, rows, number_of, top, reach, lean):
    sequence = jax.random.permutation(own_key, number_of)
    crowded, ordinary = load_shares(number_of, rows * top, reach, lean, True), load_shares(number_of, rows * top, reach, lean, False)
    places = jnp.arange(number_of)

    def named(sizes, turn):
        used = int((sizes > 0).sum())
        fixed = max(1, used // 4)
        moved = fixed + (places - fixed + turn * (used - fixed)) % max(1, number_of - fixed)
        return jnp.zeros((number_of,), jnp.int32).at[sequence[jnp.where(places < fixed, places, moved)]].set(jnp.asarray(sizes, jnp.int32))

    sizes = jnp.where(number % 4 == 0, named(crowded, number // 4), named(ordinary, number - number // 4 - 1))
    mixed = jax.random.permutation(jax.random.fold_in(own, 3), number_of)
    giver, sink = mixed[0:number_of // 2 * 2:2], mixed[1:number_of // 2 * 2:2]
    margin = jnp.minimum(sizes[giver] - 1, reach - sizes[sink]) // 2
    margin = jnp.where((giver == sequence[0]) | (sink == sequence[0]) | (sizes[sink] == 0), 0, jnp.maximum(margin, 0))
    moved = jax.random.randint(jax.random.fold_in(own, 4), (number_of // 2,), 0, 1 << 20) % (margin + 1)
    sizes = sizes.at[giver].add(-moved).at[sink].add(moved)
    labels = jnp.searchsorted(jnp.cumsum(sizes), jnp.arange(rows * top), side="right").astype(jnp.int32)
    grid = labels.reshape(top, rows).T
    grid = grid[jax.random.permutation(jax.random.fold_in(own, 1), rows)]
    turn = jax.random.randint(jax.random.fold_in(own, 2), (rows, 1), 0, top)
    return jnp.take_along_axis(grid, (jnp.arange(top)[None, :] + turn) % top, axis=1)


def load_shares(amount, total, most, skew, full):
    weights = [(1 << 20) // math.isqrt(grade ** skew) + 1 for grade in range(1, amount + 1)]
    largest = most if full else min(most, max(-(-total // amount), total * weights[0] // sum(weights)))
    least = 1 if total - largest >= amount - 1 else 0
    holding, spare = [largest] + [least] * (amount - 1), total - largest - least * (amount - 1)
    while spare > 0:
        movable = [i for i in range(1, amount) if holding[i] < largest] or [i for i in range(1, amount) if holding[i] < most]
        mass, left = sum([weights[i] for i in movable]), spare
        for i in movable:
            addition = min(most - holding[i], max(1, left * weights[i] // mass), spare)
            holding[i] = holding[i] + addition
            spare = spare - addition
    return np.array(holding)


def noise(stream_key, dims, deviation, limit, pieces=(), held_as=jnp.bfloat16):
    result = jax.random.normal(stream_key, dims, jnp.float32) * deviation
    if len(pieces) > 0:
        result = steps_of(stream_key, dims, pieces, -0.22, 0.18) * result
    return jnp.clip(result, min=-limit, max=limit).astype(held_as)


def setup_inputs(seed: int = 0) -> dict:
    seeds = jax.random.split(jax.random.key(seed), 14)
    inputs = noise(seeds[0], (2, MICRO, TOKENS, D), 1.0, 6.0, ((0, 2), (2, 16)))
    cotangent = noise(seeds[1], (2, MICRO, TOKENS, D), 1.0, 6.0, ((0, 2), (2, 16)))
    segments = jax.vmap(lambda own: jnp.searchsorted(jnp.cumsum(uneven_parts(own, TOKENS * 4 // TOK_DEV, TOKENS, TOK_DEV, 2)), jnp.arange(TOKENS), side="right"))(jax.random.split(seeds[2], 2 * MICRO)).reshape((2, MICRO, TOKENS)).astype(jnp.int32)
    tasks_keys = jax.random.split(jax.random.fold_in(seeds[3], 1), 2 * MICRO * TOKENS // TOK_DEV)
    tasks_turns = jax.random.permutation(jax.random.fold_in(seeds[3], 3), 2 * MICRO * TOKENS // TOK_DEV)
    tasks = jax.vmap(lambda own, number: shared_out(jax.random.fold_in(seeds[3], 2), own, number, TOK_DEV, TASKS, 1, SEND, 4))(tasks_keys, tasks_turns).reshape((2, MICRO, TOKENS, 1))
    table = draw_table(jax.random.fold_in(seeds[13], 71), 0)
    capacity = draw_capacity(jax.random.fold_in(seeds[13], 71), 0)
    gains = jnp.clip(1.0 + 0.18 * jax.random.normal(seeds[6], (2, 3, D), jnp.float32), 0.1, 1.9)
    w_qkv = noise(seeds[7], (2, D, 3 * D), D ** -0.5, 0.25, ((0, 2),))
    w_out = noise(seeds[8], (2, D, D), (D // 8) ** -0.5, 0.75, ((0, 2),))
    w_cross = draw_w_cross(jax.random.fold_in(seeds[13], 71), 0)
    w_router = noise(seeds[10], (2, D, EXPERTS), (2 * D) ** -0.5, 0.1875, ((0, 2),))
    w_up = noise(seeds[11], (2, EXPERTS, D, F), D ** -0.5, 0.25, ((0, 2), (1, 16)))
    w_down = noise(seeds[12], (2, EXPERTS, F, D), F ** -0.5, 0.125, ((0, 2), (1, 16)))
    return {"inputs": inputs, "cotangent": cotangent, "segments": segments, "tasks": tasks, "table": table, "capacity": capacity, "gains": gains, "w_qkv": w_qkv, "w_out": w_out, "w_cross": w_cross, "w_router": w_router, "w_up": w_up, "w_down": w_down}


@jax.custom_vjp
def low(v):
    return lax.optimization_barrier(v.astype(jnp.bfloat16)).astype(jnp.float32)

@jax.custom_vjp
def low_back(v):
    return v

def low_keep(v):
    return (low(v), None)

def low_pass(kept, grad):
    return (grad,)

def back_keep(v):
    return (v, None)

def back_low(kept, grad):
    return (low(grad),)
low.defvjp(low_keep, low_pass)
low_back.defvjp(back_keep, back_low)
EPSILON = 1e-06

def rms_norm(value, gain):
    return value * lax.rsqrt(lax.optimization_barrier(jnp.mean(value * value, axis=-1, keepdims=True)) + EPSILON) * gain

def product(left, right):
    return jnp.dot(left, right, precision=lax.Precision.HIGHEST)

def attend(queries, key_heads, value_heads, allowed):
    score_scale = queries.shape[-1] ** (-0.5)
    raw_scores = jnp.einsum('qhd,khd->hqk', queries, key_heads, precision=lax.Precision.HIGHEST)
    scores = low_back(raw_scores * score_scale)
    attn_probs = jax.nn.softmax(jnp.where(allowed[None], scores, -1000000000.0), axis=-1)
    return jnp.einsum('hqk,khd->qhd', low(attn_probs), value_heads, precision=lax.Precision.HIGHEST)

def self_block(inputs_now, seg_now, gain, qkv_weight, out_weight, causal):
    tok_rows, model_width = inputs_now.shape
    pack_count = tok_rows // TOK_DEV
    head_size = model_width // HEADS
    qkv_rows = low(low_back(product(low(rms_norm(inputs_now, gain)), qkv_weight)))
    head_packs = qkv_rows.reshape(pack_count, TOK_DEV, 3, HEADS, head_size)
    seg_packs = seg_now.reshape(pack_count, TOK_DEV)
    positions = jnp.arange(TOK_DEV, dtype=jnp.int32)
    earlier = positions[None, :] <= positions[:, None]

    def one_pack(packed):
        head_block, seg_block = packed
        allowed = seg_block[:, None] == seg_block[None, :]
        if causal:
            allowed = allowed & earlier
        return attend(head_block[:, 0], head_block[:, 1], head_block[:, 2], allowed)
    mixed_rows = lax.map(jax.checkpoint(one_pack), (head_packs, seg_packs))
    attn_rows = low(low_back(mixed_rows.reshape(tok_rows, model_width)))
    return inputs_now + low_back(product(attn_rows, out_weight))

def cross_block(after_self, memory, gain, cross_weight):
    tok_rows, model_width = after_self.shape
    pack_count = tok_rows // TOK_DEV
    head_size = model_width // HEADS
    cross_q = low(low_back(product(low(rms_norm(after_self, gain)), cross_weight[:, :model_width])))
    query_packs = cross_q.reshape(pack_count, TOK_DEV, HEADS, head_size)
    key_packs = memory[:, :model_width].reshape(pack_count, TOK_DEV, HEADS, head_size)
    value_packs = memory[:, model_width:].reshape(pack_count, TOK_DEV, HEADS, head_size)
    all_keys = jnp.ones((TOK_DEV, TOK_DEV), jnp.bool_)

    def one_pack(packed):
        return attend(packed[0], packed[1], packed[2], all_keys)
    mixed_rows = lax.map(jax.checkpoint(one_pack), (query_packs, key_packs, value_packs))
    cross_rows = low(low_back(mixed_rows.reshape(tok_rows, model_width)))
    return after_self + low_back(product(cross_rows, cross_weight[:, model_width:].T))

def gate_values(normed, router, expert_pick):
    logits = jnp.dot(normed, router, precision=lax.Precision.HIGHEST)
    chosen = jnp.take_along_axis(logits, expert_pick, axis=1)
    return jax.nn.softmax(chosen, axis=-1)

def moe_block(after_cross, task_now, table_now, cap_now, gain, router, up_weight, down_weight):
    tok_rows, model_width = after_cross.shape
    expert_count = up_weight.shape[0]
    normed = low(rms_norm(after_cross, gain))
    expert_pick = table_now[task_now]
    gate_now = gate_values(normed, router, expert_pick)
    flat_pick = expert_pick.reshape(-1)
    onehot = (flat_pick[:, None] == jnp.arange(expert_count, dtype=jnp.int32)[None, :]).astype(jnp.int32)
    slot = lax.optimization_barrier(jnp.sum((jnp.cumsum(onehot, axis=0) - onehot) * onehot, axis=1))
    kept = slot < cap_now
    target = jnp.where(kept, flat_pick * CAP + slot, expert_count * CAP)
    order_rows = jnp.zeros((expert_count * CAP + 1,), jnp.int32).at[target].set(jnp.arange(2 * tok_rows, dtype=jnp.int32))[:expert_count * CAP]
    filled = jnp.zeros((expert_count * CAP + 1,), jnp.float32).at[target].set(1.0)[:expert_count * CAP]
    copies = jnp.stack([low_back(normed), low_back(normed)], axis=1).reshape(2 * tok_rows, model_width)
    slot_rows = (copies[order_rows] * filled[:, None]).reshape(expert_count, CAP, model_width)

    def one_expert(packed):
        rows_now, up_now, down_now = packed
        hidden = low_back(product(rows_now, up_now))
        act = low(jax.nn.gelu(hidden))
        return low(low_back(product(act, down_now)))
    expert_rows = lax.map(jax.checkpoint(one_expert), (slot_rows, up_weight, down_weight))
    expert_rows = expert_rows.reshape(expert_count * CAP, model_width)
    returned = expert_rows[jnp.where(kept, target, 0)] * kept.astype(jnp.float32)[:, None]
    returned = returned.reshape(tok_rows, 2, model_width)
    return after_cross + lax.optimization_barrier(jnp.sum(gate_now[:, :, None] * returned, axis=1))

def run_layer(layer_index, inputs_now, seg_now, task_now, table_now, cap_now, gains_now, qkv_weight, out_weight, cross_weight, router, up_weight, down_weight, memory):
    after_self = self_block(inputs_now, seg_now, gains_now[0], qkv_weight, out_weight, layer_index == 1)
    if memory is None:
        after_cross = after_self
    else:
        after_cross = cross_block(after_self, memory, gains_now[1], cross_weight)
    return moe_block(after_cross, task_now, table_now, cap_now, gains_now[2], router, up_weight, down_weight)

def reference(inputs, cotangent, segments, tasks, table, capacity, gains, w_qkv, w_out, w_cross, w_router, w_up, w_down):

    def forward(inputs_f, gains_f, qkv_f, out_f, cross_f, router_f, up_f, down_f):
        results = []
        for micro_step in range(MICRO):
            encoded = run_layer(0, inputs_f[0, micro_step], segments[0, micro_step], tasks[0, micro_step, :, 0], table[0], capacity[0], gains_f[0], qkv_f[0], out_f[0], cross_f[0], router_f[0], up_f[0], down_f[0], None)
            memory = low(low_back(product(low(rms_norm(encoded, gains_f[0, 1])), cross_f[0])))
            decoded = run_layer(1, inputs_f[1, micro_step], segments[1, micro_step], tasks[1, micro_step, :, 0], table[1], capacity[1], gains_f[1], qkv_f[1], out_f[1], cross_f[1], router_f[1], up_f[1], down_f[1], memory)
            results.append(jnp.stack([encoded, decoded]))
        return jnp.stack(results, axis=1)
    layer_out, pullback = jax.vjp(forward, inputs.astype(jnp.float32), gains, w_qkv.astype(jnp.float32), w_out.astype(jnp.float32), w_cross.astype(jnp.float32), w_router.astype(jnp.float32), w_up.astype(jnp.float32), w_down.astype(jnp.float32))
    grads = pullback(cotangent.astype(jnp.float32))
    return (layer_out.astype(jnp.bfloat16), grads[0], grads[1], grads[2], grads[3], grads[4], grads[5], grads[6], grads[7])
```

```python
import math
from types import SimpleNamespace

import jax
import jax.numpy as jnp
from jax import lax
from jax.experimental import pallas as pl
from jax.experimental.pallas import tpu as pltpu
from jax.sharding import PartitionSpec as P

HEADS = 8
EPSILON = 1e-06
LANES = 128
MESH = pl.DeviceIdType.MESH
F32 = jnp.float32
BF16 = jnp.bfloat16

SEG, TASK, TABLE, CAPACITY = (0, 2, 4, 5)
INFO_TASK, INFO_RANK, INFO_COUNT = (0, 2, 4)


def round_up(value, unit):
    return -(-value // unit) * unit


def dot(left, right):
    return jnp.dot(left, right, preferred_element_type=F32)


def dot_rows(left, right):
    return lax.dot_general(left, right, (((0,), (0,)), ((), ())), preferred_element_type=F32)


def dot_cols(left, right):
    return lax.dot_general(left, right, (((1,), (1,)), ((), ())), preferred_element_type=F32)


def lane_sum(value):
    return jnp.sum(value, axis=-1, keepdims=True)


def row_sum(value):
    return jnp.sum(value, axis=0, keepdims=True)


def when_equal(left, right, value=1.0):
    return jnp.where(left == right, value, 0.0)


def iota(shape, axis):
    return lax.broadcasted_iota(jnp.int32, shape, axis).astype(F32)


def whole_part(value, unit):
    return jnp.floor((value + 0.5) * (1.0 / unit))


def inverse_rms(value):
    return lax.rsqrt(jnp.mean(value * value, axis=-1, keepdims=True) + EPSILON)


def norm(value, gain):
    return value * inverse_rms(value) * gain


def norm_back(value, gain, grad):
    scale = inverse_rms(value)
    unit = value * scale
    scaled = grad * gain
    grad_value = scale * (scaled - unit * jnp.mean(scaled * unit, axis=-1, keepdims=True))
    return grad_value, row_sum(grad * unit)


def gelu_and_slope(hidden):
    rate = math.sqrt(2.0 / math.pi)
    square = hidden * hidden
    bend = jnp.tanh(hidden * (rate + rate * 0.044715 * square))
    share = 0.5 + 0.5 * bend
    act = hidden * share
    slope = share + act * (1.0 - bend) * (rate + 3.0 * rate * 0.044715 * square)
    return act, slope


class Sizes:
    def __init__(self, inputs, w_qkv, w_cross, w_router, w_up, table, experts):
        _, self.micro, self.tok, self.model = inputs.shape
        self.hidden = w_up.shape[-1]
        self.experts = experts
        self.tasks = table.shape[1]
        self.slots = 2 * self.tok
        self.halves = 2
        self.group = experts // self.halves
        self.bound = max(2, 6 * self.tok // experts)
        self.send = round_up(self.bound, 16)
        self.merged = self.halves * self.bound <= self.send
        self.flights = 1 if self.merged else self.halves
        self.half_rows = self.group * self.send
        self.all_rows = self.flights * self.half_rows
        self.misc = round_up(w_router.shape[-1] + 3, LANES)
        self.qkv_blocks = w_qkv.shape[-1] // LANES
        self.out_blocks = self.model // LANES
        self.cross_blocks = w_cross.shape[-1] // LANES
        self.misc_blocks = self.misc // LANES
        self.blocks = self.qkv_blocks + self.out_blocks + self.cross_blocks + self.misc_blocks
        self.bits = experts.bit_length() - 1
        unit = 16 * experts
        units = -(-self.blocks * self.model // unit)
        share = -(-units // 3)
        self.parts = []
        start = 0
        for part in range(3):
            size = min(share, units - start // unit) * unit
            self.parts.append((start, size))
            start += size
        self.dense_rows = start


def kernel_body(z, names, *refs):
    r = SimpleNamespace(**dict(zip(names, refs)))
    me = lax.axis_index("expert")
    section = lax.axis_index("section")
    is_dec = section == 1
    tok, model, micro, group, send, slots = (z.tok, z.model, z.micro, z.group, z.send, z.slots)
    here = lax.rem(me, group)
    base = me - here
    mirror = lax.rem(me + group, z.experts)
    me_f = me.astype(F32)
    here_f = here.astype(F32)
    base_f = base.astype(F32)
    enc_f = 1.0 - section.astype(F32)

    def enc(run):
        pl.when(section == 0)(run)

    def dec(run):
        pl.when(section == 1)(run)

    loads = [
        pltpu.make_async_copy(source, target, r.load_sem.at[i])
        for i, (source, target) in enumerate(
            (
                (r.w_qkv, r.wqkv),
                (r.w_out, r.wout),
                (r.w_cross, r.wcross),
                (r.w_up, r.wup),
                (r.w_down, r.wdown),
            )
        )
    ]
    for load in loads:
        load.start()

    barrier = pltpu.get_barrier_semaphore()

    def greet(step, _):
        pl.semaphore_signal(
            barrier,
            inc=1,
            device_id={"expert": lax.rem(me + step, z.experts)},
            device_id_type=MESH,
        )
        return 0

    lax.fori_loop(1, z.experts, greet, 0)
    pl.semaphore_signal(
        barrier, inc=1, device_id={"section": 1 - section}, device_id_type=MESH
    )

    meta = r.meta[...].astype(F32)
    meta_cols = jnp.transpose(
        jnp.concatenate([meta, jnp.zeros((LANES - 8, LANES), F32)], axis=0)
    )
    lane = iota((1, LANES), 1)
    earlier = jnp.where(iota((tok, tok), 0) < iota((tok, tok), 1), 1.0, 0.0)
    task_rows, rank_rows, count_rows = ([], [], [])
    for m in range(micro):
        task_col = meta_cols[:, TASK + m : TASK + m + 1]
        task_row = meta[TASK + m : TASK + m + 1, :]
        task_rows.append(task_row)
        rank_rows.append(row_sum(when_equal(task_col, task_row) * earlier))
        count_rows.append(row_sum(when_equal(task_col, lane)))
    r.infos[0] = jnp.concatenate(
        task_rows + rank_rows + count_rows + [jnp.zeros((8 - 3 * micro, LANES), F32)], axis=0
    )

    pl.semaphore_wait(barrier, z.experts)

    def tell(step, _):
        pltpu.make_async_remote_copy(
            src_ref=r.infos.at[0],
            dst_ref=r.infos.at[step],
            send_sem=r.info_send,
            recv_sem=r.info_recv,
            device_id={"expert": lax.rem(me + step, z.experts)},
            device_id_type=MESH,
        ).start()
        return 0

    lax.fori_loop(1, z.experts, tell, 0)

    def settle(ref, sem):
        pltpu.make_async_copy(ref, ref, sem).wait()

    low_lane = jnp.where(iota((1, LANES), 1) < LANES // 2, 1.0, 0.0)
    high_lane = 1.0 - low_lane
    low_bf, high_bf = (low_lane.astype(BF16), high_lane.astype(BF16))
    pairs = model // LANES
    score_scale = (model // HEADS) ** (-0.5)

    def stacked(block):
        return jnp.concatenate([block * low_bf, block * high_bf], axis=0)

    def merged(block):
        return block[:tok] * low_lane + block[tok:] * high_lane

    def attend(queries, keys, values, allowed):
        scores = dot_cols(stacked(queries), keys) * score_scale
        if allowed is not None:
            scores = jnp.where(allowed > 0.5, scores, -1000000000.0)
        top = jnp.max(scores, axis=-1, keepdims=True)
        grown = jnp.exp(scores - top)
        probs = grown / lane_sum(grown)
        return probs, merged(dot(probs.astype(BF16), values))

    def attend_back(queries, keys, values, probs, grad_mixed):
        grad_stack = stacked(grad_mixed)
        grad_probs = dot_cols(grad_stack, values)
        inner = lane_sum(probs * grad_probs)
        grad_scores = (probs * (grad_probs - inner)).astype(BF16)
        grad_queries = merged(dot(grad_scores, keys)) * score_scale
        grad_keys = dot_rows(grad_scores, stacked(queries)) * score_scale
        grad_values = dot_rows(probs.astype(BF16), grad_stack)
        return grad_queries, grad_keys, grad_values

    def cols(index, start=0):
        return pl.ds(start + index * LANES, LANES)

    gains = r.gains[...]
    gain_a, gain_c, gain_m = (gains[0:1], gains[1:2], gains[2:3])

    loads[0].wait()
    loads[1].wait()
    for m in range(micro):
        x_in = r.inputs[m].astype(F32)
        normed_a = norm(x_in, gain_a).astype(BF16)
        r.normed_a[m] = normed_a
        r.qkv[m] = dot(normed_a, r.wqkv[...]).astype(BF16)
        seg_col = meta_cols[:, SEG + m : SEG + m + 1]
        seg_row = meta[SEG + m : SEG + m + 1, :]
        causal = jnp.where(iota((tok, tok), 1) <= iota((tok, tok), 0), 1.0, enc_f)
        allowed = when_equal(seg_col, seg_row) * causal
        allowed = jnp.concatenate([allowed, allowed], axis=0)
        for pair in range(pairs):
            probs, mixed = attend(
                r.qkv[m, :, cols(pair)],
                r.qkv[m, :, cols(pair, model)],
                r.qkv[m, :, cols(pair, 2 * model)],
                allowed,
            )
            r.probs_self[m, pair] = probs
            r.attn_rows[m, :, cols(pair)] = mixed.astype(BF16)
        r.after_self[m] = x_in + dot(r.attn_rows[m], r.wout[...])

    settle(r.infos.at[pl.ds(1, z.experts - 1)], r.info_recv)
    table_row = meta[TABLE : TABLE + 1, :]
    table_task = whole_part(lane, 2)
    own_task = lane_sum(when_equal(table_row, me_f, table_task))
    partner = lane_sum(jnp.where((table_task == own_task) & (table_row >= 0.0), table_row, 0.0)) - me_f
    capacity = meta[CAPACITY : CAPACITY + 1, 0:1]

    line = iota((z.half_rows, 1), 0)
    line_block = whole_part(line, send)
    line_rank = line - line_block * send
    line_place = here_f + line_block
    line_place = jnp.where(line_place >= group, line_place - group, line_place)
    line_task = lane_sum(when_equal(table_row, base_f + line_place, table_task))

    place = iota((1, z.all_rows), 1)
    block = whole_part(place, send)
    place_rank = place - block * send
    place_half = whole_part(block, group)
    sender = here_f - (block - place_half * group)
    if z.merged:
        place_half = jnp.minimum(whole_part(place_rank, z.bound), 1.0)
        place_rank = place_rank - place_half * z.bound
    sender = base_f + jnp.where(sender < 0.0, sender + group, sender) + place_half * group
    sender = jnp.where(sender >= z.experts, sender - z.experts, sender)
    teller = me_f - iota((z.experts, 1), 0)
    teller = jnp.where(teller < 0.0, teller + z.experts, teller)
    own_slot = iota((slots, 1), 0)
    for m in range(micro):
        for half in range(z.halves):
            info = r.infos[half * group]
            hit = (info[INFO_TASK + m : INFO_TASK + m + 1] == line_task) & (
                info[INFO_RANK + m : INFO_RANK + m + 1] == line_rank - (half * z.bound if z.merged else 0)
            )
            r.pick[half, m] = jnp.where(hit, 1.0, 0.0).astype(BF16)
        counts = lane_sum(
            jnp.where(lane == own_task, r.infos[:, INFO_COUNT + m, :], 0.0)
        )
        count = row_sum(when_equal(teller, sender, counts))
        slot = row_sum(jnp.where(teller < sender, counts, 0.0)) + place_rank
        slot = jnp.where((place_rank < count) & (slot < capacity), slot, -1.0)
        r.compact[m] = when_equal(own_slot, slot).astype(BF16)

    def spread(way, m, half, rows, back):
        packed, landed = (
            (r.reply_out, r.reply_in) if back else (r.rows_out, r.rows_in)
        )
        send_sem, recv_sem = (
            (r.reply_send, r.reply_recv) if back else (r.rows_send, r.rows_recv)
        )
        packed[way, m, half] = rows.reshape(group, send, model)
        landed[way, m, half, 0] = rows[:send]

        def push(step, _):
            if back:
                other = lax.rem(here + group - step, group)
            else:
                other = lax.rem(here + step, group)
            pltpu.make_async_remote_copy(
                src_ref=packed.at[way, m, half, step],
                dst_ref=landed.at[way, m, half, step],
                send_sem=send_sem.at[way, m, half],
                recv_sem=recv_sem.at[way, m, half],
                device_id={"expert": base + other},
                device_id_type=MESH,
            ).start()
            return 0

        lax.fori_loop(1, group, push, 0)

    def swap(source, target, send_sem, recv_sem):
        return pltpu.make_async_remote_copy(
            src_ref=source,
            dst_ref=target,
            send_sem=send_sem,
            recv_sem=recv_sem,
            device_id={"expert": mirror},
            device_id_type=MESH,
        )

    def swap_rows(way, m, source):
        return swap(
            source.at[m], r.mirror_rows.at[way, m], r.mirror_send.at[way, m], r.mirror_recv.at[way, m]
        )

    def swap_sums(way, m):
        return swap(
            r.sums_out.at[way, m], r.sums_in.at[way, m], r.sums_send.at[way, m], r.sums_recv.at[way, m]
        )

    def dispatch(way, m, source):
        swap_rows(way, m, source).start()
        if not z.merged:
            spread(way, m, 0, dot(r.pick[0, m], source[m]).astype(BF16), False)

    def dispatch_mirror(way, m, source):
        swap_rows(way, m, source).wait_recv()
        rows = dot(r.pick[1, m], r.mirror_rows[way, m])
        if z.merged:
            rows += dot(r.pick[0, m], source[m])
        spread(way, m, z.flights - 1, rows.astype(BF16), False)

    def arrived(way, m):
        for half in range(z.flights):
            settle(r.rows_in.at[way, m, half, pl.ds(1, group - 1)], r.rows_recv.at[way, m, half])
        return dot(r.compact[m], r.rows_in[way, m].reshape(z.all_rows, model))

    def combine(way, m, rows):
        reply = dot_rows(r.compact[m], rows).astype(BF16)
        for half in reversed(range(z.flights)):
            spread(way, m, half, reply[half * z.half_rows : (half + 1) * z.half_rows], True)

    def gathered(way, m, half):
        flight = 0 if z.merged else half
        if not z.merged or half == 1:
            settle(r.reply_in.at[way, m, flight, pl.ds(1, group - 1)], r.reply_recv.at[way, m, flight])
        return dot_rows(r.pick[half, m], r.reply_in[way, m, flight].reshape(z.half_rows, model))

    def combine_mirror(way, m):
        r.sums_out[way, m] = gathered(way, m, 1).astype(BF16)
        swap_sums(way, m).start()

    def combine_end(way, m):
        own = gathered(way, m, 0)
        swap_sums(way, m).wait_recv()
        return own + r.sums_in[way, m].astype(F32)

    @dec
    def _():
        for m in range(micro):
            dispatch(1, m, r.cotangent)
        for m in range(micro):
            dispatch_mirror(1, m, r.cotangent)

    loads[2].wait()

    def memory_copy(m):
        return pltpu.make_async_remote_copy(
            src_ref=r.memory_out.at[m],
            dst_ref=r.memory.at[m],
            send_sem=r.memory_send.at[m],
            recv_sem=r.memory_recv.at[m],
            device_id={"section": 1 - section},
            device_id_type=MESH,
        )

    def grad_memory_copy(m):
        return pltpu.make_async_remote_copy(
            src_ref=r.memory_out.at[m],
            dst_ref=r.memory.at[m],
            send_sem=r.memory_send.at[micro + m],
            recv_sem=r.memory_recv.at[micro + m],
            device_id={"section": 1 - section},
            device_id_type=MESH,
        )

    for m in range(micro):

        @enc
        def _():
            r.after_cross[m] = r.after_self[m]

        @dec
        def _():
            after_self = r.after_self[m]
            normed_c = norm(after_self, gain_c).astype(BF16)
            r.normed_c[m] = normed_c
            r.cross_q[m] = dot(normed_c, r.wcross[:, :model]).astype(BF16)
            memory_copy(m).wait_recv()
            for pair in range(pairs):
                probs, mixed = attend(
                    r.cross_q[m, :, cols(pair)],
                    r.memory[m, :, cols(pair)],
                    r.memory[m, :, cols(pair, model)],
                    None,
                )
                r.probs_cross[m, pair] = probs
                r.cross_rows[m, :, cols(pair)] = mixed.astype(BF16)
            r.after_cross[m] = after_self + dot_cols(r.cross_rows[m], r.wcross[:, model:])

        r.normed_m[m] = norm(r.after_cross[m], gain_m).astype(BF16)
        dispatch(0, m, r.normed_m)
    for m in range(micro):
        dispatch_mirror(0, m, r.normed_m)

    router = r.w_router[...]
    expert_lane = iota((8, router.shape[-1]), 1)
    sign = when_equal(expert_lane, me_f) - when_equal(expert_lane, partner)
    router_step = dot_cols(sign.astype(BF16), router)[0:1]
    tile = 256
    loads[3].wait()
    loads[4].wait()
    for m in range(micro):
        taken = arrived(0, m).astype(BF16)
        r.taken[m] = taken

        def up_tile(index, _):
            at = pl.ds(pl.multiple_of(index * tile, tile), tile)
            hidden = dot(r.taken[m], r.wup[:, at])
            act, slope = gelu_and_slope(hidden)
            r.act[m, :, at] = act.astype(BF16)
            r.slope[m, :, at] = slope.astype(BF16)
            return 0

        lax.fori_loop(0, z.hidden // tile, up_tile, 0)
        gap = lane_sum(taken.astype(F32) * router_step)
        small = jnp.exp(-jnp.abs(gap))
        large = 1.0 / (1.0 + small)
        gate = jnp.where(gap >= 0.0, large, small * large)
        r.gate[m] = gate
        r.gate_slope[m] = small * large * large

        def down_tile(index, _):
            at = pl.ds(pl.multiple_of(index * tile, tile), tile)
            r.expert_out[m, :, at] = dot(r.act[m], r.wdown[:, at]).astype(BF16)
            return 0

        lax.fori_loop(0, model // tile, down_tile, 0)
        r.gated[m] = (gate * r.expert_out[m].astype(F32)).astype(BF16)

        @enc
        def _():
            combine(0, m, r.gated[m])

    @enc
    def _():
        for m in range(micro):
            combine_mirror(0, m)
        for m in range(micro):
            layer_final = r.after_cross[m] + combine_end(0, m)
            r.layer_final[m] = layer_final
            r.layer_out[m] = layer_final.astype(BF16)
            normed_k = norm(layer_final, gain_c).astype(BF16)
            r.normed_c[m] = normed_k
            r.memory_out[m] = dot(normed_k, r.wcross[...]).astype(BF16)
            memory_copy(m).start()
        gain_grad = jnp.zeros((1, model), F32)
        for m in range(micro):
            grad_memory_copy(m).wait_recv()
            grad_normed = dot_cols(r.memory[m], r.wcross[...])
            grad_state, grad_gain = norm_back(r.layer_final[m], gain_c, grad_normed)
            gain_grad += grad_gain
            grad_final = r.cotangent[m].astype(F32) + grad_state
            r.grad_state[m] = grad_final
            r.grad_rows[m] = grad_final.astype(BF16)
            dispatch(1, m, r.grad_rows)
        for m in range(micro):
            dispatch_mirror(1, m, r.grad_rows)
        r.gain_grads[1:2] = gain_grad

    @dec
    def _():
        for m in range(micro):
            r.grad_state[m] = r.cotangent[m].astype(F32)

    for m in range(micro):
        grad_final = arrived(1, m)
        grad_gate = lane_sum(r.expert_out[m].astype(F32) * grad_final)
        grad_gap = r.gate_slope[m] * grad_gate
        r.grad_gap[m] = grad_gap
        r.grad_out[m] = (r.gate[m] * grad_final).astype(BF16)

        def act_tile(index, _):
            at = pl.ds(pl.multiple_of(index * tile, tile), tile)
            grad_act = dot_cols(r.grad_out[m], r.wdown[at, :])
            r.grad_hidden[m, :, at] = (grad_act * r.slope[m, :, at].astype(F32)).astype(BF16)
            return 0

        lax.fori_loop(0, z.hidden // tile, act_tile, 0)

        def taken_tile(index, _):
            at = pl.ds(pl.multiple_of(index * tile, tile), tile)
            r.grad_taken[:, at] = dot_cols(r.grad_hidden[m], r.wup[at, :])
            return 0

        lax.fori_loop(0, model // tile, taken_tile, 0)
        rounded = r.grad_taken[...].astype(BF16).astype(F32)
        combine(1, m, (rounded + grad_gap * router_step).astype(BF16))
    for m in range(micro):
        combine_mirror(1, m)

    @dec
    def _():
        for m in range(micro):
            combine(0, m, r.gated[m])

    gain_grad = jnp.zeros((1, model), F32)
    for m in range(micro):
        grad_state, grad_gain = norm_back(r.after_cross[m], gain_m, combine_end(1, m))
        gain_grad += grad_gain
        r.grad_state[m] += grad_state

        @dec
        def _():
            grad_y = r.grad_state[m].astype(BF16)
            r.grad_cross[m] = grad_y
            grad_mix = dot(grad_y, r.wcross[:, model:]).astype(BF16)
            for pair in range(pairs):
                at = cols(pair)
                grad_q, grad_k, grad_v = attend_back(
                    r.cross_q[m, :, at],
                    r.memory[m, :, at],
                    r.memory[m, :, cols(pair, model)],
                    r.probs_cross[m, pair],
                    grad_mix[:, pair * LANES : (pair + 1) * LANES],
                )
                r.grad_cross_q[m, :, at] = grad_q.astype(BF16)
                r.memory_out[m, :, at] = grad_k.astype(BF16)
                r.memory_out[m, :, cols(pair, model)] = grad_v.astype(BF16)
            grad_memory_copy(m).start()

    r.gain_grads[2:3] = gain_grad

    @dec
    def _():
        gain_grad = jnp.zeros((1, model), F32)
        for m in range(micro):
            grad_normed = dot_cols(r.grad_cross_q[m], r.wcross[:, :model])
            grad_state, grad_gain = norm_back(r.after_self[m], gain_c, grad_normed)
            gain_grad += grad_gain
            r.grad_state[m] += grad_state
        r.gain_grads[1:2] = gain_grad
        for m in range(micro):
            combine_mirror(0, m)
        for m in range(micro):
            r.layer_out[m] = (r.after_cross[m] + combine_end(0, m)).astype(BF16)

    gain_grad = jnp.zeros((1, model), F32)
    for m in range(micro):
        grad_top = r.grad_state[m]
        grad_y = grad_top.astype(BF16)
        r.grad_self[m] = grad_y
        grad_mix = dot_cols(grad_y, r.wout[...]).astype(BF16)
        for pair in range(pairs):
            grads = attend_back(
                r.qkv[m, :, cols(pair)],
                r.qkv[m, :, cols(pair, model)],
                r.qkv[m, :, cols(pair, 2 * model)],
                r.probs_self[m, pair],
                grad_mix[:, pair * LANES : (pair + 1) * LANES],
            )
            for third, grad in enumerate(grads):
                r.grad_qkv[m, :, cols(pair, third * model)] = grad.astype(BF16)
        grad_normed = dot_cols(r.grad_qkv[m], r.wqkv[...])
        grad_state, grad_gain = norm_back(r.inputs[m].astype(F32), gain_a, grad_normed)
        gain_grad += grad_gain
        r.inputs_grad[m] = grad_top + grad_state
    r.gain_grads[0:1] = gain_grad
    r.gain_grads[3:8] = jnp.zeros((5, model), F32)

    def flat(ref):
        return ref[...].reshape(micro * tok, ref.shape[-1])

    def store_blocks(first, left, right):
        width = 2 * LANES
        left = flat(left)
        for start in range(0, right.shape[-1], width):
            part = dot_rows(left, right[:, :, start : start + width].reshape(micro * tok, width))
            at = (first + start // LANES) * model
            r.dense[at : at + model] = part[:, :LANES].astype(BF16)
            r.dense[at + model : at + 2 * model] = part[:, LANES:].astype(BF16)

    first_out = z.qkv_blocks
    first_cross = first_out + z.out_blocks
    first_misc = first_cross + z.cross_blocks
    store_blocks(0, r.normed_a, r.grad_qkv)
    store_blocks(first_out, r.attn_rows, r.grad_self)

    @enc
    def _():
        store_blocks(first_cross, r.normed_c, r.memory)

    @dec
    def _():
        store_blocks(first_cross, r.normed_c, r.grad_cross_q)
        store_blocks(first_cross + z.out_blocks, r.grad_cross, r.cross_rows)

    misc_lane = iota((1, z.misc), 1)
    misc_sign = when_equal(misc_lane, me_f) - when_equal(misc_lane, partner)
    misc = jnp.zeros((model, z.misc), F32)
    for m in range(micro):
        steps = r.grad_gap[m] * misc_sign
        top = steps.astype(BF16)
        rest = (steps - top.astype(F32)).astype(BF16)
        misc += dot_rows(r.taken[m], top) + dot_rows(r.taken[m], rest)
    place_gain = when_equal(iota((8, z.misc), 1), iota((8, z.misc), 0) + router.shape[-1])
    misc += dot_rows(r.gain_grads[...].astype(BF16), place_gain.astype(BF16))
    for index in range(z.misc_blocks):
        at = (first_misc + index) * model
        r.dense[at : at + model] = misc[:, index * LANES : (index + 1) * LANES].astype(BF16)
    used = z.blocks * model
    if used < z.dense_rows:
        r.dense[used:] = jnp.zeros((z.dense_rows - used, LANES), BF16)

    saves = [
        pltpu.make_async_copy(source, target, r.load_sem.at[i])
        for i, (source, target) in enumerate(
            (
                (r.taken, r.taken_out),
                (r.grad_hidden, r.grad_hidden_out),
                (r.act, r.act_out),
                (r.grad_out, r.grad_out_out),
            )
        )
    ]
    for save in saves:
        save.start()

    bits = list(range(z.bits))
    lead = min(3, z.bits)
    orders = [bits[:lead][p % lead :] + bits[:lead][: p % lead] + bits[lead:] for p in range(3)]
    offs = [jnp.int32(start) for start, _ in z.parts]
    sizes = [size for _, size in z.parts]
    lands = [start for start, _ in z.parts]

    def aligned(start, size):
        return pl.ds(pl.multiple_of(start, 16), size)

    def other_of(part, step):
        stride = 1 << orders[part][step]
        bit = lax.rem(lax.div(me, stride), 2)
        return bit, me + (1 - 2 * bit) * stride

    def exchange(part, step, source_ref, source, target, target_ref, stage):
        _, other = other_of(part, step)
        return pltpu.make_async_remote_copy(
            src_ref=source_ref.at[source],
            dst_ref=target_ref.at[target],
            send_sem=r.sum_send.at[part, stage],
            recv_sem=r.sum_recv.at[part, stage],
            device_id={"expert": other},
            device_id_type=MESH,
        )

    flights = [None] * 3

    def start_halving(part, step):
        bit, _ = other_of(part, step)
        half = sizes[part] // 2
        give = offs[part] + (1 - bit) * half
        keep = offs[part] + bit * half
        landing = pl.ds(lands[part], half)
        copy = exchange(part, step, r.dense, aligned(give, half), landing, r.partial, step)
        copy.start()
        offs[part] = keep
        sizes[part] = half
        lands[part] += half
        flights[part] = (copy, landing)

    def end_halving(part):
        copy, landing = flights[part]
        copy.wait()
        at = aligned(offs[part], sizes[part])
        target = r.dense if sizes[part] > z.parts[part][1] >> z.bits else r.total
        target[at] = (r.dense[at].astype(F32) + r.partial[landing].astype(F32)).astype(BF16)

    def start_doubling(part, step):
        at = aligned(offs[part], sizes[part])
        copy = exchange(part, step, r.total, at, at, r.total, z.bits + step)
        copy.start()
        flights[part] = copy

    def end_doubling(part, step):
        flights[part].wait()
        bit, _ = other_of(part, step)
        offs[part] = offs[part] - bit * sizes[part]
        sizes[part] *= 2

    live = [part for part in range(3) if sizes[part] > 0]
    for step in range(z.bits):
        for part in live:
            if step > 0:
                end_halving(part)
            start_halving(part, step)
    for step in reversed(range(z.bits)):
        for part in live:
            if step == z.bits - 1:
                end_halving(part)
            else:
                end_doubling(part, step + 1)
            start_doubling(part, step)
    for part in live:
        end_doubling(part, 0)

    dense_save = pltpu.make_async_copy(r.total, r.dense_out, r.load_sem.at[4])
    dense_save.start()
    for save in saves:
        save.wait()
    dense_save.wait()

    settle(r.infos.at[pl.ds(1, z.experts - 1)], r.info_send)
    for way in range(2):
        for m in range(micro):
            for half in range(z.flights):
                others = pl.ds(1, group - 1)
                settle(r.rows_out.at[way, m, half, others], r.rows_send.at[way, m, half])
                settle(r.reply_out.at[way, m, half, others], r.reply_send.at[way, m, half])
            settle(r.mirror_rows.at[way, m], r.mirror_send.at[way, m])
            settle(r.sums_out.at[way, m], r.sums_send.at[way, m])

    @enc
    def _():
        for m in range(micro):
            memory_copy(m).wait_send()

    @dec
    def _():
        for m in range(micro):
            grad_memory_copy(m).wait_send()


def run_kernel(z, meta, arrays):
    micro, tok, model, hidden = (z.micro, z.tok, z.model, z.hidden)
    vmem = pl.BlockSpec(memory_space=pltpu.VMEM)
    hbm = pl.BlockSpec(memory_space=pl.ANY)
    inputs = dict(
        meta=(meta, vmem),
        inputs=(arrays.inputs, vmem),
        cotangent=(arrays.cotangent, vmem),
        gains=(arrays.gains, vmem),
        w_router=(arrays.w_router, vmem),
        w_qkv=(arrays.w_qkv, hbm),
        w_out=(arrays.w_out, hbm),
        w_cross=(arrays.w_cross, hbm),
        w_up=(arrays.w_up, hbm),
        w_down=(arrays.w_down, hbm),
    )
    rows = (micro, tok, model)
    slot_rows = (micro, z.slots, model)
    slot_hidden = (micro, z.slots, hidden)
    outputs = dict(
        layer_out=(rows, BF16, vmem),
        inputs_grad=(rows, F32, vmem),
        dense_out=((z.dense_rows, LANES), BF16, hbm),
        taken_out=(slot_rows, BF16, hbm),
        grad_hidden_out=(slot_hidden, BF16, hbm),
        act_out=(slot_hidden, BF16, hbm),
        grad_out_out=(slot_rows, BF16, hbm),
    )
    blocks = (2, micro, z.flights, z.group, z.send, model)
    pairs = model // LANES
    dma = pltpu.SemaphoreType.DMA
    scratch = dict(
        wqkv=pltpu.VMEM(arrays.w_qkv.shape, BF16),
        wout=pltpu.VMEM(arrays.w_out.shape, BF16),
        wcross=pltpu.VMEM(arrays.w_cross.shape, BF16),
        wup=pltpu.VMEM(arrays.w_up.shape, BF16),
        wdown=pltpu.VMEM(arrays.w_down.shape, BF16),
        infos=pltpu.VMEM((z.experts, 8, LANES), F32),
        normed_a=pltpu.VMEM(rows, BF16),
        qkv=pltpu.VMEM((micro, tok, 3 * model), BF16),
        probs_self=pltpu.VMEM((micro, pairs, 2 * tok, tok), F32),
        attn_rows=pltpu.VMEM(rows, BF16),
        after_self=pltpu.VMEM(rows, F32),
        normed_c=pltpu.VMEM(rows, BF16),
        cross_q=pltpu.VMEM(rows, BF16),
        probs_cross=pltpu.VMEM((micro, pairs, 2 * tok, tok), F32),
        cross_rows=pltpu.VMEM(rows, BF16),
        memory_out=pltpu.VMEM((micro, tok, 2 * model), BF16),
        memory=pltpu.VMEM((micro, tok, 2 * model), BF16),
        after_cross=pltpu.VMEM(rows, F32),
        normed_m=pltpu.VMEM(rows, BF16),
        layer_final=pltpu.VMEM(rows, F32),
        grad_state=pltpu.VMEM(rows, F32),
        grad_rows=pltpu.VMEM(rows, BF16),
        grad_cross=pltpu.VMEM(rows, BF16),
        grad_cross_q=pltpu.VMEM(rows, BF16),
        grad_self=pltpu.VMEM(rows, BF16),
        grad_qkv=pltpu.VMEM((micro, tok, 3 * model), BF16),
        gain_grads=pltpu.VMEM((8, model), F32),
        pick=pltpu.VMEM((z.halves, micro, z.half_rows, tok), BF16),
        compact=pltpu.VMEM((micro, z.slots, z.all_rows), BF16),
        rows_out=pltpu.VMEM(blocks, BF16),
        rows_in=pltpu.VMEM(blocks, BF16),
        reply_out=pltpu.VMEM(blocks, BF16),
        reply_in=pltpu.VMEM(blocks, BF16),
        mirror_rows=pltpu.VMEM((2,) + rows, BF16),
        sums_out=pltpu.VMEM((2,) + rows, BF16),
        sums_in=pltpu.VMEM((2,) + rows, BF16),
        taken=pltpu.VMEM(slot_rows, BF16),
        slope=pltpu.VMEM(slot_hidden, BF16),
        act=pltpu.VMEM(slot_hidden, BF16),
        expert_out=pltpu.VMEM(slot_rows, BF16),
        gated=pltpu.VMEM(slot_rows, BF16),
        gate=pltpu.VMEM((micro, z.slots, 1), F32),
        gate_slope=pltpu.VMEM((micro, z.slots, 1), F32),
        grad_gap=pltpu.VMEM((micro, z.slots, 1), F32),
        grad_out=pltpu.VMEM(slot_rows, BF16),
        grad_hidden=pltpu.VMEM(slot_hidden, BF16),
        grad_taken=pltpu.VMEM((z.slots, model), F32),
        dense=pltpu.VMEM((z.dense_rows, LANES), BF16),
        total=pltpu.VMEM((z.dense_rows, LANES), BF16),
        partial=pltpu.VMEM((z.dense_rows, LANES), BF16),
        load_sem=dma((5,)),
        info_send=dma(()),
        info_recv=dma(()),
        rows_send=dma((2, micro, z.flights)),
        rows_recv=dma((2, micro, z.flights)),
        reply_send=dma((2, micro, z.flights)),
        reply_recv=dma((2, micro, z.flights)),
        mirror_send=dma((2, micro)),
        mirror_recv=dma((2, micro)),
        sums_send=dma((2, micro)),
        sums_recv=dma((2, micro)),
        memory_send=dma((2 * micro,)),
        memory_recv=dma((2 * micro,)),
        sum_send=dma((3, 2 * z.bits)),
        sum_recv=dma((3, 2 * z.bits)),
    )
    names = [*inputs, *outputs, *scratch]

    def body(*refs):
        kernel_body(z, names, *refs)

    return pl.pallas_call(
        body,
        name="layer_step",
        out_shape=[jax.ShapeDtypeStruct(shape, dtype) for shape, dtype, _ in outputs.values()],
        in_specs=[spec for _, spec in inputs.values()],
        out_specs=[spec for _, _, spec in outputs.values()],
        scratch_shapes=list(scratch.values()),
        compiler_params=pltpu.CompilerParams(
            collective_id=0, has_side_effects=True, vmem_limit_bytes=62 * 1024 * 1024
        ),
    )(*[value for value, _ in inputs.values()])


def shards(
    inputs,
    cotangent,
    segments,
    tasks,
    table,
    capacity,
    gains,
    w_qkv,
    w_out,
    w_cross,
    w_router,
    w_up,
    w_down,
):
    experts = lax.axis_size("expert")
    z = Sizes(inputs, w_qkv, w_cross, w_router, w_up, table, experts)
    model = z.model
    table_flat = table.reshape(1, 2 * z.tasks)
    meta = jnp.concatenate(
        [
            segments[0],
            tasks[0, :, :, 0],
            jnp.pad(table_flat, ((0, 0), (0, LANES - 2 * z.tasks)), constant_values=-1),
            jnp.broadcast_to(capacity.reshape(1, 1), (1, LANES)),
            jnp.zeros((2, LANES), jnp.int32),
        ],
        axis=0,
    )
    arrays = SimpleNamespace(
        inputs=inputs[0],
        cotangent=cotangent[0],
        gains=gains[0],
        w_router=w_router[0],
        w_qkv=w_qkv[0],
        w_out=w_out[0],
        w_cross=w_cross[0],
        w_up=w_up[0, 0],
        w_down=w_down[0, 0],
    )
    layer_out, inputs_grad, dense, taken, grad_hidden, act, grad_out = run_kernel(z, meta, arrays)

    def rows_of(value):
        return value.reshape(z.micro * z.slots, value.shape[-1])

    grad_up = dot_rows(rows_of(taken), rows_of(grad_hidden))
    grad_down = dot_rows(rows_of(act), rows_of(grad_out))

    def blocks_of(first, count):
        part = dense[first * model : (first + count) * model].reshape(count, model, LANES)
        return part.transpose(1, 0, 2).reshape(model, count * LANES).astype(F32)

    first_out = z.qkv_blocks
    first_cross = first_out + z.out_blocks
    first_misc = first_cross + z.cross_blocks
    misc = blocks_of(first_misc, z.misc_blocks)
    routers = w_router.shape[-1]
    return (
        layer_out[None],
        inputs_grad[None],
        misc[:, routers : routers + 3].T[None],
        blocks_of(0, z.qkv_blocks)[None],
        blocks_of(first_out, z.out_blocks)[None],
        blocks_of(first_cross, z.cross_blocks)[None],
        misc[:, :routers][None],
        grad_up[None, None],
        grad_down[None, None],
    )


def solution(mesh):
    in_specs = (
        P("section", None, "expert", None),
        P("section", None, "expert", None),
        P("section", None, "expert"),
        P("section", None, "expert", None),
        P("section", None, None),
        P("section"),
        P("section", None, None),
        P("section", None, None),
        P("section", None, None),
        P("section", None, None),
        P("section", None, None),
        P("section", "expert", None, None),
        P("section", "expert", None, None),
    )
    out_specs = (
        P("section", None, "expert", None),
        P("section", None, "expert", None),
        P("section", None, None),
        P("section", None, None),
        P("section", None, None),
        P("section", None, None),
        P("section", None, None),
        P("section", "expert", None, None),
        P("section", "expert", None, None),
    )
    return jax.shard_map(shards, mesh=mesh, in_specs=in_specs, out_specs=out_specs, check_vma=False)
```

```python
import math
from types import SimpleNamespace

import jax
import jax.numpy as jnp
from jax import lax
from jax.experimental import pallas as pl
from jax.experimental.pallas import tpu as pltpu
from jax.sharding import PartitionSpec as P

HEADS = 8
EPSILON = 1e-06
LANES = 128
UNROLL = 4
MESH = pl.DeviceIdType.MESH
F32 = jnp.float32
BF16 = jnp.bfloat16

INFO_TASK, INFO_RANK, INFO_COUNT = (0, 2, 4)
ROWS, REPLY, MIRROR, SUMS, MEMORY, SENT = (1000, 2000, 3000, 4000, 5000, 10000)


def round_up(value, unit):
    return -(-value // unit) * unit


def dot(left, right):
    return jnp.dot(left, right, preferred_element_type=F32)


def dot_rows(left, right):
    return lax.dot_general(left, right, (((0,), (0,)), ((), ())), preferred_element_type=F32)


def dot_cols(left, right):
    return lax.dot_general(left, right, (((1,), (1,)), ((), ())), preferred_element_type=F32)


def lane_sum(value):
    return jnp.sum(value, axis=-1, keepdims=True)


def row_sum(value):
    return jnp.sum(value, axis=0, keepdims=True)


def when_equal(left, right, value=1.0):
    return jnp.where(left == right, value, 0.0)


def iota(shape, axis):
    return lax.broadcasted_iota(jnp.int32, shape, axis).astype(F32)


def whole_part(value, unit):
    return jnp.floor((value + 0.5) * (1.0 / unit))


def inverse_rms(value):
    return lax.rsqrt(jnp.mean(value * value, axis=-1, keepdims=True) + EPSILON)


def norm(value, gain):
    return value * inverse_rms(value) * gain


def norm_back(value, gain, grad):
    scale = inverse_rms(value)
    unit = value * scale
    scaled = grad * gain
    grad_value = scale * (scaled - unit * jnp.mean(scaled * unit, axis=-1, keepdims=True))
    return grad_value, row_sum(grad * unit)


def gelu_and_slope(hidden):
    rate = math.sqrt(2.0 / math.pi)
    square = hidden * hidden
    bend = jnp.tanh(hidden * (rate + rate * 0.044715 * square))
    share = 0.5 + 0.5 * bend
    act = hidden * share
    slope = share + act * (1.0 - bend) * (rate + 3.0 * rate * 0.044715 * square)
    return act, slope


class Sizes:
    def __init__(self, inputs, w_qkv, w_cross, w_router, w_up, table, experts):
        _, self.micro, self.tok, self.model = inputs.shape
        self.hidden = w_up.shape[-1]
        self.experts = experts
        self.tasks = table.shape[1]
        self.slots = 2 * self.tok
        self.halves = 2
        self.group = experts // self.halves
        self.bound = max(2, 6 * self.tok // experts)
        self.send = round_up(self.bound, 16)
        self.merged = self.halves * self.bound <= self.send
        self.flights = 1 if self.merged else self.halves
        self.half_rows = self.group * self.send
        self.all_rows = self.flights * self.half_rows
        self.misc = round_up(w_router.shape[-1] + 3, LANES)
        self.qkv_blocks = w_qkv.shape[-1] // LANES
        self.out_blocks = self.model // LANES
        self.cross_blocks = w_cross.shape[-1] // LANES
        self.misc_blocks = self.misc // LANES
        self.blocks = self.qkv_blocks + self.out_blocks + self.cross_blocks + self.misc_blocks
        self.bits = experts.bit_length() - 1
        unit = 16 * experts
        self.groups = []
        start = 0
        for blocks, count in (
            (self.cross_blocks, 3),
            (self.out_blocks, 2),
            (self.qkv_blocks + self.misc_blocks, 6),
        ):
            units = -(-blocks * self.model // unit)
            count = min(count, units)
            group = []
            for part in range(count):
                size = (units // count + (part < units % count)) * unit
                group.append((start, size))
                start += size
            self.groups.append(group)
        self.parts = sum(len(group) for group in self.groups)
        self.dense_rows = start


def kernel_body(z, names, *refs):
    r = SimpleNamespace(**dict(zip(names, refs)))
    me = lax.axis_index("expert")
    section = lax.axis_index("section")
    tok, model, micro, group, send, slots = (z.tok, z.model, z.micro, z.group, z.send, z.slots)
    here = lax.rem(me, group)
    base = me - here
    mirror = lax.rem(me + group, z.experts)
    me_f = me.astype(F32)
    here_f = here.astype(F32)
    base_f = base.astype(F32)
    enc_f = 1.0 - section.astype(F32)

    side = [None]
    owed = {}

    def on_section(index):
        def put(run):
            side[0] = index
            pl.when(section == index)(run)
            side[0] = None

        return put

    enc, dec = (on_section(0), on_section(1))

    def wait_for(ref, sem):
        pltpu.make_async_copy(ref, ref, sem).wait()

    def owe(key, copy):
        owed[side[0], key] = copy

    def settle(key):
        found = [e for e in owed if e[1] == key and (side[0] in (None, e[0]) or e[0] is None)]
        copies = [owed.pop(entry) for entry in found]
        if side[0] is not None and found[0][0] is None:
            owed[1 - side[0], key] = copies[0]
        wait_for(*copies[0]())

    def settle_all():
        for index in (None, 0, 1):
            waits = [owed.pop(entry) for entry in list(owed) if entry[0] == index]

            def run():
                for copy in waits:
                    wait_for(*copy())

            if index is None:
                run()
            else:
                pl.when(section == index)(run)

    loads = [
        pltpu.make_async_copy(source, target, r.load_sem.at[i])
        for i, (source, target) in enumerate(
            (
                (r.w_qkv, r.wqkv),
                (r.w_out, r.wout),
                (r.w_cross, r.wcross),
                (r.w_up, r.wup),
                (r.w_down, r.wdown),
            )
        )
    ]
    for load in loads:
        load.start()

    barrier = pltpu.get_barrier_semaphore()

    def greet(step, _):
        pl.semaphore_signal(
            barrier,
            inc=1,
            device_id={"expert": lax.rem(me + step, z.experts)},
            device_id_type=MESH,
        )
        return 0

    lax.fori_loop(1, z.experts, greet, 0)
    pl.semaphore_signal(
        barrier, inc=1, device_id={"section": 1 - section}, device_id_type=MESH
    )

    seg_rows = r.segments[...].astype(F32)
    task_rows = r.tasks[...].astype(F32)
    blank = jnp.zeros((LANES - 2 * micro, LANES), F32)
    flipped = jnp.transpose(jnp.concatenate([seg_rows, task_rows, blank], axis=0))
    lane = iota((1, LANES), 1)
    earlier = jnp.where(iota((tok, tok), 0) < iota((tok, tok), 1), 1.0, 0.0)
    ranks, counts = ([], [])
    for m in range(micro):
        task_col = flipped[:, micro + m : micro + m + 1]
        ranks.append(row_sum(when_equal(task_col, task_rows[m : m + 1]) * earlier))
        counts.append(row_sum(when_equal(task_col, lane)))
    r.infos[0] = jnp.concatenate(
        [task_rows, *ranks, *counts, jnp.zeros((8 - 3 * micro, LANES), F32)], axis=0
    )

    table = r.table[...].astype(F32)
    table_lane = iota((1, z.tasks), 1)

    def task_of(expert):
        return lane_sum(
            when_equal(table[0:1], expert, table_lane) + when_equal(table[1:2], expert, table_lane)
        )

    line = iota((z.half_rows, 1), 0)
    line_block = whole_part(line, send)
    line_rank = line - line_block * send
    line_place = here_f + line_block
    line_place = jnp.where(line_place >= group, line_place - group, line_place)
    line_task = task_of(base_f + line_place)

    def fill_pick(half):
        rank_here = line_rank - (half * z.bound if z.merged else 0)
        info = r.infos[half * group]
        for m in range(micro):
            hit = (info[INFO_TASK + m : INFO_TASK + m + 1] == line_task) & (
                info[INFO_RANK + m : INFO_RANK + m + 1] == rank_here
            )
            r.pick[half, m] = jnp.where(hit, 1.0, 0.0).astype(BF16)

    fill_pick(0)

    pl.semaphore_wait(barrier, z.experts)

    def tell(step, _):
        pltpu.make_async_remote_copy(
            src_ref=r.infos.at[0],
            dst_ref=r.infos.at[step],
            send_sem=r.info_send,
            recv_sem=r.info_recv,
            device_id={"expert": lax.rem(me + step, z.experts)},
            device_id_type=MESH,
        ).start()
        return 0

    lax.fori_loop(1, z.experts, tell, 0)
    others_told = pl.ds(1, z.experts - 1)
    owe(SENT, lambda: (r.infos.at[others_told], r.info_send))
    owe(0, lambda: (r.infos.at[others_told], r.info_recv))

    def spread(way, m, half, rows, back):
        packed, landed = (
            (r.reply_out, r.reply_in) if back else (r.rows_out, r.rows_in)
        )
        send_sem, recv_sem = (
            (r.reply_send, r.reply_recv) if back else (r.rows_send, r.rows_recv)
        )
        packed[way, m, half] = rows.reshape(group, send, model)
        landed[way, m, half, 0] = rows[:send]

        def push(step, _):
            if back:
                other = lax.rem(here + group - step, group)
            else:
                other = lax.rem(here + step, group)
            pltpu.make_async_remote_copy(
                src_ref=packed.at[way, m, half, step],
                dst_ref=landed.at[way, m, half, step],
                send_sem=send_sem.at[way, m, half],
                recv_sem=recv_sem.at[way, m, half],
                device_id={"expert": base + other},
                device_id_type=MESH,
            ).start()
            return 0

        lax.fori_loop(1, group, push, 0, unroll=group <= 8)
        key = (REPLY if back else ROWS) + 100 * way + 10 * m + half
        others = pl.ds(1, group - 1)
        at = (way, m, half)
        owe(SENT + key, lambda: (packed.at[(*at, others)], send_sem.at[at]))
        owe(key, lambda: (landed.at[(*at, others)], recv_sem.at[at]))

    def ship(key, source, target, sems, device_id):
        copy = pltpu.make_async_remote_copy(
            src_ref=source(),
            dst_ref=target(),
            send_sem=sems()[0],
            recv_sem=sems()[1],
            device_id=device_id,
            device_id_type=MESH,
        )
        copy.start()
        owe(SENT + key, lambda: (source(), sems()[0]))

    def swap(key, source, target, sems):
        ship(key, source, target, sems, {"expert": mirror})
        owe(key, lambda: (target(), sems()[1]))

    def dispatch(way, m, source):
        swap(
            MIRROR + 10 * way + m,
            lambda: source.at[m],
            lambda: r.mirror_rows.at[way, m],
            lambda: (r.mirror_send.at[way, m], r.mirror_recv.at[way, m]),
        )
        if not z.merged:
            spread(way, m, 0, dot(r.pick[0, m], source[m]).astype(BF16), False)

    def dispatch_mirror(way, m, source):
        settle(MIRROR + 10 * way + m)
        rows = dot(r.pick[1, m], r.mirror_rows[way, m])
        if z.merged:
            rows += dot(r.pick[0, m], source[m])
        spread(way, m, z.flights - 1, rows.astype(BF16), False)

    def arrived(way, m):
        for half in range(z.flights):
            settle(ROWS + 100 * way + 10 * m + half)
        return dot(r.compact[m], r.rows_in[way, m].reshape(z.all_rows, model))

    def combine(way, m, rows):
        reply = dot_rows(r.compact[m], rows).astype(BF16)
        for half in reversed(range(z.flights)):
            spread(way, m, half, reply[half * z.half_rows : (half + 1) * z.half_rows], True)

    def gathered(way, m, half):
        flight = 0 if z.merged else half
        if not z.merged or half == 1:
            settle(REPLY + 100 * way + 10 * m + flight)
        return dot_rows(r.pick[half, m], r.reply_in[way, m, flight].reshape(z.half_rows, model))

    def combine_mirror(way, m):
        r.sums_out[way, m] = gathered(way, m, 1).astype(BF16)
        swap(
            SUMS + 10 * way + m,
            lambda: r.sums_out.at[way, m],
            lambda: r.sums_in.at[way, m],
            lambda: (r.sums_send.at[way, m], r.sums_recv.at[way, m]),
        )

    def combine_end(way, m):
        own = gathered(way, m, 0)
        settle(SUMS + 10 * way + m)
        return own + r.sums_in[way, m].astype(F32)

    def know_others():
        settle(0)
        fill_pick(1)

    @dec
    def _():
        dispatch(1, 0, r.cotangent)
        know_others()
        dispatch_mirror(1, 0, r.cotangent)

    low_lane = jnp.where(iota((1, LANES), 1) < LANES // 2, 1.0, 0.0)
    high_lane = 1.0 - low_lane
    low_bf, high_bf = (low_lane.astype(BF16), high_lane.astype(BF16))
    pairs = model // LANES
    score_scale = (model // HEADS) ** (-0.5)

    def stacked(block):
        return jnp.concatenate([block * low_bf, block * high_bf], axis=0)

    def merged(block):
        return block[:tok] * low_lane + block[tok:] * high_lane

    def attend(queries, keys, values, allowed):
        scores = dot_cols(stacked(queries), keys) * score_scale
        if allowed is not None:
            scores = jnp.where(allowed > 0.5, scores, -1000000000.0)
        top = jnp.max(scores, axis=-1, keepdims=True)
        grown = jnp.exp(scores - top)
        probs = grown / lane_sum(grown)
        return probs, merged(dot(probs.astype(BF16), values))

    def attend_back(queries, keys, values, probs, grad_mixed):
        grad_stack = stacked(grad_mixed)
        grad_probs = dot_cols(grad_stack, values)
        inner = lane_sum(probs * grad_probs)
        grad_scores = (probs * (grad_probs - inner)).astype(BF16)
        grad_queries = merged(dot(grad_scores, keys)) * score_scale
        grad_keys = dot_rows(grad_scores, stacked(queries)) * score_scale
        grad_values = dot_rows(probs.astype(BF16), grad_stack)
        return grad_queries, grad_keys, grad_values

    def cols(index, start=0):
        return pl.ds(pl.multiple_of(start + index * LANES, LANES), LANES)

    def each_pair(run):
        def step(pair, _):
            run(pair)
            return 0

        lax.fori_loop(0, pairs, step, 0, unroll=UNROLL)

    gain_a, gain_c, gain_m = [r.gains[:, i * model : (i + 1) * model] for i in range(3)]

    def enter_experts(m):
        r.normed_m[m] = norm(r.after_cross[m], gain_m).astype(BF16)
        dispatch(0, m, r.normed_m)

    loads[0].wait()
    loads[1].wait()
    for m in range(micro):
        x_in = r.inputs[m].astype(F32)
        normed_a = norm(x_in, gain_a).astype(BF16)
        r.normed_a[m] = normed_a
        r.qkv[m] = dot(normed_a, r.wqkv[...]).astype(BF16)
        causal = jnp.where(iota((tok, tok), 1) <= iota((tok, tok), 0), 1.0, enc_f)
        allowed = when_equal(flipped[:, m : m + 1], seg_rows[m : m + 1]) * causal
        allowed = jnp.concatenate([allowed, allowed], axis=0)
        @each_pair
        def _(pair):
            probs, mixed = attend(
                r.qkv[m, :, cols(pair)],
                r.qkv[m, :, cols(pair, model)],
                r.qkv[m, :, cols(pair, 2 * model)],
                allowed,
            )
            r.probs_self[m, pair] = probs
            r.attn_rows[m, :, cols(pair)] = mixed.astype(BF16)
        after_self = x_in + dot(r.attn_rows[m], r.wout[...])

        @enc
        def _():
            r.after_cross[m] = after_self
            enter_experts(m)

        @dec
        def _():
            r.after_self[m] = after_self

    loads[2].wait()

    def send_memory(m):
        index = m + micro * side[0]
        ship(
            MEMORY + index,
            lambda: r.memory_out.at[m],
            lambda: r.memory.at[m],
            lambda: (r.memory_send.at[index], r.memory_recv.at[index]),
            {"section": 1 - section},
        )

    def wait_memory(m):
        index = m + micro * (1 - side[0])
        owe(MEMORY + index, lambda: (r.memory.at[m], r.memory_recv.at[index]))
        settle(MEMORY + index)

    @enc
    def _():
        know_others()

    @dec
    def _():
        for m in range(micro):
            after_self = r.after_self[m]
            normed_c = norm(after_self, gain_c).astype(BF16)
            r.normed_c[m] = normed_c
            r.cross_q[m] = dot(normed_c, r.wcross[:, :model]).astype(BF16)
            wait_memory(m)

            @each_pair
            def _(pair):
                probs, mixed = attend(
                    r.cross_q[m, :, cols(pair)],
                    r.memory[m, :, cols(pair)],
                    r.memory[m, :, cols(pair, model)],
                    None,
                )
                r.probs_cross[m, pair] = probs
                r.cross_rows[m, :, cols(pair)] = mixed.astype(BF16)

            r.after_cross[m] = after_self + dot_cols(r.cross_rows[m], r.wcross[:, model:])
            enter_experts(m)

    for m in range(micro):
        dispatch_mirror(0, m, r.normed_m)

    @dec
    def _():
        for m in range(1, micro):
            dispatch(1, m, r.cotangent)
        for m in range(1, micro):
            dispatch_mirror(1, m, r.cotangent)

    own_task = task_of(me_f)
    partner = lane_sum(when_equal(table_lane, own_task, table[0:1] + table[1:2])) - me_f
    capacity = r.capacity[0].astype(F32)
    place = iota((1, z.all_rows), 1)
    block = whole_part(place, send)
    place_rank = place - block * send
    place_half = whole_part(block, group)
    sender = here_f - (block - place_half * group)
    if z.merged:
        place_half = jnp.minimum(whole_part(place_rank, z.bound), 1.0)
        place_rank = place_rank - place_half * z.bound
    sender = base_f + jnp.where(sender < 0.0, sender + group, sender) + place_half * group
    sender = jnp.where(sender >= z.experts, sender - z.experts, sender)
    teller = me_f - iota((z.experts, 1), 0)
    teller = jnp.where(teller < 0.0, teller + z.experts, teller)
    for m in range(micro):
        told = lane_sum(jnp.where(lane == own_task, r.infos[:, INFO_COUNT + m, :], 0.0))
        count = row_sum(when_equal(teller, sender, told))
        slot = row_sum(jnp.where(teller < sender, told, 0.0)) + place_rank
        slot = jnp.where((place_rank < count) & (slot < capacity), slot, -1.0)
        r.compact[m] = when_equal(iota((slots, 1), 0), slot).astype(BF16)

    router = r.w_router[...]
    routers = router.shape[0]
    expert_lane = iota((8, routers), 1)
    sign = when_equal(expert_lane, me_f) - when_equal(expert_lane, partner)
    router_step = dot(sign.astype(BF16), router)[0:1]
    tile = 1024

    def each_tile(width, run):
        def step(index, _):
            run(pl.ds(pl.multiple_of(index * tile, tile), tile))
            return 0

        lax.fori_loop(0, width // tile, step, 0)

    def expert_forward(m):
        taken = arrived(0, m).astype(BF16)
        r.taken[m] = taken

        def up_tile(at):
            act, slope = gelu_and_slope(dot(r.taken[m], r.wup[:, at]))
            r.act[m, :, at] = act.astype(BF16)
            r.slope[m, :, at] = slope.astype(BF16)

        each_tile(z.hidden, up_tile)
        gap = lane_sum(taken.astype(F32) * router_step)
        small = jnp.exp(-jnp.abs(gap))
        large = 1.0 / (1.0 + small)
        gate = jnp.where(gap >= 0.0, large, small * large)
        r.gate[m] = gate
        r.gate_slope[m] = small * large * large

        r.expert_out[m] = dot(r.act[m], r.wdown[...]).astype(BF16)
        r.gated[m] = (gate * r.expert_out[m].astype(F32)).astype(BF16)

    def expert_backward(m):
        grad_final = arrived(1, m)
        grad_gate = lane_sum(r.expert_out[m].astype(F32) * grad_final)
        grad_gap = r.gate_slope[m] * grad_gate
        r.grad_gap[m] = grad_gap
        r.grad_out[m] = (r.gate[m] * grad_final).astype(BF16)

        def act_tile(at):
            grad_act = dot_cols(r.grad_out[m], r.wdown[at, :])
            r.grad_hidden[m, :, at] = (grad_act * r.slope[m, :, at].astype(F32)).astype(BF16)

        each_tile(z.hidden, act_tile)

        rounded = dot_cols(r.grad_hidden[m], r.wup[...]).astype(BF16).astype(F32)
        combine(1, m, (rounded + grad_gap * router_step).astype(BF16))

    loads[3].wait()
    loads[4].wait()

    @dec
    def _():
        for m in range(micro):
            expert_forward(m)
            expert_backward(m)
        for m in range(micro):
            r.grad_state[m] = r.cotangent[m].astype(F32)

    @enc
    def _():
        for m in range(micro):
            expert_forward(m)
            combine(0, m, r.gated[m])
        for m in range(micro):
            combine_mirror(0, m)
        for m in range(micro):
            layer_final = r.after_cross[m] + combine_end(0, m)
            r.layer_final[m] = layer_final
            r.layer_out[m] = layer_final.astype(BF16)
            normed_k = norm(layer_final, gain_c).astype(BF16)
            r.normed_c[m] = normed_k
            r.memory_out[m] = dot(normed_k, r.wcross[...]).astype(BF16)
            send_memory(m)
        gain_grad = jnp.zeros((1, model), F32)
        for m in range(micro):
            wait_memory(m)
            grad_normed = dot_cols(r.memory[m], r.wcross[...])
            grad_state, grad_gain = norm_back(r.layer_final[m], gain_c, grad_normed)
            gain_grad += grad_gain
            grad_final = r.cotangent[m].astype(F32) + grad_state
            r.grad_state[m] = grad_final
            r.grad_rows[m] = grad_final.astype(BF16)
            dispatch(1, m, r.grad_rows)
        for m in range(micro):
            dispatch_mirror(1, m, r.grad_rows)
        r.gain_grads[1:2] = gain_grad
        for m in range(micro):
            expert_backward(m)

    def flat(ref, at=slice(None)):
        value = ref[:, :, at]
        return value.reshape(value.shape[0] * value.shape[1], value.shape[2])

    saves = []

    def save(source, target):
        copy = pltpu.make_async_copy(source, target, r.save_sem.at[len(saves)])
        copy.start()
        saves.append(copy)

    def up_grad(at):
        r.wup[:, at] = dot_rows(flat(r.taken), flat(r.grad_hidden, at)).astype(BF16)

    def down_grad(at):
        r.wdown[at, :] = dot_rows(flat(r.act, at), flat(r.grad_out)).astype(BF16)

    each_tile(z.hidden, up_grad)
    save(r.wup, r.up_grad)
    for m in range(micro):
        combine_mirror(1, m)
    each_tile(z.hidden, down_grad)
    save(r.wdown, r.down_grad)

    gain_grad = jnp.zeros((1, model), F32)
    for m in range(micro):
        grad_state, grad_gain = norm_back(r.after_cross[m], gain_m, combine_end(1, m))
        gain_grad += grad_gain
        r.grad_state[m] += grad_state

        @dec
        def _():
            grad_y = r.grad_state[m].astype(BF16)
            r.grad_cross[m] = grad_y
            r.grad_mix[...] = dot(grad_y, r.wcross[:, model:]).astype(BF16)

            @each_pair
            def _(pair):
                at = cols(pair)
                grad_q, grad_k, grad_v = attend_back(
                    r.cross_q[m, :, at],
                    r.memory[m, :, at],
                    r.memory[m, :, cols(pair, model)],
                    r.probs_cross[m, pair],
                    r.grad_mix[:, at],
                )
                r.grad_cross_q[m, :, at] = grad_q.astype(BF16)
                r.memory_out[m, :, at] = grad_k.astype(BF16)
                r.memory_out[m, :, cols(pair, model)] = grad_v.astype(BF16)
            send_memory(m)

    r.gain_grads[2:3] = gain_grad

    @dec
    def _():
        gain_grad = jnp.zeros((1, model), F32)
        for m in range(micro):
            grad_normed = dot_cols(r.grad_cross_q[m], r.wcross[:, :model])
            grad_state, grad_gain = norm_back(r.after_self[m], gain_c, grad_normed)
            gain_grad += grad_gain
            r.grad_state[m] += grad_state
        r.gain_grads[1:2] = gain_grad
        for m in range(micro):
            combine(0, m, r.gated[m])

    first_cross = 0
    first_out = first_cross + z.cross_blocks
    first_qkv = first_out + z.out_blocks
    first_misc = first_qkv + z.qkv_blocks

    def store_blocks(first, left, right):
        width = 2 * LANES
        left = flat(left)
        for start in range(0, right.shape[-1], width):
            grad = dot_rows(left, flat(right, pl.ds(start, width))).astype(BF16)
            at = (first + start // LANES) * model
            r.dense[at : at + model] = grad[:, :LANES]
            r.dense[at + model : at + 2 * model] = grad[:, LANES:]

    bits = list(range(z.bits))
    lead = min(3, z.bits)
    parts = []
    for group_index, group_parts in enumerate(z.groups):
        for start, size in group_parts:
            turn = len(parts) % lead
            parts.append(
                SimpleNamespace(
                    index=len(parts),
                    group=group_index,
                    order=bits[turn:lead] + bits[:turn] + bits[lead:],
                    at=jnp.int32(start),
                    size=size,
                    land=start,
                    stage=0,
                    copy=None,
                )
            )

    def aligned(start, size):
        return pl.ds(pl.multiple_of(start, 16), size)

    def start_stage(part):
        halving = part.stage < z.bits
        stride = 1 << part.order[part.stage if halving else 2 * z.bits - 1 - part.stage]
        part.bit = lax.rem(lax.div(me, stride), 2)
        if halving:
            half = part.size // 2
            source = r.dense.at[aligned(part.at + (1 - part.bit) * half, half)]
            target = r.partial.at[pl.ds(part.land, half)]
        else:
            source = target = r.total.at[aligned(part.at, part.size)]
        part.copy = pltpu.make_async_remote_copy(
            src_ref=source,
            dst_ref=target,
            send_sem=r.sum_send.at[part.index, part.stage],
            recv_sem=r.sum_recv.at[part.index, part.stage],
            device_id={"expert": me + (1 - 2 * part.bit) * stride},
            device_id_type=MESH,
        )
        part.copy.start()

    def end_stage(part):
        part.copy.wait()
        if part.stage < z.bits:
            half = part.size // 2
            part.at = part.at + part.bit * half
            rows = aligned(part.at, half)
            came = r.partial[pl.ds(part.land, half)].astype(F32)
            target = r.total if part.stage == z.bits - 1 else r.dense
            target[rows] = (r.dense[rows].astype(F32) + came).astype(BF16)
            part.land += half
            part.size = half
        else:
            part.at = part.at - part.bit * part.size
            part.size *= 2
        part.stage += 1

    def begin(group_index):
        for part in parts:
            if part.group == group_index:
                start_stage(part)

    def advance(group_index):
        for part in parts:
            if part.group == group_index and part.stage < 2 * z.bits:
                end_stage(part)
                if part.stage < 2 * z.bits:
                    start_stage(part)

    @enc
    def _():
        store_blocks(first_cross, r.normed_c, r.memory)

    @dec
    def _():
        store_blocks(first_cross, r.normed_c, r.grad_cross_q)
        store_blocks(first_cross + z.out_blocks, r.grad_cross, r.cross_rows)

    begin(0)
    for m in range(micro):
        r.grad_self[m] = r.grad_state[m].astype(BF16)
    store_blocks(first_out, r.attn_rows, r.grad_self)
    begin(1)

    gain_grad = jnp.zeros((1, model), F32)
    for m in range(micro):
        grad_top = r.grad_state[m]
        grad_y = r.grad_self[m]
        r.grad_mix[...] = dot_cols(grad_y, r.wout[...]).astype(BF16)

        @each_pair
        def _(pair):
            grads = attend_back(
                r.qkv[m, :, cols(pair)],
                r.qkv[m, :, cols(pair, model)],
                r.qkv[m, :, cols(pair, 2 * model)],
                r.probs_self[m, pair],
                r.grad_mix[:, cols(pair)],
            )
            for third, grad in enumerate(grads):
                r.grad_qkv[m, :, cols(pair, third * model)] = grad.astype(BF16)
        grad_normed = dot_cols(r.grad_qkv[m], r.wqkv[...])
        grad_state, grad_gain = norm_back(r.inputs[m].astype(F32), gain_a, grad_normed)
        gain_grad += grad_gain
        r.inputs_grad[m] = grad_top + grad_state
    r.gain_grads[0:1] = gain_grad
    r.gain_grads[3:8] = jnp.zeros((5, model), F32)

    store_blocks(first_qkv, r.normed_a, r.grad_qkv)
    misc_row = iota((1, z.misc), 1)
    misc_sign = when_equal(misc_row, me_f) - when_equal(misc_row, partner)
    misc = jnp.zeros((z.misc, model), F32)
    for m in range(micro):
        steps = r.grad_gap[m] * misc_sign
        top = steps.astype(BF16)
        rest = (steps - top.astype(F32)).astype(BF16)
        misc += dot_rows(top, r.taken[m]) + dot_rows(rest, r.taken[m])
    place_gain = when_equal(iota((8, z.misc), 1), iota((8, z.misc), 0) + routers)
    misc += dot_rows(place_gain.astype(BF16), r.gain_grads[...].astype(BF16))
    misc_rows = [
        pl.ds(first_misc * model + index * z.misc, z.misc) for index in range(model // LANES)
    ]
    for index, rows in enumerate(misc_rows):
        r.dense[rows] = misc[:, index * LANES : (index + 1) * LANES].astype(BF16)
    used = z.blocks * model
    if used < z.dense_rows:
        r.dense[used:] = jnp.zeros((z.dense_rows - used, LANES), BF16)
    begin(2)
    advance(0)
    advance(1)

    @dec
    def _():
        for m in range(micro):
            combine_mirror(0, m)
        for m in range(micro):
            r.layer_out[m] = (r.after_cross[m] + combine_end(0, m)).astype(BF16)

    while any(part.stage < 2 * z.bits for part in parts):
        for group_index in range(3):
            advance(group_index)

    for target, first, count in (
        (r.cross_grad, first_cross, z.cross_blocks),
        (r.out_grad, first_out, z.out_blocks),
        (r.qkv_grad, first_qkv, z.qkv_blocks),
    ):
        for index in range(count):
            rows = pl.ds((first + index) * model, model)
            save(r.total.at[rows], target.at[:, pl.ds(index * LANES, LANES)])
    for index, rows in enumerate(misc_rows):
        sums = r.total[rows].astype(F32)
        r.router_grad[:, index * LANES : (index + 1) * LANES] = sums[:routers]
        for row in range(3):
            at = row * model + index * LANES
            r.gains_grad[:, at : at + LANES] = sums[routers + row : routers + row + 1]
    for copy in saves:
        copy.wait()

    settle_all()


def vmem_bytes(buffers):
    total = 0
    for buffer in buffers:
        if buffer.memory_space == pltpu.VMEM:
            *lead, rows, lanes = buffer.shape
            size = math.prod(lead) * round_up(rows, 8) * round_up(lanes, LANES)
            total += size * jnp.dtype(buffer.dtype).itemsize
    return min(total + 5 * 1024 * 1024, 62 * 1024 * 1024)


def run_kernel(z, arrays):
    micro, tok, model, hidden = (z.micro, z.tok, z.model, z.hidden)
    vmem = pl.BlockSpec(memory_space=pltpu.VMEM)
    hbm = pl.BlockSpec(memory_space=pl.ANY)
    inputs = dict(
        segments=(arrays.segments, vmem),
        tasks=(arrays.tasks, vmem),
        table=(arrays.table, vmem),
        capacity=(arrays.capacity, pl.BlockSpec(memory_space=pltpu.SMEM)),
        inputs=(arrays.inputs, vmem),
        cotangent=(arrays.cotangent, vmem),
        gains=(arrays.gains, vmem),
        w_router=(arrays.w_router, vmem),
        w_qkv=(arrays.w_qkv, hbm),
        w_out=(arrays.w_out, hbm),
        w_cross=(arrays.w_cross, hbm),
        w_up=(arrays.w_up, hbm),
        w_down=(arrays.w_down, hbm),
    )
    rows = (micro, tok, model)
    slot_rows = (micro, z.slots, model)
    slot_hidden = (micro, z.slots, hidden)
    outputs = dict(
        layer_out=(rows, BF16, vmem),
        inputs_grad=(rows, F32, vmem),
        gains_grad=((1, 3 * model), F32, vmem),
        router_grad=(arrays.w_router.shape, F32, vmem),
        qkv_grad=(arrays.w_qkv.shape, BF16, hbm),
        out_grad=(arrays.w_out.shape, BF16, hbm),
        cross_grad=(arrays.w_cross.shape, BF16, hbm),
        up_grad=(arrays.w_up.shape, BF16, hbm),
        down_grad=(arrays.w_down.shape, BF16, hbm),
    )
    blocks = (2, micro, z.flights, z.group, z.send, model)
    pairs = model // LANES
    dma = pltpu.SemaphoreType.DMA
    scratch = dict(
        wqkv=pltpu.VMEM(arrays.w_qkv.shape, BF16),
        wout=pltpu.VMEM(arrays.w_out.shape, BF16),
        wcross=pltpu.VMEM(arrays.w_cross.shape, BF16),
        wup=pltpu.VMEM(arrays.w_up.shape, BF16),
        wdown=pltpu.VMEM(arrays.w_down.shape, BF16),
        infos=pltpu.VMEM((z.experts, 8, LANES), F32),
        normed_a=pltpu.VMEM(rows, BF16),
        qkv=pltpu.VMEM((micro, tok, 3 * model), BF16),
        probs_self=pltpu.VMEM((micro, pairs, 2 * tok, tok), F32),
        attn_rows=pltpu.VMEM(rows, BF16),
        after_self=pltpu.VMEM(rows, F32),
        normed_c=pltpu.VMEM(rows, BF16),
        cross_q=pltpu.VMEM(rows, BF16),
        probs_cross=pltpu.VMEM((micro, pairs, 2 * tok, tok), F32),
        cross_rows=pltpu.VMEM(rows, BF16),
        memory_out=pltpu.VMEM((micro, tok, 2 * model), BF16),
        memory=pltpu.VMEM((micro, tok, 2 * model), BF16),
        after_cross=pltpu.VMEM(rows, F32),
        normed_m=pltpu.VMEM(rows, BF16),
        layer_final=pltpu.VMEM(rows, F32),
        grad_state=pltpu.VMEM(rows, F32),
        grad_rows=pltpu.VMEM(rows, BF16),
        grad_cross=pltpu.VMEM(rows, BF16),
        grad_cross_q=pltpu.VMEM(rows, BF16),
        grad_self=pltpu.VMEM(rows, BF16),
        grad_mix=pltpu.VMEM((tok, model), BF16),
        grad_qkv=pltpu.VMEM((micro, tok, 3 * model), BF16),
        gain_grads=pltpu.VMEM((8, model), F32),
        pick=pltpu.VMEM((z.halves, micro, z.half_rows, tok), BF16),
        compact=pltpu.VMEM((micro, z.slots, z.all_rows), BF16),
        rows_out=pltpu.VMEM(blocks, BF16),
        rows_in=pltpu.VMEM(blocks, BF16),
        reply_out=pltpu.VMEM(blocks, BF16),
        reply_in=pltpu.VMEM(blocks, BF16),
        mirror_rows=pltpu.VMEM((2,) + rows, BF16),
        sums_out=pltpu.VMEM((2,) + rows, BF16),
        sums_in=pltpu.VMEM((2,) + rows, BF16),
        taken=pltpu.VMEM(slot_rows, BF16),
        slope=pltpu.VMEM(slot_hidden, BF16),
        act=pltpu.VMEM(slot_hidden, BF16),
        expert_out=pltpu.VMEM(slot_rows, BF16),
        gated=pltpu.VMEM(slot_rows, BF16),
        gate=pltpu.VMEM((micro, z.slots, 1), F32),
        gate_slope=pltpu.VMEM((micro, z.slots, 1), F32),
        grad_gap=pltpu.VMEM((micro, z.slots, 1), F32),
        grad_out=pltpu.VMEM(slot_rows, BF16),
        grad_hidden=pltpu.VMEM(slot_hidden, BF16),
        dense=pltpu.VMEM((z.dense_rows, LANES), BF16),
        total=pltpu.VMEM((z.dense_rows, LANES), BF16),
        partial=pltpu.VMEM((z.dense_rows, LANES), BF16),
        load_sem=dma((5,)),
        save_sem=dma((2 + z.blocks - z.misc_blocks,)),
        info_send=dma(()),
        info_recv=dma(()),
        rows_send=dma((2, micro, z.flights)),
        rows_recv=dma((2, micro, z.flights)),
        reply_send=dma((2, micro, z.flights)),
        reply_recv=dma((2, micro, z.flights)),
        mirror_send=dma((2, micro)),
        mirror_recv=dma((2, micro)),
        sums_send=dma((2, micro)),
        sums_recv=dma((2, micro)),
        memory_send=dma((2 * micro,)),
        memory_recv=dma((2 * micro,)),
        sum_send=dma((z.parts, 2 * z.bits)),
        sum_recv=dma((z.parts, 2 * z.bits)),
    )
    names = [*inputs, *outputs, *scratch]

    def body(*refs):
        kernel_body(z, names, *refs)

    return pl.pallas_call(
        body,
        name="layer_step",
        out_shape=[jax.ShapeDtypeStruct(shape, dtype) for shape, dtype, _ in outputs.values()],
        in_specs=[spec for _, spec in inputs.values()],
        out_specs=[spec for _, _, spec in outputs.values()],
        scratch_shapes=list(scratch.values()),
        compiler_params=pltpu.CompilerParams(
            collective_id=0, has_side_effects=True, vmem_limit_bytes=vmem_bytes(scratch.values())
        ),
    )(*[value for value, _ in inputs.values()])


def shards(
    inputs,
    cotangent,
    segments,
    tasks,
    table,
    capacity,
    gains,
    w_qkv,
    w_out,
    w_cross,
    w_router,
    w_up,
    w_down,
):
    experts = lax.axis_size("expert")
    z = Sizes(inputs, w_qkv, w_cross, w_router, w_up, table, experts)
    model = z.model
    arrays = SimpleNamespace(
        segments=segments[0],
        tasks=tasks[0, :, :, 0],
        table=table[0].T,
        capacity=capacity,
        inputs=inputs[0],
        cotangent=cotangent[0],
        gains=gains.reshape(1, 3 * model),
        w_router=w_router[0].T,
        w_qkv=w_qkv[0],
        w_out=w_out[0],
        w_cross=w_cross[0],
        w_up=w_up[0, 0],
        w_down=w_down[0, 0],
    )
    out, inputs_grad, gains_grad, router_grad, *grads = run_kernel(z, arrays)
    qkv_grad, out_grad, cross_grad, up_grad, down_grad = [grad.astype(F32) for grad in grads]
    return (
        out[None],
        inputs_grad[None],
        gains_grad.reshape(1, 3, model),
        qkv_grad[None],
        out_grad[None],
        cross_grad[None],
        router_grad.T[None],
        up_grad[None, None],
        down_grad[None, None],
    )


def solution(mesh):
    in_specs = (
        P("section", None, "expert", None),
        P("section", None, "expert", None),
        P("section", None, "expert"),
        P("section", None, "expert", None),
        P("section", None, None),
        P("section"),
        P("section", None, None),
        P("section", None, None),
        P("section", None, None),
        P("section", None, None),
        P("section", None, None),
        P("section", "expert", None, None),
        P("section", "expert", None, None),
    )
    out_specs = (
        P("section", None, "expert", None),
        P("section", None, "expert", None),
        P("section", None, None),
        P("section", None, None),
        P("section", None, None),
        P("section", None, None),
        P("section", None, None),
        P("section", "expert", None, None),
        P("section", "expert", None, None),
    )
    return jax.shard_map(shards, mesh=mesh, in_specs=in_specs, out_specs=out_specs, check_vma=False)
```

```python
import math
from types import SimpleNamespace

import jax
import jax.numpy as jnp
from jax import lax
from jax.experimental import pallas as pl
from jax.experimental.pallas import tpu as pltpu
from jax.sharding import PartitionSpec as P

HEADS = 8
EPSILON = 1e-06
LANES = 128
UNROLL = 4
MESH = pl.DeviceIdType.MESH
F32 = jnp.float32
BF16 = jnp.bfloat16

INFO_TASK, INFO_RANK, INFO_COUNT = (0, 2, 4)
ROWS, REPLY, MIRROR, SUMS, MEMORY, SENT = (1000, 2000, 3000, 4000, 5000, 10000)


def round_up(value, unit):
    return -(-value // unit) * unit


def dot(left, right):
    return jnp.dot(left, right, preferred_element_type=F32)


def dot_rows(left, right):
    return lax.dot_general(left, right, (((0,), (0,)), ((), ())), preferred_element_type=F32)


def dot_cols(left, right):
    return lax.dot_general(left, right, (((1,), (1,)), ((), ())), preferred_element_type=F32)


def lane_sum(value):
    return jnp.sum(value, axis=-1, keepdims=True)


def row_sum(value):
    return jnp.sum(value, axis=0, keepdims=True)


def when_equal(left, right, value=1.0):
    return jnp.where(left == right, value, 0.0)


def iota(shape, axis):
    return lax.broadcasted_iota(jnp.int32, shape, axis).astype(F32)


def whole_part(value, unit):
    return jnp.floor((value + 0.5) * (1.0 / unit))


def inverse_rms(value):
    return lax.rsqrt(jnp.mean(value * value, axis=-1, keepdims=True) + EPSILON)


def norm(value, gain):
    return value * inverse_rms(value) * gain


def norm_back(value, gain, grad):
    scale = inverse_rms(value)
    unit = value * scale
    scaled = grad * gain
    grad_value = scale * (scaled - unit * jnp.mean(scaled * unit, axis=-1, keepdims=True))
    return grad_value, row_sum(grad * unit)


def gelu_and_slope(hidden):
    rate = math.sqrt(2.0 / math.pi)
    square = hidden * hidden
    bend = jnp.tanh(hidden * (rate + rate * 0.044715 * square))
    share = 0.5 + 0.5 * bend
    act = hidden * share
    slope = share + act * (1.0 - bend) * (rate + 3.0 * rate * 0.044715 * square)
    return act, slope


class Sizes:
    def __init__(self, inputs, w_qkv, w_cross, w_router, w_up, table, experts):
        _, self.micro, self.tok, self.model = inputs.shape
        self.hidden = w_up.shape[-1]
        self.experts = experts
        self.tasks = table.shape[1]
        self.slots = 2 * self.tok
        self.halves = 2
        self.group = experts // self.halves
        self.bound = max(2, 6 * self.tok // experts)
        self.send = round_up(self.bound, 16)
        self.merged = self.halves * self.bound <= self.send
        self.flights = 1 if self.merged else self.halves
        self.half_rows = self.group * self.send
        self.all_rows = self.flights * self.half_rows
        self.misc = round_up(w_router.shape[-1] + 3, LANES)
        self.qkv_blocks = w_qkv.shape[-1] // LANES
        self.out_blocks = self.model // LANES
        self.cross_blocks = w_cross.shape[-1] // LANES
        self.misc_blocks = self.misc // LANES
        self.blocks = self.qkv_blocks + self.out_blocks + self.cross_blocks + self.misc_blocks
        self.bits = experts.bit_length() - 1
        unit = 16 * experts
        self.groups = []
        start = 0
        for blocks, count in (
            (self.cross_blocks, 3),
            (self.out_blocks, 2),
            (self.qkv_blocks + self.misc_blocks, 6),
        ):
            units = -(-blocks * self.model // unit)
            count = min(count, units)
            group = []
            for part in range(count):
                size = (units // count + (part < units % count)) * unit
                group.append((start, size))
                start += size
            self.groups.append(group)
        self.parts = sum(len(group) for group in self.groups)
        self.dense_rows = start


def kernel_body(z, names, *refs):
    r = SimpleNamespace(**dict(zip(names, refs)))
    me = lax.axis_index("expert")
    section = lax.axis_index("section")
    tok, model, micro, group, send, slots = (z.tok, z.model, z.micro, z.group, z.send, z.slots)
    here = lax.rem(me, group)
    base = me - here
    mirror = lax.rem(me + group, z.experts)
    me_f = me.astype(F32)
    here_f = here.astype(F32)
    base_f = base.astype(F32)
    enc_f = 1.0 - section.astype(F32)

    side = [None]
    owed = {}

    def on_section(index):
        def put(run):
            side[0] = index
            pl.when(section == index)(run)
            side[0] = None

        return put

    enc, dec = (on_section(0), on_section(1))

    def wait_for(ref, sem):
        pltpu.make_async_copy(ref, ref, sem).wait()

    def owe(key, copy):
        owed[side[0], key] = copy

    def settle(key):
        found = [e for e in owed if e[1] == key and (side[0] in (None, e[0]) or e[0] is None)]
        copies = [owed.pop(entry) for entry in found]
        if side[0] is not None and found[0][0] is None:
            owed[1 - side[0], key] = copies[0]
        wait_for(*copies[0]())

    def settle_all():
        for index in (None, 0, 1):
            waits = [owed.pop(entry) for entry in list(owed) if entry[0] == index]

            def run():
                for copy in waits:
                    wait_for(*copy())

            if index is None:
                run()
            else:
                pl.when(section == index)(run)

    loads = [
        pltpu.make_async_copy(source, target, r.load_sem.at[i])
        for i, (source, target) in enumerate(
            (
                (r.w_qkv, r.wqkv),
                (r.w_out, r.wout),
                (r.w_cross, r.wcross),
                (r.w_up, r.wup),
                (r.w_down, r.wdown),
            )
        )
    ]
    for load in loads:
        load.start()

    barrier = pltpu.get_barrier_semaphore()

    def greet(step, _):
        pl.semaphore_signal(
            barrier,
            inc=1,
            device_id={"expert": lax.rem(me + step, z.experts)},
            device_id_type=MESH,
        )
        return 0

    lax.fori_loop(1, z.experts, greet, 0)
    pl.semaphore_signal(
        barrier, inc=1, device_id={"section": 1 - section}, device_id_type=MESH
    )

    seg_rows = r.segments[...].astype(F32)
    task_rows = r.tasks[...].astype(F32)
    blank = jnp.zeros((LANES - 2 * micro, LANES), F32)
    flipped = jnp.transpose(jnp.concatenate([seg_rows, task_rows, blank], axis=0))
    lane = iota((1, LANES), 1)
    earlier = jnp.where(iota((tok, tok), 0) < iota((tok, tok), 1), 1.0, 0.0)
    ranks, counts = ([], [])
    for m in range(micro):
        task_col = flipped[:, micro + m : micro + m + 1]
        ranks.append(row_sum(when_equal(task_col, task_rows[m : m + 1]) * earlier))
        counts.append(row_sum(when_equal(task_col, lane)))
    r.infos[0] = jnp.concatenate(
        [task_rows, *ranks, *counts, jnp.zeros((8 - 3 * micro, LANES), F32)], axis=0
    )

    table = r.table[...].astype(F32)
    table_lane = iota((1, z.tasks), 1)

    def task_of(expert):
        return lane_sum(
            when_equal(table[0:1], expert, table_lane) + when_equal(table[1:2], expert, table_lane)
        )

    line = iota((z.half_rows, 1), 0)
    line_block = whole_part(line, send)
    line_rank = line - line_block * send
    line_place = here_f + line_block
    line_place = jnp.where(line_place >= group, line_place - group, line_place)
    line_task = task_of(base_f + line_place)

    def fill_pick(half):
        rank_here = line_rank - (half * z.bound if z.merged else 0)
        info = r.infos[half * group]
        for m in range(micro):
            hit = (info[INFO_TASK + m : INFO_TASK + m + 1] == line_task) & (
                info[INFO_RANK + m : INFO_RANK + m + 1] == rank_here
            )
            r.pick[half, m] = jnp.where(hit, 1.0, 0.0).astype(BF16)

    fill_pick(0)

    def greet_back():
        pl.semaphore_wait(barrier, z.experts)

        def tell(step, _):
            pltpu.make_async_remote_copy(
                src_ref=r.infos.at[0],
                dst_ref=r.infos.at[step],
                send_sem=r.info_send,
                recv_sem=r.info_recv,
                device_id={"expert": lax.rem(me + step, z.experts)},
                device_id_type=MESH,
            ).start()
            return 0

        lax.fori_loop(1, z.experts, tell, 0)
        others_told = pl.ds(1, z.experts - 1)
        owe(SENT, lambda: (r.infos.at[others_told], r.info_send))
        owe(0, lambda: (r.infos.at[others_told], r.info_recv))

    def spread(way, m, half, rows, back):
        packed, landed = (
            (r.reply_out, r.reply_in) if back else (r.rows_out, r.rows_in)
        )
        send_sem, recv_sem = (
            (r.reply_send, r.reply_recv) if back else (r.rows_send, r.rows_recv)
        )
        packed[way, m, half] = rows.reshape(group, send, model)
        landed[way, m, half, 0] = rows[:send]

        def push(step, _):
            if back:
                other = lax.rem(here + group - step, group)
            else:
                other = lax.rem(here + step, group)
            pltpu.make_async_remote_copy(
                src_ref=packed.at[way, m, half, step],
                dst_ref=landed.at[way, m, half, step],
                send_sem=send_sem.at[way, m, half],
                recv_sem=recv_sem.at[way, m, half],
                device_id={"expert": base + other},
                device_id_type=MESH,
            ).start()
            return 0

        lax.fori_loop(1, group, push, 0, unroll=group <= 8)
        key = (REPLY if back else ROWS) + 100 * way + 10 * m + half
        others = pl.ds(1, group - 1)
        at = (way, m, half)
        owe(SENT + key, lambda: (packed.at[(*at, others)], send_sem.at[at]))
        owe(key, lambda: (landed.at[(*at, others)], recv_sem.at[at]))

    def ship(key, source, target, sems, device_id):
        copy = pltpu.make_async_remote_copy(
            src_ref=source(),
            dst_ref=target(),
            send_sem=sems()[0],
            recv_sem=sems()[1],
            device_id=device_id,
            device_id_type=MESH,
        )
        copy.start()
        owe(SENT + key, lambda: (source(), sems()[0]))

    def swap(key, source, target, sems):
        ship(key, source, target, sems, {"expert": mirror})
        owe(key, lambda: (target(), sems()[1]))

    def dispatch(way, m, source):
        swap(
            MIRROR + 10 * way + m,
            lambda: source.at[m],
            lambda: r.mirror_rows.at[way, m],
            lambda: (r.mirror_send.at[way, m], r.mirror_recv.at[way, m]),
        )
        if not z.merged:
            spread(way, m, 0, dot(r.pick[0, m], source[m]).astype(BF16), False)

    def dispatch_mirror(way, m, source):
        settle(MIRROR + 10 * way + m)
        rows = dot(r.pick[1, m], r.mirror_rows[way, m])
        if z.merged:
            rows += dot(r.pick[0, m], source[m])
        spread(way, m, z.flights - 1, rows.astype(BF16), False)

    def arrived(way, m):
        for half in range(z.flights):
            settle(ROWS + 100 * way + 10 * m + half)
        return dot(r.compact[m], r.rows_in[way, m].reshape(z.all_rows, model))

    def combine(way, m, rows):
        reply = dot_rows(r.compact[m], rows).astype(BF16)
        for half in reversed(range(z.flights)):
            spread(way, m, half, reply[half * z.half_rows : (half + 1) * z.half_rows], True)

    def gathered(way, m, half):
        flight = 0 if z.merged else half
        if not z.merged or half == 1:
            settle(REPLY + 100 * way + 10 * m + flight)
        return dot_rows(r.pick[half, m], r.reply_in[way, m, flight].reshape(z.half_rows, model))

    def combine_mirror(way, m):
        r.sums_out[way, m] = gathered(way, m, 1).astype(BF16)
        swap(
            SUMS + 10 * way + m,
            lambda: r.sums_out.at[way, m],
            lambda: r.sums_in.at[way, m],
            lambda: (r.sums_send.at[way, m], r.sums_recv.at[way, m]),
        )

    def combine_end(way, m):
        own = gathered(way, m, 0)
        settle(SUMS + 10 * way + m)
        return own + r.sums_in[way, m].astype(F32)

    greet_back()

    @dec
    def _():
        dispatch(1, 0, r.cotangent)
        settle(0)
        fill_pick(1)
        dispatch_mirror(1, 0, r.cotangent)

    low_lane = jnp.where(iota((1, LANES), 1) < LANES // 2, 1.0, 0.0)
    high_lane = 1.0 - low_lane
    low_bf, high_bf = (low_lane.astype(BF16), high_lane.astype(BF16))
    pairs = model // LANES
    score_scale = (model // HEADS) ** (-0.5)

    def stacked(block):
        return jnp.concatenate([block * low_bf, block * high_bf], axis=0)

    def merged(block):
        return block[:tok] * low_lane + block[tok:] * high_lane

    def attend(queries, keys, values, allowed):
        scores = dot_cols(stacked(queries), keys) * score_scale
        if allowed is not None:
            scores = jnp.where(allowed > 0.5, scores, -1000000000.0)
        top = jnp.max(scores, axis=-1, keepdims=True)
        grown = jnp.exp(scores - top)
        probs = grown / lane_sum(grown)
        return probs, merged(dot(probs.astype(BF16), values))

    def attend_back(queries, keys, values, probs, grad_mixed):
        grad_stack = stacked(grad_mixed)
        grad_probs = dot_cols(grad_stack, values)
        inner = lane_sum(probs * grad_probs)
        grad_scores = (probs * (grad_probs - inner)).astype(BF16)
        grad_queries = merged(dot(grad_scores, keys)) * score_scale
        grad_keys = dot_rows(grad_scores, stacked(queries)) * score_scale
        grad_values = dot_rows(probs.astype(BF16), grad_stack)
        return grad_queries, grad_keys, grad_values

    def cols(index, start=0):
        return pl.ds(pl.multiple_of(start + index * LANES, LANES), LANES)

    def each_pair(run):
        def step(pair, _):
            run(pair)
            return 0

        lax.fori_loop(0, pairs, step, 0, unroll=UNROLL)

    gain_a, gain_c, gain_m = [r.gains[:, i * model : (i + 1) * model] for i in range(3)]

    def enter_experts(m):
        r.normed_m[m] = norm(r.after_cross[m], gain_m).astype(BF16)
        dispatch(0, m, r.normed_m)

    loads[0].wait()
    loads[1].wait()
    for m in range(micro):
        x_in = r.inputs[m].astype(F32)
        normed_a = norm(x_in, gain_a).astype(BF16)
        r.normed_a[m] = normed_a
        r.qkv[m] = dot(normed_a, r.wqkv[...]).astype(BF16)
        causal = jnp.where(iota((tok, tok), 1) <= iota((tok, tok), 0), 1.0, enc_f)
        allowed = when_equal(flipped[:, m : m + 1], seg_rows[m : m + 1]) * causal
        allowed = jnp.concatenate([allowed, allowed], axis=0)
        @each_pair
        def _(pair):
            probs, mixed = attend(
                r.qkv[m, :, cols(pair)],
                r.qkv[m, :, cols(pair, model)],
                r.qkv[m, :, cols(pair, 2 * model)],
                allowed,
            )
            r.probs_self[m, pair] = probs
            r.attn_rows[m, :, cols(pair)] = mixed.astype(BF16)
        after_self = x_in + dot(r.attn_rows[m], r.wout[...])

        @enc
        def _():
            r.after_cross[m] = after_self
            enter_experts(m)

        @dec
        def _():
            r.after_self[m] = after_self

    loads[2].wait()

    def send_memory(m):
        index = m + micro * side[0]
        ship(
            MEMORY + index,
            lambda: r.memory_out.at[m],
            lambda: r.memory.at[m],
            lambda: (r.memory_send.at[index], r.memory_recv.at[index]),
            {"section": 1 - section},
        )

    def wait_memory(m):
        index = m + micro * (1 - side[0])
        owe(MEMORY + index, lambda: (r.memory.at[m], r.memory_recv.at[index]))
        settle(MEMORY + index)

    @enc
    def _():
        settle(0)
        fill_pick(1)

    @dec
    def _():
        for m in range(micro):
            after_self = r.after_self[m]
            normed_c = norm(after_self, gain_c).astype(BF16)
            r.normed_c[m] = normed_c
            r.cross_q[m] = dot(normed_c, r.wcross[:, :model]).astype(BF16)
            wait_memory(m)

            @each_pair
            def _(pair):
                probs, mixed = attend(
                    r.cross_q[m, :, cols(pair)],
                    r.memory[m, :, cols(pair)],
                    r.memory[m, :, cols(pair, model)],
                    None,
                )
                r.probs_cross[m, pair] = probs
                r.cross_rows[m, :, cols(pair)] = mixed.astype(BF16)

            r.after_cross[m] = after_self + dot_cols(r.cross_rows[m], r.wcross[:, model:])
            enter_experts(m)

    for m in range(micro):
        dispatch_mirror(0, m, r.normed_m)

    @dec
    def _():
        for m in range(1, micro):
            dispatch(1, m, r.cotangent)
        for m in range(1, micro):
            dispatch_mirror(1, m, r.cotangent)

    own_task = task_of(me_f)
    partner = lane_sum(when_equal(table_lane, own_task, table[0:1] + table[1:2])) - me_f
    capacity = r.capacity[0].astype(F32)
    place = iota((1, z.all_rows), 1)
    block = whole_part(place, send)
    place_rank = place - block * send
    place_half = whole_part(block, group)
    sender = here_f - (block - place_half * group)
    if z.merged:
        place_half = jnp.minimum(whole_part(place_rank, z.bound), 1.0)
        place_rank = place_rank - place_half * z.bound
    sender = base_f + jnp.where(sender < 0.0, sender + group, sender) + place_half * group
    sender = jnp.where(sender >= z.experts, sender - z.experts, sender)
    teller = me_f - iota((z.experts, 1), 0)
    teller = jnp.where(teller < 0.0, teller + z.experts, teller)
    for m in range(micro):
        told = lane_sum(jnp.where(lane == own_task, r.infos[:, INFO_COUNT + m, :], 0.0))
        count = row_sum(when_equal(teller, sender, told))
        slot = row_sum(jnp.where(teller < sender, told, 0.0)) + place_rank
        slot = jnp.where((place_rank < count) & (slot < capacity), slot, -1.0)
        r.compact[m] = when_equal(iota((slots, 1), 0), slot).astype(BF16)

    router = r.w_router[...]
    routers = router.shape[0]
    expert_lane = iota((8, routers), 1)
    sign = when_equal(expert_lane, me_f) - when_equal(expert_lane, partner)
    router_step = dot(sign.astype(BF16), router)[0:1]
    tile = 1024

    def each_tile(width, run):
        def step(index, _):
            run(pl.ds(pl.multiple_of(index * tile, tile), tile))
            return 0

        lax.fori_loop(0, width // tile, step, 0)

    def expert_forward(m):
        taken = arrived(0, m).astype(BF16)
        r.taken[m] = taken

        def up_tile(at):
            act, slope = gelu_and_slope(dot(r.taken[m], r.wup[:, at]))
            r.act[m, :, at] = act.astype(BF16)
            r.slope[m, :, at] = slope.astype(BF16)

        each_tile(z.hidden, up_tile)
        gap = lane_sum(taken.astype(F32) * router_step)
        small = jnp.exp(-jnp.abs(gap))
        large = 1.0 / (1.0 + small)
        gate = jnp.where(gap >= 0.0, large, small * large)
        r.gate[m] = gate
        r.gate_slope[m] = small * large * large

        r.expert_out[m] = dot(r.act[m], r.wdown[...]).astype(BF16)
        r.gated[m] = (gate * r.expert_out[m].astype(F32)).astype(BF16)

    def expert_backward(m):
        grad_final = arrived(1, m)
        grad_gate = lane_sum(r.expert_out[m].astype(F32) * grad_final)
        grad_gap = r.gate_slope[m] * grad_gate
        r.grad_gap[m] = grad_gap
        r.grad_out[m] = (r.gate[m] * grad_final).astype(BF16)

        def act_tile(at):
            grad_act = dot_cols(r.grad_out[m], r.wdown[at, :])
            r.grad_hidden[m, :, at] = (grad_act * r.slope[m, :, at].astype(F32)).astype(BF16)

        each_tile(z.hidden, act_tile)

        rounded = dot_cols(r.grad_hidden[m], r.wup[...]).astype(BF16).astype(F32)
        combine(1, m, (rounded + grad_gap * router_step).astype(BF16))

    loads[3].wait()
    loads[4].wait()

    @dec
    def _():
        for m in range(micro):
            expert_forward(m)
            expert_backward(m)
        for m in range(micro):
            combine(0, m, r.gated[m])
            r.grad_state[m] = r.cotangent[m].astype(F32)

    @enc
    def _():
        for m in range(micro):
            expert_forward(m)
            combine(0, m, r.gated[m])
        for m in range(micro):
            combine_mirror(0, m)
        for m in range(micro):
            layer_final = r.after_cross[m] + combine_end(0, m)
            r.layer_final[m] = layer_final
            r.layer_out[m] = layer_final.astype(BF16)
            normed_k = norm(layer_final, gain_c).astype(BF16)
            r.normed_c[m] = normed_k
            r.memory_out[m] = dot(normed_k, r.wcross[...]).astype(BF16)
            send_memory(m)
        gain_grad = jnp.zeros((1, model), F32)
        for m in range(micro):
            wait_memory(m)
            grad_normed = dot_cols(r.memory[m], r.wcross[...])
            grad_state, grad_gain = norm_back(r.layer_final[m], gain_c, grad_normed)
            gain_grad += grad_gain
            grad_final = r.cotangent[m].astype(F32) + grad_state
            r.grad_state[m] = grad_final
            r.grad_rows[m] = grad_final.astype(BF16)
            dispatch(1, m, r.grad_rows)
        for m in range(micro):
            dispatch_mirror(1, m, r.grad_rows)
        r.gain_grads[1:2] = gain_grad
        for m in range(micro):
            expert_backward(m)

    def flat(ref, at=slice(None)):
        value = ref[:, :, at]
        return value.reshape(value.shape[0] * value.shape[1], value.shape[2])

    saves = []

    def save(source, target):
        copy = pltpu.make_async_copy(source, target, r.save_sem.at[len(saves)])
        copy.start()
        saves.append(copy)

    def up_grad(at):
        r.wup[:, at] = dot_rows(flat(r.taken), flat(r.grad_hidden, at)).astype(BF16)

    def down_grad(at):
        r.wdown[at, :] = dot_rows(flat(r.act, at), flat(r.grad_out)).astype(BF16)

    each_tile(z.hidden, up_grad)
    save(r.wup, r.up_grad)
    for m in range(micro):
        combine_mirror(1, m)
    each_tile(z.hidden, down_grad)
    save(r.wdown, r.down_grad)

    gain_grad = jnp.zeros((1, model), F32)
    for m in range(micro):
        grad_state, grad_gain = norm_back(r.after_cross[m], gain_m, combine_end(1, m))
        gain_grad += grad_gain
        r.grad_state[m] += grad_state

        @dec
        def _():
            grad_y = r.grad_state[m].astype(BF16)
            r.grad_cross[m] = grad_y
            r.grad_mix[...] = dot(grad_y, r.wcross[:, model:]).astype(BF16)

            @each_pair
            def _(pair):
                at = cols(pair)
                grad_q, grad_k, grad_v = attend_back(
                    r.cross_q[m, :, at],
                    r.memory[m, :, at],
                    r.memory[m, :, cols(pair, model)],
                    r.probs_cross[m, pair],
                    r.grad_mix[:, at],
                )
                r.grad_cross_q[m, :, at] = grad_q.astype(BF16)
                r.memory_out[m, :, at] = grad_k.astype(BF16)
                r.memory_out[m, :, cols(pair, model)] = grad_v.astype(BF16)
            send_memory(m)

    r.gain_grads[2:3] = gain_grad

    @dec
    def _():
        gain_grad = jnp.zeros((1, model), F32)
        for m in range(micro):
            grad_normed = dot_cols(r.grad_cross_q[m], r.wcross[:, :model])
            grad_state, grad_gain = norm_back(r.after_self[m], gain_c, grad_normed)
            gain_grad += grad_gain
            r.grad_state[m] += grad_state
        r.gain_grads[1:2] = gain_grad

    first_cross = 0
    first_out = first_cross + z.cross_blocks
    first_qkv = first_out + z.out_blocks
    first_misc = first_qkv + z.qkv_blocks

    def store_blocks(first, left, right):
        width = 2 * LANES
        left = flat(left)
        for start in range(0, right.shape[-1], width):
            grad = dot_rows(left, flat(right, pl.ds(start, width))).astype(BF16)
            at = (first + start // LANES) * model
            r.dense[at : at + model] = grad[:, :LANES]
            r.dense[at + model : at + 2 * model] = grad[:, LANES:]

    bits = list(range(z.bits))
    lead = min(3, z.bits)
    parts = []
    for group_index, group_parts in enumerate(z.groups):
        for start, size in group_parts:
            turn = len(parts) % lead
            parts.append(
                SimpleNamespace(
                    index=len(parts),
                    group=group_index,
                    order=bits[turn:lead] + bits[:turn] + bits[lead:],
                    at=jnp.int32(start),
                    size=size,
                    land=start,
                    stage=0,
                    copy=None,
                )
            )

    def aligned(start, size):
        return pl.ds(pl.multiple_of(start, 16), size)

    def start_stage(part):
        halving = part.stage < z.bits
        stride = 1 << part.order[part.stage if halving else 2 * z.bits - 1 - part.stage]
        part.bit = lax.rem(lax.div(me, stride), 2)
        if halving:
            half = part.size // 2
            source = r.dense.at[aligned(part.at + (1 - part.bit) * half, half)]
            target = r.partial.at[pl.ds(part.land, half)]
        else:
            source = target = r.total.at[aligned(part.at, part.size)]
        part.copy = pltpu.make_async_remote_copy(
            src_ref=source,
            dst_ref=target,
            send_sem=r.sum_send.at[part.index, part.stage],
            recv_sem=r.sum_recv.at[part.index, part.stage],
            device_id={"expert": me + (1 - 2 * part.bit) * stride},
            device_id_type=MESH,
        )
        part.copy.start()

    def end_stage(part):
        part.copy.wait()
        if part.stage < z.bits:
            half = part.size // 2
            part.at = part.at + part.bit * half
            rows = aligned(part.at, half)
            came = r.partial[pl.ds(part.land, half)].astype(F32)
            target = r.total if part.stage == z.bits - 1 else r.dense
            target[rows] = (r.dense[rows].astype(F32) + came).astype(BF16)
            part.land += half
            part.size = half
        else:
            part.at = part.at - part.bit * part.size
            part.size *= 2
        part.stage += 1

    def begin(group_index):
        for part in parts:
            if part.group == group_index:
                start_stage(part)

    def advance(group_index):
        for part in parts:
            if part.group == group_index and part.stage < 2 * z.bits:
                end_stage(part)
                if part.stage < 2 * z.bits:
                    start_stage(part)

    @enc
    def _():
        store_blocks(first_cross, r.normed_c, r.memory)

    @dec
    def _():
        store_blocks(first_cross, r.normed_c, r.grad_cross_q)
        store_blocks(first_cross + z.out_blocks, r.grad_cross, r.cross_rows)

    begin(0)
    for m in range(micro):
        r.grad_self[m] = r.grad_state[m].astype(BF16)
    store_blocks(first_out, r.attn_rows, r.grad_self)
    begin(1)

    gain_grad = jnp.zeros((1, model), F32)
    for m in range(micro):
        grad_top = r.grad_state[m]
        grad_y = r.grad_self[m]
        r.grad_mix[...] = dot_cols(grad_y, r.wout[...]).astype(BF16)

        @each_pair
        def _(pair):
            grads = attend_back(
                r.qkv[m, :, cols(pair)],
                r.qkv[m, :, cols(pair, model)],
                r.qkv[m, :, cols(pair, 2 * model)],
                r.probs_self[m, pair],
                r.grad_mix[:, cols(pair)],
            )
            for third, grad in enumerate(grads):
                r.grad_qkv[m, :, cols(pair, third * model)] = grad.astype(BF16)
        grad_normed = dot_cols(r.grad_qkv[m], r.wqkv[...])
        grad_state, grad_gain = norm_back(r.inputs[m].astype(F32), gain_a, grad_normed)
        gain_grad += grad_gain
        r.inputs_grad[m] = grad_top + grad_state
    r.gain_grads[0:1] = gain_grad
    r.gain_grads[3:8] = jnp.zeros((5, model), F32)

    store_blocks(first_qkv, r.normed_a, r.grad_qkv)
    misc_row = iota((1, z.misc), 1)
    misc_sign = when_equal(misc_row, me_f) - when_equal(misc_row, partner)
    misc = jnp.zeros((z.misc, model), F32)
    for m in range(micro):
        steps = r.grad_gap[m] * misc_sign
        top = steps.astype(BF16)
        rest = (steps - top.astype(F32)).astype(BF16)
        misc += dot_rows(top, r.taken[m]) + dot_rows(rest, r.taken[m])
    place_gain = when_equal(iota((8, z.misc), 1), iota((8, z.misc), 0) + routers)
    misc += dot_rows(place_gain.astype(BF16), r.gain_grads[...].astype(BF16))
    misc_rows = [
        pl.ds(first_misc * model + index * z.misc, z.misc) for index in range(model // LANES)
    ]
    for index, rows in enumerate(misc_rows):
        r.dense[rows] = misc[:, index * LANES : (index + 1) * LANES].astype(BF16)
    used = z.blocks * model
    if used < z.dense_rows:
        r.dense[used:] = jnp.zeros((z.dense_rows - used, LANES), BF16)
    begin(2)
    advance(0)
    advance(1)

    @dec
    def _():
        for m in range(micro):
            combine_mirror(0, m)
        for m in range(micro):
            r.layer_out[m] = (r.after_cross[m] + combine_end(0, m)).astype(BF16)

    while any(part.stage < 2 * z.bits for part in parts):
        for group_index in range(3):
            advance(group_index)

    for target, first, count in (
        (r.cross_grad, first_cross, z.cross_blocks),
        (r.out_grad, first_out, z.out_blocks),
        (r.qkv_grad, first_qkv, z.qkv_blocks),
    ):
        for index in range(count):
            rows = pl.ds((first + index) * model, model)
            save(r.total.at[rows], target.at[:, pl.ds(index * LANES, LANES)])
    for index, rows in enumerate(misc_rows):
        sums = r.total[rows].astype(F32)
        r.router_grad[:, index * LANES : (index + 1) * LANES] = sums[:routers]
        for row in range(3):
            at = row * model + index * LANES
            r.gains_grad[:, at : at + LANES] = sums[routers + row : routers + row + 1]
    for copy in saves:
        copy.wait()

    settle_all()


def vmem_bytes(buffers):
    total = 0
    for buffer in buffers:
        if buffer.memory_space == pltpu.VMEM:
            *lead, rows, lanes = buffer.shape
            size = math.prod(lead) * round_up(rows, 8) * round_up(lanes, LANES)
            total += size * jnp.dtype(buffer.dtype).itemsize
    return min(total + 5 * 1024 * 1024, 62 * 1024 * 1024)


def run_kernel(z, arrays):
    micro, tok, model, hidden = (z.micro, z.tok, z.model, z.hidden)
    vmem = pl.BlockSpec(memory_space=pltpu.VMEM)
    hbm = pl.BlockSpec(memory_space=pl.ANY)
    inputs = dict(
        segments=(arrays.segments, vmem),
        tasks=(arrays.tasks, vmem),
        table=(arrays.table, vmem),
        capacity=(arrays.capacity, pl.BlockSpec(memory_space=pltpu.SMEM)),
        inputs=(arrays.inputs, vmem),
        cotangent=(arrays.cotangent, vmem),
        gains=(arrays.gains, vmem),
        w_router=(arrays.w_router, vmem),
        w_qkv=(arrays.w_qkv, hbm),
        w_out=(arrays.w_out, hbm),
        w_cross=(arrays.w_cross, hbm),
        w_up=(arrays.w_up, hbm),
        w_down=(arrays.w_down, hbm),
    )
    rows = (micro, tok, model)
    slot_rows = (micro, z.slots, model)
    slot_hidden = (micro, z.slots, hidden)
    outputs = dict(
        layer_out=(rows, BF16, vmem),
        inputs_grad=(rows, F32, vmem),
        gains_grad=((1, 3 * model), F32, vmem),
        router_grad=(arrays.w_router.shape, F32, vmem),
        qkv_grad=(arrays.w_qkv.shape, BF16, hbm),
        out_grad=(arrays.w_out.shape, BF16, hbm),
        cross_grad=(arrays.w_cross.shape, BF16, hbm),
        up_grad=(arrays.w_up.shape, BF16, hbm),
        down_grad=(arrays.w_down.shape, BF16, hbm),
    )
    blocks = (2, micro, z.flights, z.group, z.send, model)
    pairs = model // LANES
    dma = pltpu.SemaphoreType.DMA
    scratch = dict(
        wqkv=pltpu.VMEM(arrays.w_qkv.shape, BF16),
        wout=pltpu.VMEM(arrays.w_out.shape, BF16),
        wcross=pltpu.VMEM(arrays.w_cross.shape, BF16),
        wup=pltpu.VMEM(arrays.w_up.shape, BF16),
        wdown=pltpu.VMEM(arrays.w_down.shape, BF16),
        infos=pltpu.VMEM((z.experts, 8, LANES), F32),
        normed_a=pltpu.VMEM(rows, BF16),
        qkv=pltpu.VMEM((micro, tok, 3 * model), BF16),
        probs_self=pltpu.VMEM((micro, pairs, 2 * tok, tok), F32),
        attn_rows=pltpu.VMEM(rows, BF16),
        after_self=pltpu.VMEM(rows, F32),
        normed_c=pltpu.VMEM(rows, BF16),
        cross_q=pltpu.VMEM(rows, BF16),
        probs_cross=pltpu.VMEM((micro, pairs, 2 * tok, tok), F32),
        cross_rows=pltpu.VMEM(rows, BF16),
        memory_out=pltpu.VMEM((micro, tok, 2 * model), BF16),
        memory=pltpu.VMEM((micro, tok, 2 * model), BF16),
        after_cross=pltpu.VMEM(rows, F32),
        normed_m=pltpu.VMEM(rows, BF16),
        layer_final=pltpu.VMEM(rows, F32),
        grad_state=pltpu.VMEM(rows, F32),
        grad_rows=pltpu.VMEM(rows, BF16),
        grad_cross=pltpu.VMEM(rows, BF16),
        grad_cross_q=pltpu.VMEM(rows, BF16),
        grad_self=pltpu.VMEM(rows, BF16),
        grad_mix=pltpu.VMEM((tok, model), BF16),
        grad_qkv=pltpu.VMEM((micro, tok, 3 * model), BF16),
        gain_grads=pltpu.VMEM((8, model), F32),
        pick=pltpu.VMEM((z.halves, micro, z.half_rows, tok), BF16),
        compact=pltpu.VMEM((micro, z.slots, z.all_rows), BF16),
        rows_out=pltpu.VMEM(blocks, BF16),
        rows_in=pltpu.VMEM(blocks, BF16),
        reply_out=pltpu.VMEM(blocks, BF16),
        reply_in=pltpu.VMEM(blocks, BF16),
        mirror_rows=pltpu.VMEM((2,) + rows, BF16),
        sums_out=pltpu.VMEM((2,) + rows, BF16),
        sums_in=pltpu.VMEM((2,) + rows, BF16),
        taken=pltpu.VMEM(slot_rows, BF16),
        slope=pltpu.VMEM(slot_hidden, BF16),
        act=pltpu.VMEM(slot_hidden, BF16),
        expert_out=pltpu.VMEM(slot_rows, BF16),
        gated=pltpu.VMEM(slot_rows, BF16),
        gate=pltpu.VMEM((micro, z.slots, 1), F32),
        gate_slope=pltpu.VMEM((micro, z.slots, 1), F32),
        grad_gap=pltpu.VMEM((micro, z.slots, 1), F32),
        grad_out=pltpu.VMEM(slot_rows, BF16),
        grad_hidden=pltpu.VMEM(slot_hidden, BF16),
        dense=pltpu.VMEM((z.dense_rows, LANES), BF16),
        total=pltpu.VMEM((z.dense_rows, LANES), BF16),
        partial=pltpu.VMEM((z.dense_rows, LANES), BF16),
        load_sem=dma((5,)),
        save_sem=dma((2 + z.blocks - z.misc_blocks,)),
        info_send=dma(()),
        info_recv=dma(()),
        rows_send=dma((2, micro, z.flights)),
        rows_recv=dma((2, micro, z.flights)),
        reply_send=dma((2, micro, z.flights)),
        reply_recv=dma((2, micro, z.flights)),
        mirror_send=dma((2, micro)),
        mirror_recv=dma((2, micro)),
        sums_send=dma((2, micro)),
        sums_recv=dma((2, micro)),
        memory_send=dma((2 * micro,)),
        memory_recv=dma((2 * micro,)),
        sum_send=dma((z.parts, 2 * z.bits)),
        sum_recv=dma((z.parts, 2 * z.bits)),
    )
    names = [*inputs, *outputs, *scratch]

    def body(*refs):
        kernel_body(z, names, *refs)

    return pl.pallas_call(
        body,
        name="layer_step",
        out_shape=[jax.ShapeDtypeStruct(shape, dtype) for shape, dtype, _ in outputs.values()],
        in_specs=[spec for _, spec in inputs.values()],
        out_specs=[spec for _, _, spec in outputs.values()],
        scratch_shapes=list(scratch.values()),
        compiler_params=pltpu.CompilerParams(
            collective_id=0, has_side_effects=True, vmem_limit_bytes=vmem_bytes(scratch.values())
        ),
    )(*[value for value, _ in inputs.values()])


def widen_body(count, *refs):
    total = (len(refs) - 2) // 4
    sources, targets, came, made = [refs[i * total : (i + 1) * total] for i in range(4)]
    come_sem, go_sem = refs[4 * total :]
    loads = [pltpu.make_async_copy(sources[i], came[i], come_sem.at[i]) for i in range(total)]
    for copy in loads:
        copy.start()
    for i in range(total):
        loads[i].wait()
        if i >= count:
            pltpu.make_async_copy(came[i], targets[i], go_sem.at[i]).start()
            continue
        rows, lanes = came[i].shape
        step_rows = 1 << (min(rows, 128 * 1024 // lanes).bit_length() - 1)

        def step(index, _):
            at = pl.ds(pl.multiple_of(index * step_rows, step_rows), step_rows)
            made[i][at] = came[i][at].astype(F32)
            pltpu.make_async_copy(made[i].at[at], targets[i].at[at], go_sem.at[i]).start()
            return 0

        lax.fori_loop(0, rows // step_rows, step, 0)
    for i in range(total):
        left = made[i] if i < count else came[i]
        pltpu.make_async_copy(left, targets[i], go_sem.at[i]).wait()


def widen(narrow, passed):
    values = [*narrow, *passed]
    count = len(narrow)
    types = [F32] * count + [value.dtype for value in passed]
    hbm = pl.BlockSpec(memory_space=pltpu.HBM)
    dma = pltpu.SemaphoreType.DMA((len(values),))
    blank = pltpu.VMEM((8, LANES), F32)
    return pl.pallas_call(
        lambda *refs: widen_body(count, *refs),
        name="widen",
        out_shape=[jax.ShapeDtypeStruct(v.shape, t) for v, t in zip(values, types)],
        in_specs=[hbm] * len(values),
        out_specs=[hbm] * len(values),
        scratch_shapes=[pltpu.VMEM(value.shape, value.dtype) for value in values]
        + [pltpu.VMEM(value.shape, F32) for value in narrow]
        + [blank] * len(passed)
        + [dma, dma],
        compiler_params=pltpu.CompilerParams(vmem_limit_bytes=62 * 1024 * 1024),
    )(*values)


def shards(
    inputs,
    cotangent,
    segments,
    tasks,
    table,
    capacity,
    gains,
    w_qkv,
    w_out,
    w_cross,
    w_router,
    w_up,
    w_down,
):
    experts = lax.axis_size("expert")
    z = Sizes(inputs, w_qkv, w_cross, w_router, w_up, table, experts)
    model = z.model
    arrays = SimpleNamespace(
        segments=segments[0],
        tasks=tasks[0, :, :, 0],
        table=table[0].T,
        capacity=capacity,
        inputs=inputs[0],
        cotangent=cotangent[0],
        gains=gains.reshape(1, 3 * model),
        w_router=w_router[0].T,
        w_qkv=w_qkv[0],
        w_out=w_out[0],
        w_cross=w_cross[0],
        w_up=w_up[0, 0],
        w_down=w_down[0, 0],
    )
    *passed, qkv_grad, out_grad, cross_grad, up_grad, down_grad = run_kernel(z, arrays)
    narrow = (up_grad, down_grad, qkv_grad, cross_grad, out_grad)
    up_grad, down_grad, qkv_grad, cross_grad, out_grad, *passed = widen(narrow, passed)
    out, inputs_grad, gains_grad, router_grad = passed
    return (
        out[None],
        inputs_grad[None],
        gains_grad.reshape(1, 3, model),
        qkv_grad[None],
        out_grad[None],
        cross_grad[None],
        router_grad.T[None],
        up_grad[None, None],
        down_grad[None, None],
    )


def solution(mesh):
    in_specs = (
        P("section", None, "expert", None),
        P("section", None, "expert", None),
        P("section", None, "expert"),
        P("section", None, "expert", None),
        P("section", None, None),
        P("section"),
        P("section", None, None),
        P("section", None, None),
        P("section", None, None),
        P("section", None, None),
        P("section", None, None),
        P("section", "expert", None, None),
        P("section", "expert", None, None),
    )
    out_specs = (
        P("section", None, "expert", None),
        P("section", None, "expert", None),
        P("section", None, None),
        P("section", None, None),
        P("section", None, None),
        P("section", None, None),
        P("section", None, None),
        P("section", "expert", None, None),
        P("section", "expert", None, None),
    )
    return jax.shard_map(shards, mesh=mesh, in_specs=in_specs, out_specs=out_specs, check_vma=False)
```

```python
import math
from types import SimpleNamespace

import jax
import jax.numpy as jnp
from jax import lax
from jax.experimental import pallas as pl
from jax.experimental.pallas import tpu as pltpu
from jax.sharding import PartitionSpec as P

HEADS = 8
EPSILON = 1e-06
LANES = 128
UNROLL = 4
MESH = pl.DeviceIdType.MESH
F32 = jnp.float32
BF16 = jnp.bfloat16

INFO_TASK, INFO_RANK, INFO_COUNT = (0, 2, 4)
ROWS, REPLY, MIRROR, SUMS, MEMORY, SENT = (1000, 2000, 3000, 4000, 5000, 10000)


def round_up(value, unit):
    return -(-value // unit) * unit


def dot(left, right):
    return jnp.dot(left, right, preferred_element_type=F32)


def dot_rows(left, right):
    return lax.dot_general(left, right, (((0,), (0,)), ((), ())), preferred_element_type=F32)


def dot_cols(left, right):
    return lax.dot_general(left, right, (((1,), (1,)), ((), ())), preferred_element_type=F32)


def lane_sum(value):
    return jnp.sum(value, axis=-1, keepdims=True)


def row_sum(value):
    return jnp.sum(value, axis=0, keepdims=True)


def when_equal(left, right, value=1.0):
    return jnp.where(left == right, value, 0.0)


def iota(shape, axis):
    return lax.broadcasted_iota(jnp.int32, shape, axis).astype(F32)


def whole_part(value, unit):
    return jnp.floor((value + 0.5) * (1.0 / unit))


def inverse_rms(value):
    return lax.rsqrt(jnp.mean(value * value, axis=-1, keepdims=True) + EPSILON)


def norm(value, gain):
    return value * inverse_rms(value) * gain


def norm_back(value, gain, grad):
    scale = inverse_rms(value)
    unit = value * scale
    scaled = grad * gain
    grad_value = scale * (scaled - unit * jnp.mean(scaled * unit, axis=-1, keepdims=True))
    return grad_value, row_sum(grad * unit)


def gelu_and_slope(hidden):
    rate = math.sqrt(2.0 / math.pi)
    square = hidden * hidden
    bend = jnp.tanh(hidden * (rate + rate * 0.044715 * square))
    share = 0.5 + 0.5 * bend
    act = hidden * share
    slope = share + act * (1.0 - bend) * (rate + 3.0 * rate * 0.044715 * square)
    return act, slope


class Sizes:
    def __init__(self, inputs, w_qkv, w_cross, w_router, w_up, table, experts):
        _, self.micro, self.tok, self.model = inputs.shape
        self.hidden = w_up.shape[-1]
        self.experts = experts
        self.tasks = table.shape[1]
        self.slots = 2 * self.tok
        self.halves = 2
        self.group = experts // self.halves
        self.bound = max(2, 6 * self.tok // experts)
        self.send = round_up(self.bound, 16)
        self.merged = self.halves * self.bound <= self.send
        self.flights = 1 if self.merged else self.halves
        self.half_rows = self.group * self.send
        self.all_rows = self.flights * self.half_rows
        self.misc = round_up(w_router.shape[-1] + 3, LANES)
        self.qkv_blocks = w_qkv.shape[-1] // LANES
        self.out_blocks = self.model // LANES
        self.cross_blocks = w_cross.shape[-1] // LANES
        self.misc_blocks = self.misc // LANES
        self.blocks = self.qkv_blocks + self.out_blocks + self.cross_blocks + self.misc_blocks
        self.bits = experts.bit_length() - 1
        unit = 16 * experts
        self.groups = []
        start = 0
        for blocks, count in (
            (self.cross_blocks, 3),
            (self.out_blocks, 2),
            (self.qkv_blocks + self.misc_blocks, 6),
        ):
            units = -(-blocks * self.model // unit)
            count = min(count, units)
            group = []
            for part in range(count):
                size = (units // count + (part < units % count)) * unit
                group.append((start, size))
                start += size
            self.groups.append(group)
        self.parts = sum(len(group) for group in self.groups)
        self.dense_rows = start


def kernel_body(z, names, *refs):
    r = SimpleNamespace(**dict(zip(names, refs)))
    me = lax.axis_index("expert")
    section = lax.axis_index("section")
    tok, model, micro, group, send, slots = (z.tok, z.model, z.micro, z.group, z.send, z.slots)
    here = lax.rem(me, group)
    base = me - here
    mirror = lax.rem(me + group, z.experts)
    me_f = me.astype(F32)
    here_f = here.astype(F32)
    base_f = base.astype(F32)
    enc_f = 1.0 - section.astype(F32)

    side = [None]
    owed = {}

    def on_section(index):
        def put(run):
            side[0] = index
            pl.when(section == index)(run)
            side[0] = None

        return put

    enc, dec = (on_section(0), on_section(1))

    def wait_for(ref, sem):
        pltpu.make_async_copy(ref, ref, sem).wait()

    def owe(key, copy):
        owed[side[0], key] = copy

    def settle(key):
        found = [e for e in owed if e[1] == key and (side[0] in (None, e[0]) or e[0] is None)]
        copies = [owed.pop(entry) for entry in found]
        if side[0] is not None and found[0][0] is None:
            owed[1 - side[0], key] = copies[0]
        wait_for(*copies[0]())

    def settle_all():
        for index in (None, 0, 1):
            waits = [owed.pop(entry) for entry in list(owed) if entry[0] == index]

            def run():
                for copy in waits:
                    wait_for(*copy())

            if index is None:
                run()
            else:
                pl.when(section == index)(run)

    loads = [
        pltpu.make_async_copy(source, target, r.load_sem.at[i])
        for i, (source, target) in enumerate(
            (
                (r.w_qkv, r.wqkv),
                (r.w_out, r.wout),
                (r.w_cross, r.wcross),
                (r.w_up, r.wup),
                (r.w_down, r.wdown),
            )
        )
    ]
    for load in loads:
        load.start()

    barrier = pltpu.get_barrier_semaphore()

    def greet(step, _):
        pl.semaphore_signal(
            barrier,
            inc=1,
            device_id={"expert": lax.rem(me + step, z.experts)},
            device_id_type=MESH,
        )
        return 0

    lax.fori_loop(1, z.experts, greet, 0)
    pl.semaphore_signal(
        barrier, inc=1, device_id={"section": 1 - section}, device_id_type=MESH
    )

    seg_rows = r.segments[...].astype(F32)
    task_rows = r.tasks[...].astype(F32)
    blank = jnp.zeros((LANES - 2 * micro, LANES), F32)
    flipped = jnp.transpose(jnp.concatenate([seg_rows, task_rows, blank], axis=0))
    lane = iota((1, LANES), 1)
    earlier = jnp.where(iota((tok, tok), 0) < iota((tok, tok), 1), 1.0, 0.0)
    ranks, counts = ([], [])
    for m in range(micro):
        task_col = flipped[:, micro + m : micro + m + 1]
        ranks.append(row_sum(when_equal(task_col, task_rows[m : m + 1]) * earlier))
        counts.append(row_sum(when_equal(task_col, lane)))
    r.infos[0] = jnp.concatenate(
        [task_rows, *ranks, *counts, jnp.zeros((8 - 3 * micro, LANES), F32)], axis=0
    )

    table = r.table[...].astype(F32)
    table_lane = iota((1, z.tasks), 1)

    def task_of(expert):
        return lane_sum(
            when_equal(table[0:1], expert, table_lane) + when_equal(table[1:2], expert, table_lane)
        )

    line = iota((z.half_rows, 1), 0)
    line_block = whole_part(line, send)
    line_rank = line - line_block * send
    line_place = here_f + line_block
    line_place = jnp.where(line_place >= group, line_place - group, line_place)
    line_task = task_of(base_f + line_place)

    def fill_pick(half):
        rank_here = line_rank - (half * z.bound if z.merged else 0)
        info = r.infos[half * group]
        for m in range(micro):
            hit = (info[INFO_TASK + m : INFO_TASK + m + 1] == line_task) & (
                info[INFO_RANK + m : INFO_RANK + m + 1] == rank_here
            )
            r.pick[half, m] = jnp.where(hit, 1.0, 0.0).astype(BF16)

    fill_pick(0)

    def greet_back():
        pl.semaphore_wait(barrier, z.experts)

        def tell(step, _):
            pltpu.make_async_remote_copy(
                src_ref=r.infos.at[0],
                dst_ref=r.infos.at[step],
                send_sem=r.info_send,
                recv_sem=r.info_recv,
                device_id={"expert": lax.rem(me + step, z.experts)},
                device_id_type=MESH,
            ).start()
            return 0

        lax.fori_loop(1, z.experts, tell, 0)
        others_told = pl.ds(1, z.experts - 1)
        owe(SENT, lambda: (r.infos.at[others_told], r.info_send))
        owe(0, lambda: (r.infos.at[others_told], r.info_recv))

    def spread(way, m, half, rows, back):
        packed, landed = (
            (r.reply_out, r.reply_in) if back else (r.rows_out, r.rows_in)
        )
        send_sem, recv_sem = (
            (r.reply_send, r.reply_recv) if back else (r.rows_send, r.rows_recv)
        )
        packed[way, m, half] = rows.reshape(group, send, model)
        landed[way, m, half, 0] = rows[:send]

        def push(step, _):
            if back:
                other = lax.rem(here + group - step, group)
            else:
                other = lax.rem(here + step, group)
            pltpu.make_async_remote_copy(
                src_ref=packed.at[way, m, half, step],
                dst_ref=landed.at[way, m, half, step],
                send_sem=send_sem.at[way, m, half],
                recv_sem=recv_sem.at[way, m, half],
                device_id={"expert": base + other},
                device_id_type=MESH,
            ).start()
            return 0

        lax.fori_loop(1, group, push, 0, unroll=group <= 8)
        key = (REPLY if back else ROWS) + 100 * way + 10 * m + half
        others = pl.ds(1, group - 1)
        at = (way, m, half)
        owe(SENT + key, lambda: (packed.at[(*at, others)], send_sem.at[at]))
        owe(key, lambda: (landed.at[(*at, others)], recv_sem.at[at]))

    def ship(key, source, target, sems, device_id):
        copy = pltpu.make_async_remote_copy(
            src_ref=source(),
            dst_ref=target(),
            send_sem=sems()[0],
            recv_sem=sems()[1],
            device_id=device_id,
            device_id_type=MESH,
        )
        copy.start()
        owe(SENT + key, lambda: (source(), sems()[0]))

    def swap(key, source, target, sems):
        ship(key, source, target, sems, {"expert": mirror})
        owe(key, lambda: (target(), sems()[1]))

    def dispatch(way, m, source):
        swap(
            MIRROR + 10 * way + m,
            lambda: source.at[m],
            lambda: r.mirror_rows.at[way, m],
            lambda: (r.mirror_send.at[way, m], r.mirror_recv.at[way, m]),
        )
        if not z.merged:
            spread(way, m, 0, dot(r.pick[0, m], source[m]).astype(BF16), False)

    def dispatch_mirror(way, m, source):
        settle(MIRROR + 10 * way + m)
        rows = dot(r.pick[1, m], r.mirror_rows[way, m])
        if z.merged:
            rows += dot(r.pick[0, m], source[m])
        spread(way, m, z.flights - 1, rows.astype(BF16), False)

    def arrived(way, m):
        for half in range(z.flights):
            settle(ROWS + 100 * way + 10 * m + half)
        return dot(r.compact[m], r.rows_in[way, m].reshape(z.all_rows, model))

    def combine(way, m, rows):
        reply = dot_rows(r.compact[m], rows).astype(BF16)
        for half in reversed(range(z.flights)):
            spread(way, m, half, reply[half * z.half_rows : (half + 1) * z.half_rows], True)

    def gathered(way, m, half):
        flight = 0 if z.merged else half
        if not z.merged or half == 1:
            settle(REPLY + 100 * way + 10 * m + flight)
        return dot_rows(r.pick[half, m], r.reply_in[way, m, flight].reshape(z.half_rows, model))

    def combine_mirror(way, m):
        r.sums_out[way, m] = gathered(way, m, 1).astype(BF16)
        swap(
            SUMS + 10 * way + m,
            lambda: r.sums_out.at[way, m],
            lambda: r.sums_in.at[way, m],
            lambda: (r.sums_send.at[way, m], r.sums_recv.at[way, m]),
        )

    def combine_end(way, m):
        own = gathered(way, m, 0)
        settle(SUMS + 10 * way + m)
        return own + r.sums_in[way, m].astype(F32)

    greet_back()

    @dec
    def _():
        dispatch(1, 0, r.cotangent)
        settle(0)
        fill_pick(1)
        dispatch_mirror(1, 0, r.cotangent)

    low_lane = jnp.where(iota((1, LANES), 1) < LANES // 2, 1.0, 0.0)
    high_lane = 1.0 - low_lane
    low_bf, high_bf = (low_lane.astype(BF16), high_lane.astype(BF16))
    pairs = model // LANES
    score_scale = (model // HEADS) ** (-0.5)

    def stacked(block):
        return jnp.concatenate([block * low_bf, block * high_bf], axis=0)

    def merged(block):
        return block[:tok] * low_lane + block[tok:] * high_lane

    def attend(queries, keys, values, allowed):
        scores = dot_cols(stacked(queries), keys) * score_scale
        if allowed is not None:
            scores = jnp.where(allowed > 0.5, scores, -1000000000.0)
        top = jnp.max(scores, axis=-1, keepdims=True)
        grown = jnp.exp(scores - top)
        probs = grown / lane_sum(grown)
        return probs, merged(dot(probs.astype(BF16), values))

    def attend_back(queries, keys, values, probs, grad_mixed):
        grad_stack = stacked(grad_mixed)
        grad_probs = dot_cols(grad_stack, values)
        inner = lane_sum(probs * grad_probs)
        grad_scores = (probs * (grad_probs - inner)).astype(BF16)
        grad_queries = merged(dot(grad_scores, keys)) * score_scale
        grad_keys = dot_rows(grad_scores, stacked(queries)) * score_scale
        grad_values = dot_rows(probs.astype(BF16), grad_stack)
        return grad_queries, grad_keys, grad_values

    def cols(index, start=0):
        return pl.ds(pl.multiple_of(start + index * LANES, LANES), LANES)

    def each_pair(run):
        def step(pair, _):
            run(pair)
            return 0

        lax.fori_loop(0, pairs, step, 0, unroll=UNROLL)

    gain_a, gain_c, gain_m = [r.gains[:, i * model : (i + 1) * model] for i in range(3)]

    def enter_experts(m):
        r.normed_m[m] = norm(r.after_cross[m], gain_m).astype(BF16)
        dispatch(0, m, r.normed_m)

    loads[0].wait()
    loads[1].wait()
    for m in range(micro):
        x_in = r.inputs[m].astype(F32)
        normed_a = norm(x_in, gain_a).astype(BF16)
        r.normed_a[m] = normed_a
        r.qkv[m] = dot(normed_a, r.wqkv[...]).astype(BF16)
        causal = jnp.where(iota((tok, tok), 1) <= iota((tok, tok), 0), 1.0, enc_f)
        allowed = when_equal(flipped[:, m : m + 1], seg_rows[m : m + 1]) * causal
        allowed = jnp.concatenate([allowed, allowed], axis=0)
        @each_pair
        def _(pair):
            probs, mixed = attend(
                r.qkv[m, :, cols(pair)],
                r.qkv[m, :, cols(pair, model)],
                r.qkv[m, :, cols(pair, 2 * model)],
                allowed,
            )
            r.probs_self[m, pair] = probs
            r.attn_rows[m, :, cols(pair)] = mixed.astype(BF16)
        after_self = x_in + dot(r.attn_rows[m], r.wout[...])

        @enc
        def _():
            r.after_cross[m] = after_self
            enter_experts(m)

        @dec
        def _():
            r.after_self[m] = after_self

    loads[2].wait()

    def send_memory(m):
        index = m + micro * side[0]
        ship(
            MEMORY + index,
            lambda: r.memory_out.at[m],
            lambda: r.memory.at[m],
            lambda: (r.memory_send.at[index], r.memory_recv.at[index]),
            {"section": 1 - section},
        )

    def wait_memory(m):
        index = m + micro * (1 - side[0])
        owe(MEMORY + index, lambda: (r.memory.at[m], r.memory_recv.at[index]))
        settle(MEMORY + index)

    @enc
    def _():
        settle(0)
        fill_pick(1)

    @dec
    def _():
        for m in range(micro):
            normed_c = norm(r.after_self[m], gain_c).astype(BF16)
            r.normed_c[m] = normed_c
            r.cross_q[m] = dot(normed_c, r.wcross[:, :model]).astype(BF16)
        for m in range(micro):
            wait_memory(m)

            @each_pair
            def _(pair):
                probs, mixed = attend(
                    r.cross_q[m, :, cols(pair)],
                    r.memory[m, :, cols(pair)],
                    r.memory[m, :, cols(pair, model)],
                    None,
                )
                r.probs_cross[m, pair] = probs
                r.cross_rows[m, :, cols(pair)] = mixed.astype(BF16)

            r.after_cross[m] = r.after_self[m] + dot_cols(r.cross_rows[m], r.wcross[:, model:])
            enter_experts(m)

    for m in range(micro):
        dispatch_mirror(0, m, r.normed_m)

    @dec
    def _():
        for m in range(1, micro):
            dispatch(1, m, r.cotangent)
        for m in range(1, micro):
            dispatch_mirror(1, m, r.cotangent)

    own_task = task_of(me_f)
    partner = lane_sum(when_equal(table_lane, own_task, table[0:1] + table[1:2])) - me_f
    capacity = r.capacity[0].astype(F32)
    place = iota((1, z.all_rows), 1)
    block = whole_part(place, send)
    place_rank = place - block * send
    place_half = whole_part(block, group)
    sender = here_f - (block - place_half * group)
    if z.merged:
        place_half = jnp.minimum(whole_part(place_rank, z.bound), 1.0)
        place_rank = place_rank - place_half * z.bound
    sender = base_f + jnp.where(sender < 0.0, sender + group, sender) + place_half * group
    sender = jnp.where(sender >= z.experts, sender - z.experts, sender)
    teller = me_f - iota((z.experts, 1), 0)
    teller = jnp.where(teller < 0.0, teller + z.experts, teller)
    for m in range(micro):
        told = lane_sum(jnp.where(lane == own_task, r.infos[:, INFO_COUNT + m, :], 0.0))
        count = row_sum(when_equal(teller, sender, told))
        slot = row_sum(jnp.where(teller < sender, told, 0.0)) + place_rank
        slot = jnp.where((place_rank < count) & (slot < capacity), slot, -1.0)
        r.compact[m] = when_equal(iota((slots, 1), 0), slot).astype(BF16)

    first_cross = 0
    first_out = first_cross + z.cross_blocks
    first_qkv = first_out + z.out_blocks
    first_misc = first_qkv + z.qkv_blocks

    def flat(ref, at=slice(None)):
        value = ref[:, :, at]
        return value.reshape(value.shape[0] * value.shape[1], value.shape[2])

    def store_blocks(first, left, right):
        width = 2 * LANES
        left = flat(left)
        for start in range(0, right.shape[-1], width):
            grad = dot_rows(left, flat(right, pl.ds(start, width))).astype(BF16)
            at = (first + start // LANES) * model
            r.dense[at : at + model] = grad[:, :LANES]
            r.dense[at + model : at + 2 * model] = grad[:, LANES:]

    bits = list(range(z.bits))
    lead = min(3, z.bits)
    last_stage = 2 * z.bits
    groups = []
    for group_parts in z.groups:
        made = sum(len(group) for group in groups)
        groups.append([])
        for index, (start, size) in enumerate(group_parts, made):
            turn = index % lead
            even = bits[turn:lead] + bits[:turn] + bits[lead:]
            light = bits[:2] if index % 2 == 0 else bits[:2][::-1]
            orders = (even, light + bits[2:])
            groups[-1].append(SimpleNamespace(index=index, start=start, size=size, orders=orders))

    def stride_of(part, level):
        first, second = [1 << order[level] for order in part.orders]
        return first + section * (second - first)

    def bit_of(part, level):
        return lax.rem(lax.div(me, stride_of(part, level)), 2)

    def rows_of(part, level, offset=0):
        size = part.size >> level
        at = part.start + offset * size
        for upper in range(level):
            at = at + bit_of(part, upper) * (part.size >> (upper + 1))
        return pl.ds(pl.multiple_of(at, 16), size)

    def landing(part, stage):
        return pl.ds(part.start + part.size - (part.size >> stage), part.size >> (stage + 1))

    def transfer(part, stage):
        halving = stage < z.bits
        level = stage if halving else last_stage - 1 - stage
        bit = bit_of(part, level)
        if halving:
            half = part.size >> (stage + 1)
            kept = rows_of(part, stage + 1)
            given = pl.ds(pl.multiple_of(kept.start + (1 - 2 * bit) * half, 16), half)
            source, target = (r.dense.at[given], r.partial.at[landing(part, stage)])
        else:
            source = target = r.total.at[rows_of(part, level + 1)]
        return pltpu.make_async_remote_copy(
            src_ref=source,
            dst_ref=target,
            send_sem=r.sum_send.at[part.index, stage],
            recv_sem=r.sum_recv.at[part.index, stage],
            device_id={"expert": me + (1 - 2 * bit) * stride_of(part, level)},
            device_id_type=MESH,
        )

    def step_group(group, stage):
        for part in groups[group]:
            if stage > 0:
                transfer(part, stage - 1).wait()
            if 0 < stage <= z.bits:
                rows = rows_of(part, stage)
                came = r.partial[landing(part, stage - 1)].astype(F32)
                target = r.total if stage == z.bits else r.dense
                target[rows] = (r.dense[rows].astype(F32) + came).astype(BF16)
            if stage < last_stage:
                transfer(part, stage).start()

    stages = [[0, 0], 0, 0]

    def advance_first(index):
        if stages[0][index] <= last_stage:
            if side[0] == index:
                step_group(0, stages[0][index])
            else:
                on_section(index)(lambda: step_group(0, stages[0][index]))
            stages[0][index] += 1

    def advance(group):
        if group == 0:
            advance_first(0)
            advance_first(1)
        elif stages[group] <= last_stage:
            step_group(group, stages[group])
            stages[group] += 1

    router = r.w_router[...]
    routers = router.shape[0]
    expert_lane = iota((8, routers), 1)
    sign = when_equal(expert_lane, me_f) - when_equal(expert_lane, partner)
    router_step = dot(sign.astype(BF16), router)[0:1]
    tile = 1024

    def each_tile(width, run):
        def step(index, _):
            run(pl.ds(pl.multiple_of(index * tile, tile), tile))
            return 0

        lax.fori_loop(0, width // tile, step, 0)

    def expert_forward(m):
        taken = arrived(0, m).astype(BF16)
        r.taken[m] = taken

        def up_tile(at):
            act, slope = gelu_and_slope(dot(r.taken[m], r.wup[:, at]))
            r.act[m, :, at] = act.astype(BF16)
            r.slope[m, :, at] = slope.astype(BF16)

        each_tile(z.hidden, up_tile)
        gap = lane_sum(taken.astype(F32) * router_step)
        small = jnp.exp(-jnp.abs(gap))
        large = 1.0 / (1.0 + small)
        gate = jnp.where(gap >= 0.0, large, small * large)
        r.gate[m] = gate
        r.gate_slope[m] = small * large * large

        r.expert_out[m] = dot(r.act[m], r.wdown[...]).astype(BF16)
        r.gated[m] = (gate * r.expert_out[m].astype(F32)).astype(BF16)

    def expert_backward(m):
        grad_final = arrived(1, m)
        grad_gate = lane_sum(r.expert_out[m].astype(F32) * grad_final)
        grad_gap = r.gate_slope[m] * grad_gate
        r.grad_gap[m] = grad_gap
        r.grad_out[m] = (r.gate[m] * grad_final).astype(BF16)

        def act_tile(at):
            grad_act = dot_cols(r.grad_out[m], r.wdown[at, :])
            r.grad_hidden[m, :, at] = (grad_act * r.slope[m, :, at].astype(F32)).astype(BF16)

        each_tile(z.hidden, act_tile)

        rounded = dot_cols(r.grad_hidden[m], r.wup[...]).astype(BF16).astype(F32)
        combine(1, m, (rounded + grad_gap * router_step).astype(BF16))

    loads[3].wait()
    loads[4].wait()

    @dec
    def _():
        for m in range(micro):
            expert_forward(m)
            expert_backward(m)
        combine_mirror(1, 0)
        for m in range(micro):
            combine(0, m, r.gated[m])
            r.grad_state[m] = r.cotangent[m].astype(F32)

    @enc
    def _():
        for m in range(micro):
            expert_forward(m)
            combine(0, m, r.gated[m])
        for m in range(micro):
            combine_mirror(0, m)
        for m in range(micro):
            layer_final = r.after_cross[m] + combine_end(0, m)
            r.layer_final[m] = layer_final
            r.layer_out[m] = layer_final.astype(BF16)
            normed_k = norm(layer_final, gain_c).astype(BF16)
            r.normed_c[m] = normed_k
            r.memory_out[m] = dot(normed_k, r.wcross[...]).astype(BF16)
            send_memory(m)
        gain_grad = jnp.zeros((1, model), F32)
        for m in range(micro):
            wait_memory(m)
            grad_normed = dot_cols(r.memory[m], r.wcross[...])
            grad_state, grad_gain = norm_back(r.layer_final[m], gain_c, grad_normed)
            gain_grad += grad_gain
            grad_final = r.cotangent[m].astype(F32) + grad_state
            r.grad_state[m] = grad_final
            r.grad_rows[m] = grad_final.astype(BF16)
            dispatch(1, m, r.grad_rows)
        for m in range(micro):
            dispatch_mirror(1, m, r.grad_rows)
        r.gain_grads[1:2] = gain_grad
        store_blocks(first_cross, r.normed_c, r.memory)
        expert_backward(0)
        for m in range(1, micro):
            expert_backward(m)
        advance_first(0)
        combine_mirror(1, 0)

    saves = []

    def save(source, target):
        copy = pltpu.make_async_copy(source, target, r.save_sem.at[len(saves)])
        copy.start()
        saves.append(copy)

    def up_grad(at):
        r.wup[:, at] = dot_rows(flat(r.taken), flat(r.grad_hidden, at)).astype(BF16)

    def down_grad(at):
        r.wdown[at, :] = dot_rows(flat(r.act, at), flat(r.grad_out)).astype(BF16)

    each_tile(z.hidden, up_grad)
    save(r.wup, r.up_grad)
    for m in range(1, micro):
        combine_mirror(1, m)
    each_tile(z.hidden, down_grad)
    save(r.wdown, r.down_grad)

    def self_back(m):
        grad_top = r.grad_state[m]
        grad_y = grad_top.astype(BF16)
        r.grad_self[m] = grad_y
        r.grad_mix[...] = dot_cols(grad_y, r.wout[...]).astype(BF16)

        @each_pair
        def _(pair):
            grads = attend_back(
                r.qkv[m, :, cols(pair)],
                r.qkv[m, :, cols(pair, model)],
                r.qkv[m, :, cols(pair, 2 * model)],
                r.probs_self[m, pair],
                r.grad_mix[:, cols(pair)],
            )
            for third, grad in enumerate(grads):
                r.grad_qkv[m, :, cols(pair, third * model)] = grad.astype(BF16)
        grad_normed = dot_cols(r.grad_qkv[m], r.wqkv[...])
        grad_state, grad_gain = norm_back(r.inputs[m].astype(F32), gain_a, grad_normed)
        r.inputs_grad[m] = grad_top + grad_state
        r.gain_grads[3 + m : 4 + m] = grad_gain

    gain_grad = jnp.zeros((1, model), F32)
    for m in range(micro):
        grad_state, grad_gain = norm_back(r.after_cross[m], gain_m, combine_end(1, m))
        gain_grad += grad_gain
        r.grad_state[m] += grad_state

        @enc
        def _():
            self_back(m)

        @dec
        def _():
            grad_y = r.grad_state[m].astype(BF16)
            r.grad_cross[m] = grad_y
            r.grad_mix[...] = dot(grad_y, r.wcross[:, model:]).astype(BF16)

            @each_pair
            def _(pair):
                at = cols(pair)
                grad_q, grad_k, grad_v = attend_back(
                    r.cross_q[m, :, at],
                    r.memory[m, :, at],
                    r.memory[m, :, cols(pair, model)],
                    r.probs_cross[m, pair],
                    r.grad_mix[:, at],
                )
                r.grad_cross_q[m, :, at] = grad_q.astype(BF16)
                r.memory_out[m, :, at] = grad_k.astype(BF16)
                r.memory_out[m, :, cols(pair, model)] = grad_v.astype(BF16)
            send_memory(m)

    r.gain_grads[2:3] = gain_grad

    @dec
    def _():
        gain_grad = jnp.zeros((1, model), F32)
        for m in range(micro):
            grad_normed = dot_cols(r.grad_cross_q[m], r.wcross[:, :model])
            grad_state, grad_gain = norm_back(r.after_self[m], gain_c, grad_normed)
            gain_grad += grad_gain
            r.grad_state[m] += grad_state
        r.gain_grads[1:2] = gain_grad
        store_blocks(first_cross, r.normed_c, r.grad_cross_q)
        store_blocks(first_cross + z.out_blocks, r.grad_cross, r.cross_rows)
        advance_first(1)
        for m in range(micro):
            self_back(m)

    advance_first(0)
    store_blocks(first_out, r.attn_rows, r.grad_self)
    advance(1)

    r.gain_grads[0:1] = row_sum(r.gain_grads[3 : 3 + micro])
    r.gain_grads[3:8] = jnp.zeros((5, model), F32)

    store_blocks(first_qkv, r.normed_a, r.grad_qkv)
    misc_row = iota((1, z.misc), 1)
    misc_sign = when_equal(misc_row, me_f) - when_equal(misc_row, partner)
    misc = jnp.zeros((z.misc, model), F32)
    for m in range(micro):
        steps = r.grad_gap[m] * misc_sign
        top = steps.astype(BF16)
        rest = (steps - top.astype(F32)).astype(BF16)
        misc += dot_rows(top, r.taken[m]) + dot_rows(rest, r.taken[m])
    place_gain = when_equal(iota((8, z.misc), 1), iota((8, z.misc), 0) + routers)
    misc += dot_rows(place_gain.astype(BF16), r.gain_grads[...].astype(BF16))
    misc_rows = [
        pl.ds(first_misc * model + index * z.misc, z.misc) for index in range(model // LANES)
    ]
    for index, rows in enumerate(misc_rows):
        r.dense[rows] = misc[:, index * LANES : (index + 1) * LANES].astype(BF16)
    used = z.blocks * model
    if used < z.dense_rows:
        r.dense[used:] = jnp.zeros((z.dense_rows - used, LANES), BF16)
    advance(2)
    advance(0)
    advance(1)

    @dec
    def _():
        for m in range(micro):
            combine_mirror(0, m)
        for m in range(micro):
            r.layer_out[m] = (r.after_cross[m] + combine_end(0, m)).astype(BF16)

    def save_blocks(target, first, count):
        for index in range(count):
            rows = pl.ds((first + index) * model, model)
            save(r.total.at[rows], target.at[:, pl.ds(index * LANES, LANES)])

    while stages[2] <= last_stage:
        if stages[0][1] <= last_stage:
            advance(0)
            if stages[0][1] > last_stage:
                save_blocks(r.cross_grad, first_cross, z.cross_blocks)
        if stages[1] <= last_stage:
            advance(1)
            if stages[1] > last_stage:
                save_blocks(r.out_grad, first_out, z.out_blocks)
        advance(2)
    save_blocks(r.qkv_grad, first_qkv, z.qkv_blocks)

    for index, rows in enumerate(misc_rows):
        sums = r.total[rows].astype(F32)
        r.router_grad[:, index * LANES : (index + 1) * LANES] = sums[:routers]
        for row in range(3):
            at = row * model + index * LANES
            r.gains_grad[:, at : at + LANES] = sums[routers + row : routers + row + 1]
    for copy in saves:
        copy.wait()

    settle_all()


def vmem_bytes(buffers):
    total = 0
    for buffer in buffers:
        if buffer.memory_space == pltpu.VMEM:
            *lead, rows, lanes = buffer.shape
            size = math.prod(lead) * round_up(rows, 8) * round_up(lanes, LANES)
            total += size * jnp.dtype(buffer.dtype).itemsize
    return min(total + 5 * 1024 * 1024, 62 * 1024 * 1024)


def run_kernel(z, arrays):
    micro, tok, model, hidden = (z.micro, z.tok, z.model, z.hidden)
    vmem = pl.BlockSpec(memory_space=pltpu.VMEM)
    hbm = pl.BlockSpec(memory_space=pl.ANY)
    inputs = dict(
        segments=(arrays.segments, vmem),
        tasks=(arrays.tasks, vmem),
        table=(arrays.table, vmem),
        capacity=(arrays.capacity, pl.BlockSpec(memory_space=pltpu.SMEM)),
        inputs=(arrays.inputs, vmem),
        cotangent=(arrays.cotangent, vmem),
        gains=(arrays.gains, vmem),
        w_router=(arrays.w_router, vmem),
        w_qkv=(arrays.w_qkv, hbm),
        w_out=(arrays.w_out, hbm),
        w_cross=(arrays.w_cross, hbm),
        w_up=(arrays.w_up, hbm),
        w_down=(arrays.w_down, hbm),
    )
    rows = (micro, tok, model)
    slot_rows = (micro, z.slots, model)
    slot_hidden = (micro, z.slots, hidden)
    outputs = dict(
        layer_out=(rows, BF16, vmem),
        inputs_grad=(rows, F32, vmem),
        gains_grad=((1, 3 * model), F32, vmem),
        router_grad=(arrays.w_router.shape, F32, vmem),
        qkv_grad=(arrays.w_qkv.shape, BF16, hbm),
        out_grad=(arrays.w_out.shape, BF16, hbm),
        cross_grad=(arrays.w_cross.shape, BF16, hbm),
        up_grad=(arrays.w_up.shape, BF16, hbm),
        down_grad=(arrays.w_down.shape, BF16, hbm),
    )
    blocks = (2, micro, z.flights, z.group, z.send, model)
    pairs = model // LANES
    dma = pltpu.SemaphoreType.DMA
    scratch = dict(
        wqkv=pltpu.VMEM(arrays.w_qkv.shape, BF16),
        wout=pltpu.VMEM(arrays.w_out.shape, BF16),
        wcross=pltpu.VMEM(arrays.w_cross.shape, BF16),
        wup=pltpu.VMEM(arrays.w_up.shape, BF16),
        wdown=pltpu.VMEM(arrays.w_down.shape, BF16),
        infos=pltpu.VMEM((z.experts, 8, LANES), F32),
        normed_a=pltpu.VMEM(rows, BF16),
        qkv=pltpu.VMEM((micro, tok, 3 * model), BF16),
        probs_self=pltpu.VMEM((micro, pairs, 2 * tok, tok), F32),
        attn_rows=pltpu.VMEM(rows, BF16),
        after_self=pltpu.VMEM(rows, F32),
        normed_c=pltpu.VMEM(rows, BF16),
        cross_q=pltpu.VMEM(rows, BF16),
        probs_cross=pltpu.VMEM((micro, pairs, 2 * tok, tok), F32),
        cross_rows=pltpu.VMEM(rows, BF16),
        memory_out=pltpu.VMEM((micro, tok, 2 * model), BF16),
        memory=pltpu.VMEM((micro, tok, 2 * model), BF16),
        after_cross=pltpu.VMEM(rows, F32),
        normed_m=pltpu.VMEM(rows, BF16),
        layer_final=pltpu.VMEM(rows, F32),
        grad_state=pltpu.VMEM(rows, F32),
        grad_rows=pltpu.VMEM(rows, BF16),
        grad_cross=pltpu.VMEM(rows, BF16),
        grad_cross_q=pltpu.VMEM(rows, BF16),
        grad_self=pltpu.VMEM(rows, BF16),
        grad_mix=pltpu.VMEM((tok, model), BF16),
        grad_qkv=pltpu.VMEM((micro, tok, 3 * model), BF16),
        gain_grads=pltpu.VMEM((8, model), F32),
        pick=pltpu.VMEM((z.halves, micro, z.half_rows, tok), BF16),
        compact=pltpu.VMEM((micro, z.slots, z.all_rows), BF16),
        rows_out=pltpu.VMEM(blocks, BF16),
        rows_in=pltpu.VMEM(blocks, BF16),
        reply_out=pltpu.VMEM(blocks, BF16),
        reply_in=pltpu.VMEM(blocks, BF16),
        mirror_rows=pltpu.VMEM((2,) + rows, BF16),
        sums_out=pltpu.VMEM((2,) + rows, BF16),
        sums_in=pltpu.VMEM((2,) + rows, BF16),
        taken=pltpu.VMEM(slot_rows, BF16),
        slope=pltpu.VMEM(slot_hidden, BF16),
        act=pltpu.VMEM(slot_hidden, BF16),
        expert_out=pltpu.VMEM(slot_rows, BF16),
        gated=pltpu.VMEM(slot_rows, BF16),
        gate=pltpu.VMEM((micro, z.slots, 1), F32),
        gate_slope=pltpu.VMEM((micro, z.slots, 1), F32),
        grad_gap=pltpu.VMEM((micro, z.slots, 1), F32),
        grad_out=pltpu.VMEM(slot_rows, BF16),
        grad_hidden=pltpu.VMEM(slot_hidden, BF16),
        dense=pltpu.VMEM((z.dense_rows, LANES), BF16),
        total=pltpu.VMEM((z.dense_rows, LANES), BF16),
        partial=pltpu.VMEM((z.dense_rows, LANES), BF16),
        load_sem=dma((5,)),
        save_sem=dma((2 + z.blocks - z.misc_blocks,)),
        info_send=dma(()),
        info_recv=dma(()),
        rows_send=dma((2, micro, z.flights)),
        rows_recv=dma((2, micro, z.flights)),
        reply_send=dma((2, micro, z.flights)),
        reply_recv=dma((2, micro, z.flights)),
        mirror_send=dma((2, micro)),
        mirror_recv=dma((2, micro)),
        sums_send=dma((2, micro)),
        sums_recv=dma((2, micro)),
        memory_send=dma((2 * micro,)),
        memory_recv=dma((2 * micro,)),
        sum_send=dma((z.parts, 2 * z.bits)),
        sum_recv=dma((z.parts, 2 * z.bits)),
    )
    names = [*inputs, *outputs, *scratch]

    def body(*refs):
        kernel_body(z, names, *refs)

    return pl.pallas_call(
        body,
        name="layer_step",
        out_shape=[jax.ShapeDtypeStruct(shape, dtype) for shape, dtype, _ in outputs.values()],
        in_specs=[spec for _, spec in inputs.values()],
        out_specs=[spec for _, _, spec in outputs.values()],
        scratch_shapes=list(scratch.values()),
        compiler_params=pltpu.CompilerParams(
            collective_id=0, has_side_effects=True, vmem_limit_bytes=vmem_bytes(scratch.values())
        ),
    )(*[value for value, _ in inputs.values()])


def widen_body(count, *refs):
    total = (len(refs) - 2) // 4
    sources, targets, came, made = [refs[i * total : (i + 1) * total] for i in range(4)]
    come_sem, go_sem = refs[4 * total :]
    loads = [pltpu.make_async_copy(sources[i], came[i], come_sem.at[i]) for i in range(total)]
    for copy in loads:
        copy.start()
    for i in range(total):
        loads[i].wait()
        if i >= count:
            pltpu.make_async_copy(came[i], targets[i], go_sem.at[i]).start()
            continue
        rows, lanes = came[i].shape
        step_rows = 1 << (min(rows, 128 * 1024 // lanes).bit_length() - 1)

        def step(index, _):
            at = pl.ds(pl.multiple_of(index * step_rows, step_rows), step_rows)
            made[i][at] = came[i][at].astype(F32)
            pltpu.make_async_copy(made[i].at[at], targets[i].at[at], go_sem.at[i]).start()
            return 0

        lax.fori_loop(0, rows // step_rows, step, 0)
    for i in range(total):
        left = made[i] if i < count else came[i]
        pltpu.make_async_copy(left, targets[i], go_sem.at[i]).wait()


def widen(narrow, passed):
    values = [*narrow, *passed]
    count = len(narrow)
    types = [F32] * count + [value.dtype for value in passed]
    hbm = pl.BlockSpec(memory_space=pltpu.HBM)
    dma = pltpu.SemaphoreType.DMA((len(values),))
    blank = pltpu.VMEM((8, LANES), F32)
    return pl.pallas_call(
        lambda *refs: widen_body(count, *refs),
        name="widen",
        out_shape=[jax.ShapeDtypeStruct(v.shape, t) for v, t in zip(values, types)],
        in_specs=[hbm] * len(values),
        out_specs=[hbm] * len(values),
        scratch_shapes=[pltpu.VMEM(value.shape, value.dtype) for value in values]
        + [pltpu.VMEM(value.shape, F32) for value in narrow]
        + [blank] * len(passed)
        + [dma, dma],
        compiler_params=pltpu.CompilerParams(vmem_limit_bytes=62 * 1024 * 1024),
    )(*values)


def shards(
    inputs,
    cotangent,
    segments,
    tasks,
    table,
    capacity,
    gains,
    w_qkv,
    w_out,
    w_cross,
    w_router,
    w_up,
    w_down,
):
    experts = lax.axis_size("expert")
    z = Sizes(inputs, w_qkv, w_cross, w_router, w_up, table, experts)
    model = z.model
    arrays = SimpleNamespace(
        segments=segments[0],
        tasks=tasks[0, :, :, 0],
        table=table[0].T,
        capacity=capacity,
        inputs=inputs[0],
        cotangent=cotangent[0],
        gains=gains.reshape(1, 3 * model),
        w_router=w_router[0].T,
        w_qkv=w_qkv[0],
        w_out=w_out[0],
        w_cross=w_cross[0],
        w_up=w_up[0, 0],
        w_down=w_down[0, 0],
    )
    *passed, qkv_grad, out_grad, cross_grad, up_grad, down_grad = run_kernel(z, arrays)
    narrow = (up_grad, down_grad, qkv_grad, cross_grad, out_grad)
    up_grad, down_grad, qkv_grad, cross_grad, out_grad, *passed = widen(narrow, passed)
    out, inputs_grad, gains_grad, router_grad = passed
    return (
        out[None],
        inputs_grad[None],
        gains_grad.reshape(1, 3, model),
        qkv_grad[None],
        out_grad[None],
        cross_grad[None],
        router_grad.T[None],
        up_grad[None, None],
        down_grad[None, None],
    )


def solution(mesh):
    in_specs = (
        P("section", None, "expert", None),
        P("section", None, "expert", None),
        P("section", None, "expert"),
        P("section", None, "expert", None),
        P("section", None, None),
        P("section"),
        P("section", None, None),
        P("section", None, None),
        P("section", None, None),
        P("section", None, None),
        P("section", None, None),
        P("section", "expert", None, None),
        P("section", "expert", None, None),
    )
    out_specs = (
        P("section", None, "expert", None),
        P("section", None, "expert", None),
        P("section", None, None),
        P("section", None, None),
        P("section", None, None),
        P("section", None, None),
        P("section", None, None),
        P("section", "expert", None, None),
        P("section", "expert", None, None),
    )
    return jax.shard_map(shards, mesh=mesh, in_specs=in_specs, out_specs=out_specs, check_vma=False)
```

```python
import math
from types import SimpleNamespace

import jax
import jax.numpy as jnp
from jax import lax
from jax.experimental import pallas as pl
from jax.experimental.pallas import tpu as pltpu
from jax.sharding import PartitionSpec as P

HEADS = 8
EPSILON = 1e-06
LANES = 128
UNROLL = 4
MESH = pl.DeviceIdType.MESH
F32 = jnp.float32
BF16 = jnp.bfloat16

INFO_TASK, INFO_RANK, INFO_COUNT = (0, 2, 4)
ROWS, REPLY, MIRROR, SUMS, MEMORY, SENT = (1000, 2000, 3000, 4000, 5000, 10000)


def round_up(value, unit):
    return -(-value // unit) * unit


def dot(left, right):
    return jnp.dot(left, right, preferred_element_type=F32)


def dot_rows(left, right):
    return lax.dot_general(left, right, (((0,), (0,)), ((), ())), preferred_element_type=F32)


def dot_cols(left, right):
    return lax.dot_general(left, right, (((1,), (1,)), ((), ())), preferred_element_type=F32)


def lane_sum(value):
    return jnp.sum(value, axis=-1, keepdims=True)


def row_sum(value):
    return jnp.sum(value, axis=0, keepdims=True)


def when_equal(left, right, value=1.0):
    return jnp.where(left == right, value, 0.0)


def iota(shape, axis):
    return lax.broadcasted_iota(jnp.int32, shape, axis).astype(F32)


def whole_part(value, unit):
    return jnp.floor((value + 0.5) * (1.0 / unit))


def inverse_rms(value):
    return lax.rsqrt(jnp.mean(value * value, axis=-1, keepdims=True) + EPSILON)


def norm(value, gain):
    return value * inverse_rms(value) * gain


def norm_back(value, gain, grad):
    scale = inverse_rms(value)
    unit = value * scale
    scaled = grad * gain
    grad_value = scale * (scaled - unit * jnp.mean(scaled * unit, axis=-1, keepdims=True))
    return grad_value, row_sum(grad * unit)


def gelu_and_slope(hidden):
    rate = math.sqrt(2.0 / math.pi)
    square = hidden * hidden
    bend = jnp.tanh(hidden * (rate + rate * 0.044715 * square))
    share = 0.5 + 0.5 * bend
    act = hidden * share
    slope = share + act * (1.0 - bend) * (rate + 3.0 * rate * 0.044715 * square)
    return act, slope


class Sizes:
    def __init__(self, inputs, w_qkv, w_cross, w_router, w_up, table, experts):
        _, self.micro, self.tok, self.model = inputs.shape
        self.hidden = w_up.shape[-1]
        self.experts = experts
        self.tasks = table.shape[1]
        self.slots = 2 * self.tok
        self.halves = 2
        self.group = experts // self.halves
        self.bound = max(2, 6 * self.tok // experts)
        self.send = round_up(self.bound, 16)
        self.merged = self.halves * self.bound <= self.send
        self.flights = 1 if self.merged else self.halves
        self.half_rows = self.group * self.send
        self.all_rows = self.flights * self.half_rows
        self.misc = round_up(w_router.shape[-1] + 3, LANES)
        self.qkv_blocks = w_qkv.shape[-1] // LANES
        self.out_blocks = self.model // LANES
        self.cross_blocks = w_cross.shape[-1] // LANES
        self.misc_blocks = self.misc // LANES
        self.blocks = self.qkv_blocks + self.out_blocks + self.cross_blocks + self.misc_blocks
        self.bits = experts.bit_length() - 1
        unit = 16 * experts
        self.groups = []
        start = 0
        for blocks, count in (
            (self.cross_blocks, 3),
            (self.out_blocks, 2),
            (self.qkv_blocks + self.misc_blocks, 6),
        ):
            units = -(-blocks * self.model // unit)
            count = min(count, units)
            group = []
            for part in range(count):
                size = (units // count + (part < units % count)) * unit
                group.append((start, size))
                start += size
            self.groups.append(group)
        self.parts = sum(len(group) for group in self.groups)
        self.dense_rows = start


def kernel_body(z, names, *refs):
    r = SimpleNamespace(**dict(zip(names, refs)))
    me = lax.axis_index("expert")
    section = lax.axis_index("section")
    tok, model, micro, group, send, slots = (z.tok, z.model, z.micro, z.group, z.send, z.slots)
    here = lax.rem(me, group)
    base = me - here
    mirror = lax.rem(me + group, z.experts)
    me_f = me.astype(F32)
    here_f = here.astype(F32)
    base_f = base.astype(F32)
    enc_f = 1.0 - section.astype(F32)

    side = [None]
    owed = {}

    def on_section(index):
        def put(run):
            side[0] = index
            pl.when(section == index)(run)
            side[0] = None

        return put

    enc, dec = (on_section(0), on_section(1))

    def wait_for(ref, sem):
        pltpu.make_async_copy(ref, ref, sem).wait()

    def owe(key, copy):
        owed[side[0], key] = copy

    def settle(key):
        found = [e for e in owed if e[1] == key and (side[0] in (None, e[0]) or e[0] is None)]
        copies = [owed.pop(entry) for entry in found]
        if side[0] is not None and found[0][0] is None:
            owed[1 - side[0], key] = copies[0]
        wait_for(*copies[0]())

    def settle_all():
        for index in (None, 0, 1):
            waits = [owed.pop(entry) for entry in list(owed) if entry[0] == index]

            def run():
                for copy in waits:
                    wait_for(*copy())

            if index is None:
                run()
            else:
                pl.when(section == index)(run)

    loads = [
        pltpu.make_async_copy(source, target, r.load_sem.at[i])
        for i, (source, target) in enumerate(
            (
                (r.w_qkv, r.wqkv),
                (r.w_out, r.wout),
                (r.w_cross, r.wcross),
                (r.w_up, r.wup),
                (r.w_down, r.wdown),
            )
        )
    ]
    for load in loads:
        load.start()

    barrier = pltpu.get_barrier_semaphore()

    def greet(step, _):
        pl.semaphore_signal(
            barrier,
            inc=1,
            device_id={"expert": lax.rem(me + step, z.experts)},
            device_id_type=MESH,
        )
        return 0

    lax.fori_loop(1, z.experts, greet, 0)
    pl.semaphore_signal(
        barrier, inc=1, device_id={"section": 1 - section}, device_id_type=MESH
    )

    seg_rows = r.segments[...].astype(F32)
    task_rows = r.tasks[...].astype(F32)
    blank = jnp.zeros((LANES - 2 * micro, LANES), F32)
    flipped = jnp.transpose(jnp.concatenate([seg_rows, task_rows, blank], axis=0))
    lane = iota((1, LANES), 1)
    earlier = jnp.where(iota((tok, tok), 0) < iota((tok, tok), 1), 1.0, 0.0)
    ranks, counts = ([], [])
    for m in range(micro):
        task_col = flipped[:, micro + m : micro + m + 1]
        ranks.append(row_sum(when_equal(task_col, task_rows[m : m + 1]) * earlier))
        counts.append(row_sum(when_equal(task_col, lane)))
    r.infos[0] = jnp.concatenate(
        [task_rows, *ranks, *counts, jnp.zeros((8 - 3 * micro, LANES), F32)], axis=0
    )

    table = r.table[...].astype(F32)
    table_lane = iota((1, z.tasks), 1)

    def task_of(expert):
        return lane_sum(
            when_equal(table[0:1], expert, table_lane) + when_equal(table[1:2], expert, table_lane)
        )

    line = iota((z.half_rows, 1), 0)
    line_block = whole_part(line, send)
    line_rank = line - line_block * send
    line_place = here_f + line_block
    line_place = jnp.where(line_place >= group, line_place - group, line_place)
    line_task = task_of(base_f + line_place)

    def fill_pick(half):
        rank_here = line_rank - (half * z.bound if z.merged else 0)
        info = r.infos[half * group]
        for m in range(micro):
            hit = (info[INFO_TASK + m : INFO_TASK + m + 1] == line_task) & (
                info[INFO_RANK + m : INFO_RANK + m + 1] == rank_here
            )
            r.pick[half, m] = jnp.where(hit, 1.0, 0.0).astype(BF16)

    fill_pick(0)

    def greet_back():
        pl.semaphore_wait(barrier, z.experts)

        def tell(step, _):
            pltpu.make_async_remote_copy(
                src_ref=r.infos.at[0],
                dst_ref=r.infos.at[step],
                send_sem=r.info_send,
                recv_sem=r.info_recv,
                device_id={"expert": lax.rem(me + step, z.experts)},
                device_id_type=MESH,
            ).start()
            return 0

        lax.fori_loop(1, z.experts, tell, 0)
        others_told = pl.ds(1, z.experts - 1)
        owe(SENT, lambda: (r.infos.at[others_told], r.info_send))
        owe(0, lambda: (r.infos.at[others_told], r.info_recv))

    def spread(way, m, half, rows, back):
        packed, landed = (
            (r.reply_out, r.reply_in) if back else (r.rows_out, r.rows_in)
        )
        send_sem, recv_sem = (
            (r.reply_send, r.reply_recv) if back else (r.rows_send, r.rows_recv)
        )
        packed[way, m, half] = rows.reshape(group, send, model)
        landed[way, m, half, 0] = rows[:send]

        def push(step, _):
            if back:
                other = lax.rem(here + group - step, group)
            else:
                other = lax.rem(here + step, group)
            pltpu.make_async_remote_copy(
                src_ref=packed.at[way, m, half, step],
                dst_ref=landed.at[way, m, half, step],
                send_sem=send_sem.at[way, m, half],
                recv_sem=recv_sem.at[way, m, half],
                device_id={"expert": base + other},
                device_id_type=MESH,
            ).start()
            return 0

        lax.fori_loop(1, group, push, 0, unroll=group <= 8)
        key = (REPLY if back else ROWS) + 100 * way + 10 * m + half
        others = pl.ds(1, group - 1)
        at = (way, m, half)
        owe(SENT + key, lambda: (packed.at[(*at, others)], send_sem.at[at]))
        owe(key, lambda: (landed.at[(*at, others)], recv_sem.at[at]))

    def ship(key, source, target, sems, device_id):
        copy = pltpu.make_async_remote_copy(
            src_ref=source(),
            dst_ref=target(),
            send_sem=sems()[0],
            recv_sem=sems()[1],
            device_id=device_id,
            device_id_type=MESH,
        )
        copy.start()
        owe(SENT + key, lambda: (source(), sems()[0]))

    def swap(key, source, target, sems):
        ship(key, source, target, sems, {"expert": mirror})
        owe(key, lambda: (target(), sems()[1]))

    def dispatch(way, m, source):
        swap(
            MIRROR + 10 * way + m,
            lambda: source.at[m],
            lambda: r.mirror_rows.at[way, m],
            lambda: (r.mirror_send.at[way, m], r.mirror_recv.at[way, m]),
        )
        if not z.merged:
            spread(way, m, 0, dot(r.pick[0, m], source[m]).astype(BF16), False)

    def dispatch_mirror(way, m, source):
        settle(MIRROR + 10 * way + m)
        rows = dot(r.pick[1, m], r.mirror_rows[way, m])
        if z.merged:
            rows += dot(r.pick[0, m], source[m])
        spread(way, m, z.flights - 1, rows.astype(BF16), False)

    def arrived(way, m):
        for half in range(z.flights):
            settle(ROWS + 100 * way + 10 * m + half)
        return dot(r.compact[m], r.rows_in[way, m].reshape(z.all_rows, model))

    def combine(way, m, rows):
        reply = dot_rows(r.compact[m], rows).astype(BF16)
        for half in reversed(range(z.flights)):
            spread(way, m, half, reply[half * z.half_rows : (half + 1) * z.half_rows], True)

    def gathered(way, m, half):
        flight = 0 if z.merged else half
        if not z.merged or half == 1:
            settle(REPLY + 100 * way + 10 * m + flight)
        return dot_rows(r.pick[half, m], r.reply_in[way, m, flight].reshape(z.half_rows, model))

    def combine_mirror(way, m):
        r.sums_out[way, m] = gathered(way, m, 1).astype(BF16)
        swap(
            SUMS + 10 * way + m,
            lambda: r.sums_out.at[way, m],
            lambda: r.sums_in.at[way, m],
            lambda: (r.sums_send.at[way, m], r.sums_recv.at[way, m]),
        )

    def combine_end(way, m):
        own = gathered(way, m, 0)
        settle(SUMS + 10 * way + m)
        return own + r.sums_in[way, m].astype(F32)

    greet_back()

    @dec
    def _():
        dispatch(1, 0, r.cotangent)
        settle(0)
        fill_pick(1)
        dispatch_mirror(1, 0, r.cotangent)

    low_lane = jnp.where(iota((1, LANES), 1) < LANES // 2, 1.0, 0.0)
    high_lane = 1.0 - low_lane
    low_bf, high_bf = (low_lane.astype(BF16), high_lane.astype(BF16))
    pairs = model // LANES
    score_scale = (model // HEADS) ** (-0.5)

    def stacked(block):
        return jnp.concatenate([block * low_bf, block * high_bf], axis=0)

    def merged(block):
        return block[:tok] * low_lane + block[tok:] * high_lane

    def attend(queries, keys, values, allowed):
        scores = dot_cols(stacked(queries), keys) * score_scale
        if allowed is not None:
            scores = jnp.where(allowed > 0.5, scores, -1000000000.0)
        top = jnp.max(scores, axis=-1, keepdims=True)
        grown = jnp.exp(scores - top)
        probs = grown / lane_sum(grown)
        return probs, merged(dot(probs.astype(BF16), values))

    def attend_back(queries, keys, values, probs, grad_mixed):
        grad_stack = stacked(grad_mixed)
        grad_probs = dot_cols(grad_stack, values)
        inner = lane_sum(probs * grad_probs)
        grad_scores = (probs * (grad_probs - inner)).astype(BF16)
        grad_queries = merged(dot(grad_scores, keys)) * score_scale
        grad_keys = dot_rows(grad_scores, stacked(queries)) * score_scale
        grad_values = dot_rows(probs.astype(BF16), grad_stack)
        return grad_queries, grad_keys, grad_values

    def cols(index, start=0):
        return pl.ds(pl.multiple_of(start + index * LANES, LANES), LANES)

    def each_pair(run):
        def step(pair, _):
            run(pair)
            return 0

        lax.fori_loop(0, pairs, step, 0, unroll=UNROLL)

    gain_a, gain_c, gain_m = [r.gains[:, i * model : (i + 1) * model] for i in range(3)]

    def enter_experts(m):
        r.normed_m[m] = norm(r.after_cross[m], gain_m).astype(BF16)
        dispatch(0, m, r.normed_m)

    loads[0].wait()
    loads[1].wait()
    for m in range(micro):
        x_in = r.inputs[m].astype(F32)
        normed_a = norm(x_in, gain_a).astype(BF16)
        r.normed_a[m] = normed_a
        r.qkv[m] = dot(normed_a, r.wqkv[...]).astype(BF16)
        causal = jnp.where(iota((tok, tok), 1) <= iota((tok, tok), 0), 1.0, enc_f)
        allowed = when_equal(flipped[:, m : m + 1], seg_rows[m : m + 1]) * causal
        allowed = jnp.concatenate([allowed, allowed], axis=0)
        @each_pair
        def _(pair):
            probs, mixed = attend(
                r.qkv[m, :, cols(pair)],
                r.qkv[m, :, cols(pair, model)],
                r.qkv[m, :, cols(pair, 2 * model)],
                allowed,
            )
            r.probs_self[m, pair] = probs
            r.attn_rows[m, :, cols(pair)] = mixed.astype(BF16)
        after_self = x_in + dot(r.attn_rows[m], r.wout[...])

        @enc
        def _():
            r.after_cross[m] = after_self
            enter_experts(m)

        @dec
        def _():
            r.after_self[m] = after_self

    loads[2].wait()

    def send_memory(m):
        index = m + micro * side[0]
        ship(
            MEMORY + index,
            lambda: r.memory_out.at[m],
            lambda: r.memory.at[m],
            lambda: (r.memory_send.at[index], r.memory_recv.at[index]),
            {"section": 1 - section},
        )

    def wait_memory(m):
        index = m + micro * (1 - side[0])
        owe(MEMORY + index, lambda: (r.memory.at[m], r.memory_recv.at[index]))
        settle(MEMORY + index)

    @enc
    def _():
        settle(0)
        fill_pick(1)

    @dec
    def _():
        for m in range(micro):
            after_self = r.after_self[m]
            normed_c = norm(after_self, gain_c).astype(BF16)
            r.normed_c[m] = normed_c
            r.cross_q[m] = dot(normed_c, r.wcross[:, :model]).astype(BF16)
            wait_memory(m)

            @each_pair
            def _(pair):
                probs, mixed = attend(
                    r.cross_q[m, :, cols(pair)],
                    r.memory[m, :, cols(pair)],
                    r.memory[m, :, cols(pair, model)],
                    None,
                )
                r.probs_cross[m, pair] = probs
                r.cross_rows[m, :, cols(pair)] = mixed.astype(BF16)

            r.after_cross[m] = after_self + dot_cols(r.cross_rows[m], r.wcross[:, model:])
            enter_experts(m)

    for m in range(micro):
        dispatch_mirror(0, m, r.normed_m)

    @dec
    def _():
        for m in range(1, micro):
            dispatch(1, m, r.cotangent)
        for m in range(1, micro):
            dispatch_mirror(1, m, r.cotangent)

    own_task = task_of(me_f)
    partner = lane_sum(when_equal(table_lane, own_task, table[0:1] + table[1:2])) - me_f
    capacity = r.capacity[0].astype(F32)
    place = iota((1, z.all_rows), 1)
    block = whole_part(place, send)
    place_rank = place - block * send
    place_half = whole_part(block, group)
    sender = here_f - (block - place_half * group)
    if z.merged:
        place_half = jnp.minimum(whole_part(place_rank, z.bound), 1.0)
        place_rank = place_rank - place_half * z.bound
    sender = base_f + jnp.where(sender < 0.0, sender + group, sender) + place_half * group
    sender = jnp.where(sender >= z.experts, sender - z.experts, sender)
    teller = me_f - iota((z.experts, 1), 0)
    teller = jnp.where(teller < 0.0, teller + z.experts, teller)
    for m in range(micro):
        told = lane_sum(jnp.where(lane == own_task, r.infos[:, INFO_COUNT + m, :], 0.0))
        count = row_sum(when_equal(teller, sender, told))
        slot = row_sum(jnp.where(teller < sender, told, 0.0)) + place_rank
        slot = jnp.where((place_rank < count) & (slot < capacity), slot, -1.0)
        r.compact[m] = when_equal(iota((slots, 1), 0), slot).astype(BF16)

    first_cross = 0
    first_out = first_cross + z.cross_blocks
    first_qkv = first_out + z.out_blocks
    first_misc = first_qkv + z.qkv_blocks

    def flat(ref, at=slice(None)):
        value = ref[:, :, at]
        return value.reshape(value.shape[0] * value.shape[1], value.shape[2])

    def store_blocks(first, left, right):
        width = 2 * LANES
        left = flat(left)
        for start in range(0, right.shape[-1], width):
            grad = dot_rows(left, flat(right, pl.ds(start, width))).astype(BF16)
            at = (first + start // LANES) * model
            r.dense[at : at + model] = grad[:, :LANES]
            r.dense[at + model : at + 2 * model] = grad[:, LANES:]

    bits = list(range(z.bits))
    lead = min(3, z.bits)
    last_stage = 2 * z.bits
    groups = []
    for group_parts in z.groups:
        made = sum(len(group) for group in groups)
        groups.append([])
        for index, (start, size) in enumerate(group_parts, made):
            turn = index % lead
            even = bits[turn:lead] + bits[:turn] + bits[lead:]
            light = bits[:2] if index % 2 == 0 else bits[:2][::-1]
            orders = (even, light + bits[2:])
            groups[-1].append(SimpleNamespace(index=index, start=start, size=size, orders=orders))

    def stride_of(part, level):
        first, second = [1 << order[level] for order in part.orders]
        return first + section * (second - first)

    def bit_of(part, level):
        return lax.rem(lax.div(me, stride_of(part, level)), 2)

    def rows_of(part, level, offset=0):
        size = part.size >> level
        at = part.start + offset * size
        for upper in range(level):
            at = at + bit_of(part, upper) * (part.size >> (upper + 1))
        return pl.ds(pl.multiple_of(at, 16), size)

    def landing(part, stage):
        return pl.ds(part.start + part.size - (part.size >> stage), part.size >> (stage + 1))

    def transfer(part, stage):
        halving = stage < z.bits
        level = stage if halving else last_stage - 1 - stage
        bit = bit_of(part, level)
        if halving:
            half = part.size >> (stage + 1)
            kept = rows_of(part, stage + 1)
            given = pl.ds(pl.multiple_of(kept.start + (1 - 2 * bit) * half, 16), half)
            source, target = (r.dense.at[given], r.partial.at[landing(part, stage)])
        else:
            source = target = r.total.at[rows_of(part, level + 1)]
        return pltpu.make_async_remote_copy(
            src_ref=source,
            dst_ref=target,
            send_sem=r.sum_send.at[part.index, stage],
            recv_sem=r.sum_recv.at[part.index, stage],
            device_id={"expert": me + (1 - 2 * bit) * stride_of(part, level)},
            device_id_type=MESH,
        )

    def step_group(group, stage):
        for part in groups[group]:
            if stage > 0:
                transfer(part, stage - 1).wait()
            if 0 < stage <= z.bits:
                rows = rows_of(part, stage)
                came = r.partial[landing(part, stage - 1)].astype(F32)
                target = r.total if stage == z.bits else r.dense
                target[rows] = (r.dense[rows].astype(F32) + came).astype(BF16)
            if stage < last_stage:
                transfer(part, stage).start()

    stages = [[0, 0], 0, 0]

    def advance_first(index):
        if stages[0][index] <= last_stage:
            if side[0] == index:
                step_group(0, stages[0][index])
            else:
                on_section(index)(lambda: step_group(0, stages[0][index]))
            stages[0][index] += 1

    def advance(group):
        if group == 0:
            advance_first(0)
            advance_first(1)
        elif stages[group] <= last_stage:
            step_group(group, stages[group])
            stages[group] += 1

    router = r.w_router[...]
    routers = router.shape[0]
    expert_lane = iota((8, routers), 1)
    sign = when_equal(expert_lane, me_f) - when_equal(expert_lane, partner)
    router_step = dot(sign.astype(BF16), router)[0:1]
    tile = 1024

    def each_tile(width, run):
        def step(index, _):
            run(pl.ds(pl.multiple_of(index * tile, tile), tile))
            return 0

        lax.fori_loop(0, width // tile, step, 0)

    def expert_forward(m):
        taken = arrived(0, m).astype(BF16)
        r.taken[m] = taken

        def up_tile(at):
            act, slope = gelu_and_slope(dot(r.taken[m], r.wup[:, at]))
            r.act[m, :, at] = act.astype(BF16)
            r.slope[m, :, at] = slope.astype(BF16)

        each_tile(z.hidden, up_tile)
        gap = lane_sum(taken.astype(F32) * router_step)
        small = jnp.exp(-jnp.abs(gap))
        large = 1.0 / (1.0 + small)
        gate = jnp.where(gap >= 0.0, large, small * large)
        r.gate[m] = gate
        r.gate_slope[m] = small * large * large

        r.expert_out[m] = dot(r.act[m], r.wdown[...]).astype(BF16)
        r.gated[m] = (gate * r.expert_out[m].astype(F32)).astype(BF16)

    def expert_backward(m):
        grad_final = arrived(1, m)
        grad_gate = lane_sum(r.expert_out[m].astype(F32) * grad_final)
        grad_gap = r.gate_slope[m] * grad_gate
        r.grad_gap[m] = grad_gap
        r.grad_out[m] = (r.gate[m] * grad_final).astype(BF16)

        def act_tile(at):
            grad_act = dot_cols(r.grad_out[m], r.wdown[at, :])
            r.grad_hidden[m, :, at] = (grad_act * r.slope[m, :, at].astype(F32)).astype(BF16)

        each_tile(z.hidden, act_tile)

        rounded = dot_cols(r.grad_hidden[m], r.wup[...]).astype(BF16).astype(F32)
        combine(1, m, (rounded + grad_gap * router_step).astype(BF16))

    loads[3].wait()
    loads[4].wait()

    @dec
    def _():
        for m in range(micro):
            expert_forward(m)
            expert_backward(m)
        for m in range(micro):
            combine(0, m, r.gated[m])
            r.grad_state[m] = r.cotangent[m].astype(F32)

    @enc
    def _():
        for m in range(micro):
            expert_forward(m)
            combine(0, m, r.gated[m])
        for m in range(micro):
            combine_mirror(0, m)
        for m in range(micro):
            layer_final = r.after_cross[m] + combine_end(0, m)
            r.layer_final[m] = layer_final
            r.layer_out[m] = layer_final.astype(BF16)
            normed_k = norm(layer_final, gain_c).astype(BF16)
            r.normed_c[m] = normed_k
            r.memory_out[m] = dot(normed_k, r.wcross[...]).astype(BF16)
            send_memory(m)
        gain_grad = jnp.zeros((1, model), F32)
        for m in range(micro):
            wait_memory(m)
            grad_normed = dot_cols(r.memory[m], r.wcross[...])
            grad_state, grad_gain = norm_back(r.layer_final[m], gain_c, grad_normed)
            gain_grad += grad_gain
            grad_final = r.cotangent[m].astype(F32) + grad_state
            r.grad_state[m] = grad_final
            r.grad_rows[m] = grad_final.astype(BF16)
            dispatch(1, m, r.grad_rows)
        for m in range(micro):
            dispatch_mirror(1, m, r.grad_rows)
        r.gain_grads[1:2] = gain_grad
        store_blocks(first_cross, r.normed_c, r.memory)
        for m in range(micro):
            expert_backward(m)
        advance_first(0)

    saves = []

    def save(source, target):
        copy = pltpu.make_async_copy(source, target, r.save_sem.at[len(saves)])
        copy.start()
        saves.append(copy)

    def up_grad(at):
        r.wup[:, at] = dot_rows(flat(r.taken), flat(r.grad_hidden, at)).astype(BF16)

    def down_grad(at):
        r.wdown[at, :] = dot_rows(flat(r.act, at), flat(r.grad_out)).astype(BF16)

    each_tile(z.hidden, up_grad)
    save(r.wup, r.up_grad)
    for m in range(micro):
        combine_mirror(1, m)
    each_tile(z.hidden, down_grad)
    save(r.wdown, r.down_grad)

    gain_grad = jnp.zeros((1, model), F32)
    for m in range(micro):
        grad_state, grad_gain = norm_back(r.after_cross[m], gain_m, combine_end(1, m))
        gain_grad += grad_gain
        r.grad_state[m] += grad_state

        @dec
        def _():
            grad_y = r.grad_state[m].astype(BF16)
            r.grad_cross[m] = grad_y
            r.grad_mix[...] = dot(grad_y, r.wcross[:, model:]).astype(BF16)

            @each_pair
            def _(pair):
                at = cols(pair)
                grad_q, grad_k, grad_v = attend_back(
                    r.cross_q[m, :, at],
                    r.memory[m, :, at],
                    r.memory[m, :, cols(pair, model)],
                    r.probs_cross[m, pair],
                    r.grad_mix[:, at],
                )
                r.grad_cross_q[m, :, at] = grad_q.astype(BF16)
                r.memory_out[m, :, at] = grad_k.astype(BF16)
                r.memory_out[m, :, cols(pair, model)] = grad_v.astype(BF16)
            send_memory(m)

    r.gain_grads[2:3] = gain_grad

    @dec
    def _():
        gain_grad = jnp.zeros((1, model), F32)
        for m in range(micro):
            grad_normed = dot_cols(r.grad_cross_q[m], r.wcross[:, :model])
            grad_state, grad_gain = norm_back(r.after_self[m], gain_c, grad_normed)
            gain_grad += grad_gain
            r.grad_state[m] += grad_state
        r.gain_grads[1:2] = gain_grad

    @dec
    def _():
        store_blocks(first_cross, r.normed_c, r.grad_cross_q)
        store_blocks(first_cross + z.out_blocks, r.grad_cross, r.cross_rows)

    advance_first(1)
    for m in range(micro):
        r.grad_self[m] = r.grad_state[m].astype(BF16)
    store_blocks(first_out, r.attn_rows, r.grad_self)
    advance(1)

    gain_grad = jnp.zeros((1, model), F32)
    for m in range(micro):
        grad_top = r.grad_state[m]
        grad_y = r.grad_self[m]
        r.grad_mix[...] = dot_cols(grad_y, r.wout[...]).astype(BF16)

        @each_pair
        def _(pair):
            grads = attend_back(
                r.qkv[m, :, cols(pair)],
                r.qkv[m, :, cols(pair, model)],
                r.qkv[m, :, cols(pair, 2 * model)],
                r.probs_self[m, pair],
                r.grad_mix[:, cols(pair)],
            )
            for third, grad in enumerate(grads):
                r.grad_qkv[m, :, cols(pair, third * model)] = grad.astype(BF16)
        grad_normed = dot_cols(r.grad_qkv[m], r.wqkv[...])
        grad_state, grad_gain = norm_back(r.inputs[m].astype(F32), gain_a, grad_normed)
        gain_grad += grad_gain
        r.inputs_grad[m] = grad_top + grad_state
    r.gain_grads[0:1] = gain_grad
    r.gain_grads[3:8] = jnp.zeros((5, model), F32)

    store_blocks(first_qkv, r.normed_a, r.grad_qkv)
    misc_row = iota((1, z.misc), 1)
    misc_sign = when_equal(misc_row, me_f) - when_equal(misc_row, partner)
    misc = jnp.zeros((z.misc, model), F32)
    for m in range(micro):
        steps = r.grad_gap[m] * misc_sign
        top = steps.astype(BF16)
        rest = (steps - top.astype(F32)).astype(BF16)
        misc += dot_rows(top, r.taken[m]) + dot_rows(rest, r.taken[m])
    place_gain = when_equal(iota((8, z.misc), 1), iota((8, z.misc), 0) + routers)
    misc += dot_rows(place_gain.astype(BF16), r.gain_grads[...].astype(BF16))
    misc_rows = [
        pl.ds(first_misc * model + index * z.misc, z.misc) for index in range(model // LANES)
    ]
    for index, rows in enumerate(misc_rows):
        r.dense[rows] = misc[:, index * LANES : (index + 1) * LANES].astype(BF16)
    used = z.blocks * model
    if used < z.dense_rows:
        r.dense[used:] = jnp.zeros((z.dense_rows - used, LANES), BF16)
    advance(2)
    advance(0)
    advance(1)

    @dec
    def _():
        for m in range(micro):
            combine_mirror(0, m)
        for m in range(micro):
            r.layer_out[m] = (r.after_cross[m] + combine_end(0, m)).astype(BF16)

    def save_blocks(target, first, count):
        for index in range(count):
            rows = pl.ds((first + index) * model, model)
            save(r.total.at[rows], target.at[:, pl.ds(index * LANES, LANES)])

    while stages[2] <= last_stage:
        if stages[0][1] <= last_stage:
            advance(0)
            if stages[0][1] > last_stage:
                save_blocks(r.cross_grad, first_cross, z.cross_blocks)
        if stages[1] <= last_stage:
            advance(1)
            if stages[1] > last_stage:
                save_blocks(r.out_grad, first_out, z.out_blocks)
        advance(2)
    save_blocks(r.qkv_grad, first_qkv, z.qkv_blocks)

    for index, rows in enumerate(misc_rows):
        sums = r.total[rows].astype(F32)
        r.router_grad[:, index * LANES : (index + 1) * LANES] = sums[:routers]
        for row in range(3):
            at = row * model + index * LANES
            r.gains_grad[:, at : at + LANES] = sums[routers + row : routers + row + 1]
    for copy in saves:
        copy.wait()

    settle_all()


def vmem_bytes(buffers):
    total = 0
    for buffer in buffers:
        if buffer.memory_space == pltpu.VMEM:
            *lead, rows, lanes = buffer.shape
            size = math.prod(lead) * round_up(rows, 8) * round_up(lanes, LANES)
            total += size * jnp.dtype(buffer.dtype).itemsize
    return min(total + 5 * 1024 * 1024, 62 * 1024 * 1024)


def run_kernel(z, arrays):
    micro, tok, model, hidden = (z.micro, z.tok, z.model, z.hidden)
    vmem = pl.BlockSpec(memory_space=pltpu.VMEM)
    hbm = pl.BlockSpec(memory_space=pl.ANY)
    inputs = dict(
        segments=(arrays.segments, vmem),
        tasks=(arrays.tasks, vmem),
        table=(arrays.table, vmem),
        capacity=(arrays.capacity, pl.BlockSpec(memory_space=pltpu.SMEM)),
        inputs=(arrays.inputs, vmem),
        cotangent=(arrays.cotangent, vmem),
        gains=(arrays.gains, vmem),
        w_router=(arrays.w_router, vmem),
        w_qkv=(arrays.w_qkv, hbm),
        w_out=(arrays.w_out, hbm),
        w_cross=(arrays.w_cross, hbm),
        w_up=(arrays.w_up, hbm),
        w_down=(arrays.w_down, hbm),
    )
    rows = (micro, tok, model)
    slot_rows = (micro, z.slots, model)
    slot_hidden = (micro, z.slots, hidden)
    outputs = dict(
        layer_out=(rows, BF16, vmem),
        inputs_grad=(rows, F32, vmem),
        gains_grad=((1, 3 * model), F32, vmem),
        router_grad=(arrays.w_router.shape, F32, vmem),
        qkv_grad=(arrays.w_qkv.shape, BF16, hbm),
        out_grad=(arrays.w_out.shape, BF16, hbm),
        cross_grad=(arrays.w_cross.shape, BF16, hbm),
        up_grad=(arrays.w_up.shape, BF16, hbm),
        down_grad=(arrays.w_down.shape, BF16, hbm),
    )
    blocks = (2, micro, z.flights, z.group, z.send, model)
    pairs = model // LANES
    dma = pltpu.SemaphoreType.DMA
    scratch = dict(
        wqkv=pltpu.VMEM(arrays.w_qkv.shape, BF16),
        wout=pltpu.VMEM(arrays.w_out.shape, BF16),
        wcross=pltpu.VMEM(arrays.w_cross.shape, BF16),
        wup=pltpu.VMEM(arrays.w_up.shape, BF16),
        wdown=pltpu.VMEM(arrays.w_down.shape, BF16),
        infos=pltpu.VMEM((z.experts, 8, LANES), F32),
        normed_a=pltpu.VMEM(rows, BF16),
        qkv=pltpu.VMEM((micro, tok, 3 * model), BF16),
        probs_self=pltpu.VMEM((micro, pairs, 2 * tok, tok), F32),
        attn_rows=pltpu.VMEM(rows, BF16),
        after_self=pltpu.VMEM(rows, F32),
        normed_c=pltpu.VMEM(rows, BF16),
        cross_q=pltpu.VMEM(rows, BF16),
        probs_cross=pltpu.VMEM((micro, pairs, 2 * tok, tok), F32),
        cross_rows=pltpu.VMEM(rows, BF16),
        memory_out=pltpu.VMEM((micro, tok, 2 * model), BF16),
        memory=pltpu.VMEM((micro, tok, 2 * model), BF16),
        after_cross=pltpu.VMEM(rows, F32),
        normed_m=pltpu.VMEM(rows, BF16),
        layer_final=pltpu.VMEM(rows, F32),
        grad_state=pltpu.VMEM(rows, F32),
        grad_rows=pltpu.VMEM(rows, BF16),
        grad_cross=pltpu.VMEM(rows, BF16),
        grad_cross_q=pltpu.VMEM(rows, BF16),
        grad_self=pltpu.VMEM(rows, BF16),
        grad_mix=pltpu.VMEM((tok, model), BF16),
        grad_qkv=pltpu.VMEM((micro, tok, 3 * model), BF16),
        gain_grads=pltpu.VMEM((8, model), F32),
        pick=pltpu.VMEM((z.halves, micro, z.half_rows, tok), BF16),
        compact=pltpu.VMEM((micro, z.slots, z.all_rows), BF16),
        rows_out=pltpu.VMEM(blocks, BF16),
        rows_in=pltpu.VMEM(blocks, BF16),
        reply_out=pltpu.VMEM(blocks, BF16),
        reply_in=pltpu.VMEM(blocks, BF16),
        mirror_rows=pltpu.VMEM((2,) + rows, BF16),
        sums_out=pltpu.VMEM((2,) + rows, BF16),
        sums_in=pltpu.VMEM((2,) + rows, BF16),
        taken=pltpu.VMEM(slot_rows, BF16),
        slope=pltpu.VMEM(slot_hidden, BF16),
        act=pltpu.VMEM(slot_hidden, BF16),
        expert_out=pltpu.VMEM(slot_rows, BF16),
        gated=pltpu.VMEM(slot_rows, BF16),
        gate=pltpu.VMEM((micro, z.slots, 1), F32),
        gate_slope=pltpu.VMEM((micro, z.slots, 1), F32),
        grad_gap=pltpu.VMEM((micro, z.slots, 1), F32),
        grad_out=pltpu.VMEM(slot_rows, BF16),
        grad_hidden=pltpu.VMEM(slot_hidden, BF16),
        dense=pltpu.VMEM((z.dense_rows, LANES), BF16),
        total=pltpu.VMEM((z.dense_rows, LANES), BF16),
        partial=pltpu.VMEM((z.dense_rows, LANES), BF16),
        load_sem=dma((5,)),
        save_sem=dma((2 + z.blocks - z.misc_blocks,)),
        info_send=dma(()),
        info_recv=dma(()),
        rows_send=dma((2, micro, z.flights)),
        rows_recv=dma((2, micro, z.flights)),
        reply_send=dma((2, micro, z.flights)),
        reply_recv=dma((2, micro, z.flights)),
        mirror_send=dma((2, micro)),
        mirror_recv=dma((2, micro)),
        sums_send=dma((2, micro)),
        sums_recv=dma((2, micro)),
        memory_send=dma((2 * micro,)),
        memory_recv=dma((2 * micro,)),
        sum_send=dma((z.parts, 2 * z.bits)),
        sum_recv=dma((z.parts, 2 * z.bits)),
    )
    names = [*inputs, *outputs, *scratch]

    def body(*refs):
        kernel_body(z, names, *refs)

    return pl.pallas_call(
        body,
        name="layer_step",
        out_shape=[jax.ShapeDtypeStruct(shape, dtype) for shape, dtype, _ in outputs.values()],
        in_specs=[spec for _, spec in inputs.values()],
        out_specs=[spec for _, _, spec in outputs.values()],
        scratch_shapes=list(scratch.values()),
        compiler_params=pltpu.CompilerParams(
            collective_id=0, has_side_effects=True, vmem_limit_bytes=vmem_bytes(scratch.values())
        ),
    )(*[value for value, _ in inputs.values()])


def widen_body(count, *refs):
    total = (len(refs) - 2) // 4
    sources, targets, came, made = [refs[i * total : (i + 1) * total] for i in range(4)]
    come_sem, go_sem = refs[4 * total :]
    loads = [pltpu.make_async_copy(sources[i], came[i], come_sem.at[i]) for i in range(total)]
    for copy in loads:
        copy.start()
    for i in range(total):
        loads[i].wait()
        if i >= count:
            pltpu.make_async_copy(came[i], targets[i], go_sem.at[i]).start()
            continue
        rows, lanes = came[i].shape
        step_rows = 1 << (min(rows, 128 * 1024 // lanes).bit_length() - 1)

        def step(index, _):
            at = pl.ds(pl.multiple_of(index * step_rows, step_rows), step_rows)
            made[i][at] = came[i][at].astype(F32)
            pltpu.make_async_copy(made[i].at[at], targets[i].at[at], go_sem.at[i]).start()
            return 0

        lax.fori_loop(0, rows // step_rows, step, 0)
    for i in range(total):
        left = made[i] if i < count else came[i]
        pltpu.make_async_copy(left, targets[i], go_sem.at[i]).wait()


def widen(narrow, passed):
    values = [*narrow, *passed]
    count = len(narrow)
    types = [F32] * count + [value.dtype for value in passed]
    hbm = pl.BlockSpec(memory_space=pltpu.HBM)
    dma = pltpu.SemaphoreType.DMA((len(values),))
    blank = pltpu.VMEM((8, LANES), F32)
    return pl.pallas_call(
        lambda *refs: widen_body(count, *refs),
        name="widen",
        out_shape=[jax.ShapeDtypeStruct(v.shape, t) for v, t in zip(values, types)],
        in_specs=[hbm] * len(values),
        out_specs=[hbm] * len(values),
        scratch_shapes=[pltpu.VMEM(value.shape, value.dtype) for value in values]
        + [pltpu.VMEM(value.shape, F32) for value in narrow]
        + [blank] * len(passed)
        + [dma, dma],
        compiler_params=pltpu.CompilerParams(vmem_limit_bytes=62 * 1024 * 1024),
    )(*values)


def shards(
    inputs,
    cotangent,
    segments,
    tasks,
    table,
    capacity,
    gains,
    w_qkv,
    w_out,
    w_cross,
    w_router,
    w_up,
    w_down,
):
    experts = lax.axis_size("expert")
    z = Sizes(inputs, w_qkv, w_cross, w_router, w_up, table, experts)
    model = z.model
    arrays = SimpleNamespace(
        segments=segments[0],
        tasks=tasks[0, :, :, 0],
        table=table[0].T,
        capacity=capacity,
        inputs=inputs[0],
        cotangent=cotangent[0],
        gains=gains.reshape(1, 3 * model),
        w_router=w_router[0].T,
        w_qkv=w_qkv[0],
        w_out=w_out[0],
        w_cross=w_cross[0],
        w_up=w_up[0, 0],
        w_down=w_down[0, 0],
    )
    *passed, qkv_grad, out_grad, cross_grad, up_grad, down_grad = run_kernel(z, arrays)
    narrow = (up_grad, down_grad, qkv_grad, cross_grad, out_grad)
    up_grad, down_grad, qkv_grad, cross_grad, out_grad, *passed = widen(narrow, passed)
    out, inputs_grad, gains_grad, router_grad = passed
    return (
        out[None],
        inputs_grad[None],
        gains_grad.reshape(1, 3, model),
        qkv_grad[None],
        out_grad[None],
        cross_grad[None],
        router_grad.T[None],
        up_grad[None, None],
        down_grad[None, None],
    )


def solution(mesh):
    in_specs = (
        P("section", None, "expert", None),
        P("section", None, "expert", None),
        P("section", None, "expert"),
        P("section", None, "expert", None),
        P("section", None, None),
        P("section"),
        P("section", None, None),
        P("section", None, None),
        P("section", None, None),
        P("section", None, None),
        P("section", None, None),
        P("section", "expert", None, None),
        P("section", "expert", None, None),
    )
    out_specs = (
        P("section", None, "expert", None),
        P("section", None, "expert", None),
        P("section", None, None),
        P("section", None, None),
        P("section", None, None),
        P("section", None, None),
        P("section", None, None),
        P("section", "expert", None, None),
        P("section", "expert", None, None),
    )
    return jax.shard_map(shards, mesh=mesh, in_specs=in_specs, out_specs=out_specs, check_vma=False)
```

```python
import math
from types import SimpleNamespace

import jax
import jax.numpy as jnp
from jax import lax
from jax.experimental import pallas as pl
from jax.experimental.pallas import tpu as pltpu
from jax.sharding import PartitionSpec as P

HEADS = 8
EPSILON = 1e-06
LANES = 128
UNROLL = 4
MESH = pl.DeviceIdType.MESH
F32 = jnp.float32
BF16 = jnp.bfloat16

INFO_TASK, INFO_RANK, INFO_COUNT = (0, 2, 4)
ROWS, REPLY, MIRROR, SUMS, MEMORY, SENT = (1000, 2000, 3000, 4000, 5000, 10000)


def round_up(value, unit):
    return -(-value // unit) * unit


def dot(left, right):
    return jnp.dot(left, right, preferred_element_type=F32)


def dot_rows(left, right):
    return lax.dot_general(left, right, (((0,), (0,)), ((), ())), preferred_element_type=F32)


def dot_cols(left, right):
    return lax.dot_general(left, right, (((1,), (1,)), ((), ())), preferred_element_type=F32)


def lane_sum(value):
    return jnp.sum(value, axis=-1, keepdims=True)


def row_sum(value):
    return jnp.sum(value, axis=0, keepdims=True)


def when_equal(left, right, value=1.0):
    return jnp.where(left == right, value, 0.0)


def iota(shape, axis):
    return lax.broadcasted_iota(jnp.int32, shape, axis).astype(F32)


def whole_part(value, unit):
    return jnp.floor((value + 0.5) * (1.0 / unit))


def inverse_rms(value):
    return lax.rsqrt(jnp.mean(value * value, axis=-1, keepdims=True) + EPSILON)


def norm(value, gain):
    return value * inverse_rms(value) * gain


def norm_back(value, gain, grad):
    scale = inverse_rms(value)
    unit = value * scale
    scaled = grad * gain
    grad_value = scale * (scaled - unit * jnp.mean(scaled * unit, axis=-1, keepdims=True))
    return grad_value, row_sum(grad * unit)


def gelu_and_slope(hidden):
    rate = math.sqrt(2.0 / math.pi)
    square = hidden * hidden
    bend = jnp.tanh(hidden * (rate + rate * 0.044715 * square))
    share = 0.5 + 0.5 * bend
    act = hidden * share
    slope = share + act * (1.0 - bend) * (rate + 3.0 * rate * 0.044715 * square)
    return act, slope


class Sizes:
    def __init__(self, inputs, w_qkv, w_cross, w_router, w_up, table, experts):
        _, self.micro, self.tok, self.model = inputs.shape
        self.hidden = w_up.shape[-1]
        self.experts = experts
        self.tasks = table.shape[1]
        self.slots = 2 * self.tok
        self.halves = 2
        self.group = experts // self.halves
        self.bound = max(2, 6 * self.tok // experts)
        self.send = round_up(self.bound, 16)
        self.merged = self.halves * self.bound <= self.send
        self.flights = 1 if self.merged else self.halves
        self.half_rows = self.group * self.send
        self.all_rows = self.flights * self.half_rows
        self.misc = round_up(w_router.shape[-1] + 3, LANES)
        self.qkv_blocks = w_qkv.shape[-1] // LANES
        self.out_blocks = self.model // LANES
        self.cross_blocks = w_cross.shape[-1] // LANES
        self.misc_blocks = self.misc // LANES
        self.blocks = self.qkv_blocks + self.out_blocks + self.cross_blocks + self.misc_blocks
        self.bits = experts.bit_length() - 1
        unit = 16 * experts
        self.groups = []
        start = 0
        for blocks, count in (
            (self.cross_blocks, 3),
            (self.out_blocks, 2),
            (self.qkv_blocks + self.misc_blocks, 6),
        ):
            units = -(-blocks * self.model // unit)
            count = min(count, units)
            group = []
            for part in range(count):
                size = (units // count + (part < units % count)) * unit
                group.append((start, size))
                start += size
            self.groups.append(group)
        self.parts = sum(len(group) for group in self.groups)
        self.dense_rows = start


def kernel_body(z, names, *refs):
    r = SimpleNamespace(**dict(zip(names, refs)))
    me = lax.axis_index("expert")
    section = lax.axis_index("section")
    tok, model, micro, group, send, slots = (z.tok, z.model, z.micro, z.group, z.send, z.slots)
    here = lax.rem(me, group)
    base = me - here
    mirror = lax.rem(me + group, z.experts)
    me_f = me.astype(F32)
    here_f = here.astype(F32)
    base_f = base.astype(F32)
    enc_f = 1.0 - section.astype(F32)

    side = [None]
    owed = {}

    def on_section(index):
        def put(run):
            side[0] = index
            pl.when(section == index)(run)
            side[0] = None

        return put

    enc, dec = (on_section(0), on_section(1))

    def wait_for(ref, sem):
        pltpu.make_async_copy(ref, ref, sem).wait()

    def owe(key, copy):
        owed[side[0], key] = copy

    def settle(key):
        found = [e for e in owed if e[1] == key and (side[0] in (None, e[0]) or e[0] is None)]
        copies = [owed.pop(entry) for entry in found]
        if side[0] is not None and found[0][0] is None:
            owed[1 - side[0], key] = copies[0]
        wait_for(*copies[0]())

    def settle_all():
        for index in (None, 0, 1):
            waits = [owed.pop(entry) for entry in list(owed) if entry[0] == index]

            def run():
                for copy in waits:
                    wait_for(*copy())

            if index is None:
                run()
            else:
                pl.when(section == index)(run)

    loads = [
        pltpu.make_async_copy(source, target, r.load_sem.at[i])
        for i, (source, target) in enumerate(
            (
                (r.w_qkv, r.wqkv),
                (r.w_out, r.wout),
                (r.w_cross, r.wcross),
                (r.w_up, r.wup),
                (r.w_down, r.wdown),
            )
        )
    ]
    for load in loads:
        load.start()

    barrier = pltpu.get_barrier_semaphore()

    def greet(step, _):
        pl.semaphore_signal(
            barrier,
            inc=1,
            device_id={"expert": lax.rem(me + step, z.experts)},
            device_id_type=MESH,
        )
        return 0

    lax.fori_loop(1, z.experts, greet, 0)
    pl.semaphore_signal(
        barrier, inc=1, device_id={"section": 1 - section}, device_id_type=MESH
    )

    seg_rows = r.segments[...].astype(F32)
    task_rows = r.tasks[...].astype(F32)
    blank = jnp.zeros((LANES - 2 * micro, LANES), F32)
    flipped = jnp.transpose(jnp.concatenate([seg_rows, task_rows, blank], axis=0))
    lane = iota((1, LANES), 1)
    earlier = jnp.where(iota((tok, tok), 0) < iota((tok, tok), 1), 1.0, 0.0)
    ranks, counts = ([], [])
    for m in range(micro):
        task_col = flipped[:, micro + m : micro + m + 1]
        ranks.append(row_sum(when_equal(task_col, task_rows[m : m + 1]) * earlier))
        counts.append(row_sum(when_equal(task_col, lane)))
    r.infos[0] = jnp.concatenate(
        [task_rows, *ranks, *counts, jnp.zeros((8 - 3 * micro, LANES), F32)], axis=0
    )

    table = r.table[...].astype(F32)
    table_lane = iota((1, z.tasks), 1)

    def task_of(expert):
        return lane_sum(
            when_equal(table[0:1], expert, table_lane) + when_equal(table[1:2], expert, table_lane)
        )

    line = iota((z.half_rows, 1), 0)
    line_block = whole_part(line, send)
    line_rank = line - line_block * send
    line_place = here_f + line_block
    line_place = jnp.where(line_place >= group, line_place - group, line_place)
    line_task = task_of(base_f + line_place)

    def fill_pick(half):
        rank_here = line_rank - (half * z.bound if z.merged else 0)
        info = r.infos[half * group]
        for m in range(micro):
            hit = (info[INFO_TASK + m : INFO_TASK + m + 1] == line_task) & (
                info[INFO_RANK + m : INFO_RANK + m + 1] == rank_here
            )
            r.pick[half, m] = jnp.where(hit, 1.0, 0.0).astype(BF16)

    fill_pick(0)

    def greet_back():
        pl.semaphore_wait(barrier, z.experts)

        def tell(step, _):
            pltpu.make_async_remote_copy(
                src_ref=r.infos.at[0],
                dst_ref=r.infos.at[step],
                send_sem=r.info_send,
                recv_sem=r.info_recv,
                device_id={"expert": lax.rem(me + step, z.experts)},
                device_id_type=MESH,
            ).start()
            return 0

        lax.fori_loop(1, z.experts, tell, 0)
        others_told = pl.ds(1, z.experts - 1)
        owe(SENT, lambda: (r.infos.at[others_told], r.info_send))
        owe(0, lambda: (r.infos.at[others_told], r.info_recv))

    def spread(way, m, half, rows, back):
        packed, landed = (
            (r.reply_out, r.reply_in) if back else (r.rows_out, r.rows_in)
        )
        send_sem, recv_sem = (
            (r.reply_send, r.reply_recv) if back else (r.rows_send, r.rows_recv)
        )
        packed[way, m, half] = rows.reshape(group, send, model)
        landed[way, m, half, 0] = rows[:send]

        def push(step, _):
            if back:
                other = lax.rem(here + group - step, group)
            else:
                other = lax.rem(here + step, group)
            pltpu.make_async_remote_copy(
                src_ref=packed.at[way, m, half, step],
                dst_ref=landed.at[way, m, half, step],
                send_sem=send_sem.at[way, m, half],
                recv_sem=recv_sem.at[way, m, half],
                device_id={"expert": base + other},
                device_id_type=MESH,
            ).start()
            return 0

        lax.fori_loop(1, group, push, 0, unroll=group <= 8)
        key = (REPLY if back else ROWS) + 100 * way + 10 * m + half
        others = pl.ds(1, group - 1)
        at = (way, m, half)
        owe(SENT + key, lambda: (packed.at[(*at, others)], send_sem.at[at]))
        owe(key, lambda: (landed.at[(*at, others)], recv_sem.at[at]))

    def ship(key, source, target, sems, device_id):
        copy = pltpu.make_async_remote_copy(
            src_ref=source(),
            dst_ref=target(),
            send_sem=sems()[0],
            recv_sem=sems()[1],
            device_id=device_id,
            device_id_type=MESH,
        )
        copy.start()
        owe(SENT + key, lambda: (source(), sems()[0]))

    def swap(key, source, target, sems):
        ship(key, source, target, sems, {"expert": mirror})
        owe(key, lambda: (target(), sems()[1]))

    def dispatch(way, m, source):
        swap(
            MIRROR + 10 * way + m,
            lambda: source.at[m],
            lambda: r.mirror_rows.at[way, m],
            lambda: (r.mirror_send.at[way, m], r.mirror_recv.at[way, m]),
        )
        if not z.merged:
            spread(way, m, 0, dot(r.pick[0, m], source[m]).astype(BF16), False)

    def dispatch_mirror(way, m, source):
        settle(MIRROR + 10 * way + m)
        rows = dot(r.pick[1, m], r.mirror_rows[way, m])
        if z.merged:
            rows += dot(r.pick[0, m], source[m])
        spread(way, m, z.flights - 1, rows.astype(BF16), False)

    def arrived(way, m):
        for half in range(z.flights):
            settle(ROWS + 100 * way + 10 * m + half)
        return dot(r.compact[m], r.rows_in[way, m].reshape(z.all_rows, model))

    def combine(way, m, rows):
        reply = dot_rows(r.compact[m], rows).astype(BF16)
        for half in reversed(range(z.flights)):
            spread(way, m, half, reply[half * z.half_rows : (half + 1) * z.half_rows], True)

    def gathered(way, m, half):
        flight = 0 if z.merged else half
        if not z.merged or half == 1:
            settle(REPLY + 100 * way + 10 * m + flight)
        return dot_rows(r.pick[half, m], r.reply_in[way, m, flight].reshape(z.half_rows, model))

    def combine_mirror(way, m):
        r.sums_out[way, m] = gathered(way, m, 1).astype(BF16)
        swap(
            SUMS + 10 * way + m,
            lambda: r.sums_out.at[way, m],
            lambda: r.sums_in.at[way, m],
            lambda: (r.sums_send.at[way, m], r.sums_recv.at[way, m]),
        )

    def combine_end(way, m):
        own = gathered(way, m, 0)
        settle(SUMS + 10 * way + m)
        return own + r.sums_in[way, m].astype(F32)

    greet_back()

    @dec
    def _():
        dispatch(1, 0, r.cotangent)
        settle(0)
        fill_pick(1)
        dispatch_mirror(1, 0, r.cotangent)

    low_lane = jnp.where(iota((1, LANES), 1) < LANES // 2, 1.0, 0.0)
    high_lane = 1.0 - low_lane
    low_bf, high_bf = (low_lane.astype(BF16), high_lane.astype(BF16))
    pairs = model // LANES
    score_scale = (model // HEADS) ** (-0.5)

    def stacked(block):
        return jnp.concatenate([block * low_bf, block * high_bf], axis=0)

    def merged(block):
        return block[:tok] * low_lane + block[tok:] * high_lane

    def attend(queries, keys, values, allowed):
        scores = dot_cols(stacked(queries), keys) * score_scale
        if allowed is not None:
            scores = jnp.where(allowed > 0.5, scores, -1000000000.0)
        top = jnp.max(scores, axis=-1, keepdims=True)
        grown = jnp.exp(scores - top)
        probs = grown / lane_sum(grown)
        return probs, merged(dot(probs.astype(BF16), values))

    def attend_back(queries, keys, values, probs, grad_mixed):
        grad_stack = stacked(grad_mixed)
        grad_probs = dot_cols(grad_stack, values)
        inner = lane_sum(probs * grad_probs)
        grad_scores = (probs * (grad_probs - inner)).astype(BF16)
        grad_queries = merged(dot(grad_scores, keys)) * score_scale
        grad_keys = dot_rows(grad_scores, stacked(queries)) * score_scale
        grad_values = dot_rows(probs.astype(BF16), grad_stack)
        return grad_queries, grad_keys, grad_values

    def cols(index, start=0):
        return pl.ds(pl.multiple_of(start + index * LANES, LANES), LANES)

    def each_pair(run):
        def step(pair, _):
            run(pair)
            return 0

        lax.fori_loop(0, pairs, step, 0, unroll=UNROLL)

    gain_a, gain_c, gain_m = [r.gains[:, i * model : (i + 1) * model] for i in range(3)]

    def enter_experts(m):
        r.normed_m[m] = norm(r.after_cross[m], gain_m).astype(BF16)
        dispatch(0, m, r.normed_m)

    loads[0].wait()
    loads[1].wait()
    for m in range(micro):
        x_in = r.inputs[m].astype(F32)
        normed_a = norm(x_in, gain_a).astype(BF16)
        r.normed_a[m] = normed_a
        r.qkv[m] = dot(normed_a, r.wqkv[...]).astype(BF16)
        causal = jnp.where(iota((tok, tok), 1) <= iota((tok, tok), 0), 1.0, enc_f)
        allowed = when_equal(flipped[:, m : m + 1], seg_rows[m : m + 1]) * causal
        allowed = jnp.concatenate([allowed, allowed], axis=0)
        @each_pair
        def _(pair):
            probs, mixed = attend(
                r.qkv[m, :, cols(pair)],
                r.qkv[m, :, cols(pair, model)],
                r.qkv[m, :, cols(pair, 2 * model)],
                allowed,
            )
            r.probs_self[m, pair] = probs
            r.attn_rows[m, :, cols(pair)] = mixed.astype(BF16)
        after_self = x_in + dot(r.attn_rows[m], r.wout[...])

        @enc
        def _():
            r.after_cross[m] = after_self
            enter_experts(m)

        @dec
        def _():
            r.after_self[m] = after_self

    loads[2].wait()

    def send_memory(m):
        index = m + micro * side[0]
        ship(
            MEMORY + index,
            lambda: r.memory_out.at[m],
            lambda: r.memory.at[m],
            lambda: (r.memory_send.at[index], r.memory_recv.at[index]),
            {"section": 1 - section},
        )

    def wait_memory(m):
        index = m + micro * (1 - side[0])
        owe(MEMORY + index, lambda: (r.memory.at[m], r.memory_recv.at[index]))
        settle(MEMORY + index)

    @enc
    def _():
        settle(0)
        fill_pick(1)

    @dec
    def _():
        for m in range(micro):
            after_self = r.after_self[m]
            normed_c = norm(after_self, gain_c).astype(BF16)
            r.normed_c[m] = normed_c
            r.cross_q[m] = dot(normed_c, r.wcross[:, :model]).astype(BF16)
            wait_memory(m)

            @each_pair
            def _(pair):
                probs, mixed = attend(
                    r.cross_q[m, :, cols(pair)],
                    r.memory[m, :, cols(pair)],
                    r.memory[m, :, cols(pair, model)],
                    None,
                )
                r.probs_cross[m, pair] = probs
                r.cross_rows[m, :, cols(pair)] = mixed.astype(BF16)

            r.after_cross[m] = after_self + dot_cols(r.cross_rows[m], r.wcross[:, model:])
            enter_experts(m)

    for m in range(micro):
        dispatch_mirror(0, m, r.normed_m)

    @dec
    def _():
        for m in range(1, micro):
            dispatch(1, m, r.cotangent)
        for m in range(1, micro):
            dispatch_mirror(1, m, r.cotangent)

    own_task = task_of(me_f)
    partner = lane_sum(when_equal(table_lane, own_task, table[0:1] + table[1:2])) - me_f
    capacity = r.capacity[0].astype(F32)
    place = iota((1, z.all_rows), 1)
    block = whole_part(place, send)
    place_rank = place - block * send
    place_half = whole_part(block, group)
    sender = here_f - (block - place_half * group)
    if z.merged:
        place_half = jnp.minimum(whole_part(place_rank, z.bound), 1.0)
        place_rank = place_rank - place_half * z.bound
    sender = base_f + jnp.where(sender < 0.0, sender + group, sender) + place_half * group
    sender = jnp.where(sender >= z.experts, sender - z.experts, sender)
    teller = me_f - iota((z.experts, 1), 0)
    teller = jnp.where(teller < 0.0, teller + z.experts, teller)
    for m in range(micro):
        told = lane_sum(jnp.where(lane == own_task, r.infos[:, INFO_COUNT + m, :], 0.0))
        count = row_sum(when_equal(teller, sender, told))
        slot = row_sum(jnp.where(teller < sender, told, 0.0)) + place_rank
        slot = jnp.where((place_rank < count) & (slot < capacity), slot, -1.0)
        r.compact[m] = when_equal(iota((slots, 1), 0), slot).astype(BF16)

    first_cross = 0
    first_out = first_cross + z.cross_blocks
    first_qkv = first_out + z.out_blocks
    first_misc = first_qkv + z.qkv_blocks

    def flat(ref, at=slice(None)):
        value = ref[:, :, at]
        return value.reshape(value.shape[0] * value.shape[1], value.shape[2])

    def store_blocks(first, left, right):
        width = 2 * LANES
        left = flat(left)
        for start in range(0, right.shape[-1], width):
            grad = dot_rows(left, flat(right, pl.ds(start, width))).astype(BF16)
            at = (first + start // LANES) * model
            r.dense[at : at + model] = grad[:, :LANES]
            r.dense[at + model : at + 2 * model] = grad[:, LANES:]

    bits = list(range(z.bits))
    lead = min(3, z.bits)
    last_stage = 2 * z.bits
    groups = []
    for group_parts in z.groups:
        made = sum(len(group) for group in groups)
        groups.append([])
        for index, (start, size) in enumerate(group_parts, made):
            turn = index % lead
            even = bits[turn:lead] + bits[:turn] + bits[lead:]
            light = bits[:2] if index % 2 == 0 else bits[:2][::-1]
            orders = (even, light + bits[2:])
            groups[-1].append(SimpleNamespace(index=index, start=start, size=size, orders=orders))

    def stride_of(part, level):
        first, second = [1 << order[level] for order in part.orders]
        return first + section * (second - first)

    def bit_of(part, level):
        return lax.rem(lax.div(me, stride_of(part, level)), 2)

    def rows_of(part, level, offset=0):
        size = part.size >> level
        at = part.start + offset * size
        for upper in range(level):
            at = at + bit_of(part, upper) * (part.size >> (upper + 1))
        return pl.ds(pl.multiple_of(at, 16), size)

    def landing(part, stage):
        return pl.ds(part.start + part.size - (part.size >> stage), part.size >> (stage + 1))

    def transfer(part, stage):
        halving = stage < z.bits
        level = stage if halving else last_stage - 1 - stage
        bit = bit_of(part, level)
        if halving:
            half = part.size >> (stage + 1)
            kept = rows_of(part, stage + 1)
            given = pl.ds(pl.multiple_of(kept.start + (1 - 2 * bit) * half, 16), half)
            source, target = (r.dense.at[given], r.partial.at[landing(part, stage)])
        else:
            source = target = r.total.at[rows_of(part, level + 1)]
        return pltpu.make_async_remote_copy(
            src_ref=source,
            dst_ref=target,
            send_sem=r.sum_send.at[part.index, stage],
            recv_sem=r.sum_recv.at[part.index, stage],
            device_id={"expert": me + (1 - 2 * bit) * stride_of(part, level)},
            device_id_type=MESH,
        )

    def step_group(group, stage):
        for part in groups[group]:
            if stage > 0:
                transfer(part, stage - 1).wait()
            if 0 < stage <= z.bits:
                rows = rows_of(part, stage)
                came = r.partial[landing(part, stage - 1)].astype(F32)
                target = r.total if stage == z.bits else r.dense
                target[rows] = (r.dense[rows].astype(F32) + came).astype(BF16)
            if stage < last_stage:
                transfer(part, stage).start()

    stages = [[0, 0], 0, 0]

    def advance_first(index):
        if stages[0][index] <= last_stage:
            if side[0] == index:
                step_group(0, stages[0][index])
            else:
                on_section(index)(lambda: step_group(0, stages[0][index]))
            stages[0][index] += 1

    def advance(group):
        if group == 0:
            advance_first(0)
            advance_first(1)
        elif stages[group] <= last_stage:
            step_group(group, stages[group])
            stages[group] += 1

    router = r.w_router[...]
    routers = router.shape[0]
    expert_lane = iota((8, routers), 1)
    sign = when_equal(expert_lane, me_f) - when_equal(expert_lane, partner)
    router_step = dot(sign.astype(BF16), router)[0:1]
    tile = 1024

    def each_tile(width, run):
        def step(index, _):
            run(pl.ds(pl.multiple_of(index * tile, tile), tile))
            return 0

        lax.fori_loop(0, width // tile, step, 0)

    def expert_forward(m):
        taken = arrived(0, m).astype(BF16)
        r.taken[m] = taken

        def up_tile(at):
            act, slope = gelu_and_slope(dot(r.taken[m], r.wup[:, at]))
            r.act[m, :, at] = act.astype(BF16)
            r.slope[m, :, at] = slope.astype(BF16)

        each_tile(z.hidden, up_tile)
        gap = lane_sum(taken.astype(F32) * router_step)
        small = jnp.exp(-jnp.abs(gap))
        large = 1.0 / (1.0 + small)
        gate = jnp.where(gap >= 0.0, large, small * large)
        r.gate[m] = gate
        r.gate_slope[m] = small * large * large

        r.expert_out[m] = dot(r.act[m], r.wdown[...]).astype(BF16)
        r.gated[m] = (gate * r.expert_out[m].astype(F32)).astype(BF16)

    def expert_backward(m):
        grad_final = arrived(1, m)
        grad_gate = lane_sum(r.expert_out[m].astype(F32) * grad_final)
        grad_gap = r.gate_slope[m] * grad_gate
        r.grad_gap[m] = grad_gap
        r.grad_out[m] = (r.gate[m] * grad_final).astype(BF16)

        def act_tile(at):
            grad_act = dot_cols(r.grad_out[m], r.wdown[at, :])
            r.grad_hidden[m, :, at] = (grad_act * r.slope[m, :, at].astype(F32)).astype(BF16)

        each_tile(z.hidden, act_tile)

        rounded = dot_cols(r.grad_hidden[m], r.wup[...]).astype(BF16).astype(F32)
        combine(1, m, (rounded + grad_gap * router_step).astype(BF16))

    loads[3].wait()
    loads[4].wait()

    @dec
    def _():
        for m in range(micro):
            expert_forward(m)
            expert_backward(m)
        for m in range(micro):
            combine(0, m, r.gated[m])
            r.grad_state[m] = r.cotangent[m].astype(F32)

    @enc
    def _():
        for m in range(micro):
            expert_forward(m)
            combine(0, m, r.gated[m])
        for m in range(micro):
            combine_mirror(0, m)
        for m in range(micro):
            layer_final = r.after_cross[m] + combine_end(0, m)
            r.layer_final[m] = layer_final
            r.layer_out[m] = layer_final.astype(BF16)
            normed_k = norm(layer_final, gain_c).astype(BF16)
            r.normed_c[m] = normed_k
            r.memory_out[m] = dot(normed_k, r.wcross[...]).astype(BF16)
            send_memory(m)
        gain_grad = jnp.zeros((1, model), F32)
        for m in range(micro):
            wait_memory(m)
            grad_normed = dot_cols(r.memory[m], r.wcross[...])
            grad_state, grad_gain = norm_back(r.layer_final[m], gain_c, grad_normed)
            gain_grad += grad_gain
            grad_final = r.cotangent[m].astype(F32) + grad_state
            r.grad_state[m] = grad_final
            r.grad_rows[m] = grad_final.astype(BF16)
            dispatch(1, m, r.grad_rows)
        for m in range(micro):
            dispatch_mirror(1, m, r.grad_rows)
        r.gain_grads[1:2] = gain_grad
        store_blocks(first_cross, r.normed_c, r.memory)
        for m in range(micro):
            expert_backward(m)
        advance_first(0)

    saves = []

    def save(source, target):
        copy = pltpu.make_async_copy(source, target, r.save_sem.at[len(saves)])
        copy.start()
        saves.append(copy)

    def up_grad(at):
        r.wup[:, at] = dot_rows(flat(r.taken), flat(r.grad_hidden, at)).astype(BF16)

    def down_grad(at):
        r.wdown[at, :] = dot_rows(flat(r.act, at), flat(r.grad_out)).astype(BF16)

    each_tile(z.hidden, up_grad)
    save(r.wup, r.up_grad)
    for m in range(micro):
        combine_mirror(1, m)
    each_tile(z.hidden, down_grad)
    save(r.wdown, r.down_grad)

    gain_grad = jnp.zeros((1, model), F32)
    for m in range(micro):
        grad_state, grad_gain = norm_back(r.after_cross[m], gain_m, combine_end(1, m))
        gain_grad += grad_gain
        r.grad_state[m] += grad_state

        @dec
        def _():
            grad_y = r.grad_state[m].astype(BF16)
            r.grad_cross[m] = grad_y
            r.grad_mix[...] = dot(grad_y, r.wcross[:, model:]).astype(BF16)

            @each_pair
            def _(pair):
                at = cols(pair)
                grad_q, grad_k, grad_v = attend_back(
                    r.cross_q[m, :, at],
                    r.memory[m, :, at],
                    r.memory[m, :, cols(pair, model)],
                    r.probs_cross[m, pair],
                    r.grad_mix[:, at],
                )
                r.grad_cross_q[m, :, at] = grad_q.astype(BF16)
                r.memory_out[m, :, at] = grad_k.astype(BF16)
                r.memory_out[m, :, cols(pair, model)] = grad_v.astype(BF16)
            send_memory(m)

    r.gain_grads[2:3] = gain_grad

    @dec
    def _():
        gain_grad = jnp.zeros((1, model), F32)
        for m in range(micro):
            grad_normed = dot_cols(r.grad_cross_q[m], r.wcross[:, :model])
            grad_state, grad_gain = norm_back(r.after_self[m], gain_c, grad_normed)
            gain_grad += grad_gain
            r.grad_state[m] += grad_state
        r.gain_grads[1:2] = gain_grad

    @dec
    def _():
        store_blocks(first_cross, r.normed_c, r.grad_cross_q)
        store_blocks(first_cross + z.out_blocks, r.grad_cross, r.cross_rows)

    advance_first(1)
    for m in range(micro):
        r.grad_self[m] = r.grad_state[m].astype(BF16)
    store_blocks(first_out, r.attn_rows, r.grad_self)
    advance(1)

    gain_grad = jnp.zeros((1, model), F32)
    for m in range(micro):
        grad_top = r.grad_state[m]
        grad_y = r.grad_self[m]
        r.grad_mix[...] = dot_cols(grad_y, r.wout[...]).astype(BF16)

        @each_pair
        def _(pair):
            grads = attend_back(
                r.qkv[m, :, cols(pair)],
                r.qkv[m, :, cols(pair, model)],
                r.qkv[m, :, cols(pair, 2 * model)],
                r.probs_self[m, pair],
                r.grad_mix[:, cols(pair)],
            )
            for third, grad in enumerate(grads):
                r.grad_qkv[m, :, cols(pair, third * model)] = grad.astype(BF16)
        grad_normed = dot_cols(r.grad_qkv[m], r.wqkv[...])
        grad_state, grad_gain = norm_back(r.inputs[m].astype(F32), gain_a, grad_normed)
        gain_grad += grad_gain
        r.inputs_grad[m] = grad_top + grad_state
    r.gain_grads[0:1] = gain_grad
    r.gain_grads[3:8] = jnp.zeros((5, model), F32)

    store_blocks(first_qkv, r.normed_a, r.grad_qkv)
    misc_row = iota((1, z.misc), 1)
    misc_sign = when_equal(misc_row, me_f) - when_equal(misc_row, partner)
    misc = jnp.zeros((z.misc, model), F32)
    for m in range(micro):
        steps = r.grad_gap[m] * misc_sign
        top = steps.astype(BF16)
        rest = (steps - top.astype(F32)).astype(BF16)
        misc += dot_rows(top, r.taken[m]) + dot_rows(rest, r.taken[m])
    place_gain = when_equal(iota((8, z.misc), 1), iota((8, z.misc), 0) + routers)
    misc += dot_rows(place_gain.astype(BF16), r.gain_grads[...].astype(BF16))
    misc_rows = [
        pl.ds(first_misc * model + index * z.misc, z.misc) for index in range(model // LANES)
    ]
    for index, rows in enumerate(misc_rows):
        r.dense[rows] = misc[:, index * LANES : (index + 1) * LANES].astype(BF16)
    used = z.blocks * model
    if used < z.dense_rows:
        r.dense[used:] = jnp.zeros((z.dense_rows - used, LANES), BF16)
    advance(2)
    advance(0)
    advance(1)

    @dec
    def _():
        for m in range(micro):
            combine_mirror(0, m)
        for m in range(micro):
            r.layer_out[m] = (r.after_cross[m] + combine_end(0, m)).astype(BF16)

    def save_blocks(target, first, count):
        for index in range(count):
            rows = pl.ds((first + index) * model, model)
            save(r.total.at[rows], target.at[:, pl.ds(index * LANES, LANES)])

    while stages[2] <= last_stage:
        if stages[0][1] <= last_stage:
            advance(0)
            if stages[0][1] > last_stage:
                save_blocks(r.cross_grad, first_cross, z.cross_blocks)
        if stages[1] <= last_stage:
            advance(1)
            if stages[1] > last_stage:
                save_blocks(r.out_grad, first_out, z.out_blocks)
        advance(2)
    save_blocks(r.qkv_grad, first_qkv, z.qkv_blocks)

    for index, rows in enumerate(misc_rows):
        sums = r.total[rows].astype(F32)
        r.router_grad[:, index * LANES : (index + 1) * LANES] = sums[:routers]
        for row in range(3):
            at = row * model + index * LANES
            r.gains_grad[:, at : at + LANES] = sums[routers + row : routers + row + 1]
    for copy in saves:
        copy.wait()

    settle_all()


def vmem_bytes(buffers):
    total = 0
    for buffer in buffers:
        if buffer.memory_space == pltpu.VMEM:
            *lead, rows, lanes = buffer.shape
            size = math.prod(lead) * round_up(rows, 8) * round_up(lanes, LANES)
            total += size * jnp.dtype(buffer.dtype).itemsize
    return min(total + 5 * 1024 * 1024, 62 * 1024 * 1024)


def run_kernel(z, arrays):
    micro, tok, model, hidden = (z.micro, z.tok, z.model, z.hidden)
    vmem = pl.BlockSpec(memory_space=pltpu.VMEM)
    hbm = pl.BlockSpec(memory_space=pl.ANY)
    inputs = dict(
        segments=(arrays.segments, vmem),
        tasks=(arrays.tasks, vmem),
        table=(arrays.table, vmem),
        capacity=(arrays.capacity, pl.BlockSpec(memory_space=pltpu.SMEM)),
        inputs=(arrays.inputs, vmem),
        cotangent=(arrays.cotangent, vmem),
        gains=(arrays.gains, vmem),
        w_router=(arrays.w_router, vmem),
        w_qkv=(arrays.w_qkv, hbm),
        w_out=(arrays.w_out, hbm),
        w_cross=(arrays.w_cross, hbm),
        w_up=(arrays.w_up, hbm),
        w_down=(arrays.w_down, hbm),
    )
    rows = (micro, tok, model)
    slot_rows = (micro, z.slots, model)
    slot_hidden = (micro, z.slots, hidden)
    outputs = dict(
        layer_out=(rows, BF16, vmem),
        inputs_grad=(rows, F32, vmem),
        gains_grad=((1, 3 * model), F32, vmem),
        router_grad=(arrays.w_router.shape, F32, vmem),
        qkv_grad=(arrays.w_qkv.shape, BF16, hbm),
        out_grad=(arrays.w_out.shape, BF16, hbm),
        cross_grad=(arrays.w_cross.shape, BF16, hbm),
        up_grad=(arrays.w_up.shape, BF16, hbm),
        down_grad=(arrays.w_down.shape, BF16, hbm),
    )
    blocks = (2, micro, z.flights, z.group, z.send, model)
    pairs = model // LANES
    dma = pltpu.SemaphoreType.DMA
    scratch = dict(
        wqkv=pltpu.VMEM(arrays.w_qkv.shape, BF16),
        wout=pltpu.VMEM(arrays.w_out.shape, BF16),
        wcross=pltpu.VMEM(arrays.w_cross.shape, BF16),
        wup=pltpu.VMEM(arrays.w_up.shape, BF16),
        wdown=pltpu.VMEM(arrays.w_down.shape, BF16),
        infos=pltpu.VMEM((z.experts, 8, LANES), F32),
        normed_a=pltpu.VMEM(rows, BF16),
        qkv=pltpu.VMEM((micro, tok, 3 * model), BF16),
        probs_self=pltpu.VMEM((micro, pairs, 2 * tok, tok), F32),
        attn_rows=pltpu.VMEM(rows, BF16),
        after_self=pltpu.VMEM(rows, F32),
        normed_c=pltpu.VMEM(rows, BF16),
        cross_q=pltpu.VMEM(rows, BF16),
        probs_cross=pltpu.VMEM((micro, pairs, 2 * tok, tok), F32),
        cross_rows=pltpu.VMEM(rows, BF16),
        memory_out=pltpu.VMEM((micro, tok, 2 * model), BF16),
        memory=pltpu.VMEM((micro, tok, 2 * model), BF16),
        after_cross=pltpu.VMEM(rows, F32),
        normed_m=pltpu.VMEM(rows, BF16),
        layer_final=pltpu.VMEM(rows, F32),
        grad_state=pltpu.VMEM(rows, F32),
        grad_rows=pltpu.VMEM(rows, BF16),
        grad_cross=pltpu.VMEM(rows, BF16),
        grad_cross_q=pltpu.VMEM(rows, BF16),
        grad_self=pltpu.VMEM(rows, BF16),
        grad_mix=pltpu.VMEM((tok, model), BF16),
        grad_qkv=pltpu.VMEM((micro, tok, 3 * model), BF16),
        gain_grads=pltpu.VMEM((8, model), F32),
        pick=pltpu.VMEM((z.halves, micro, z.half_rows, tok), BF16),
        compact=pltpu.VMEM((micro, z.slots, z.all_rows), BF16),
        rows_out=pltpu.VMEM(blocks, BF16),
        rows_in=pltpu.VMEM(blocks, BF16),
        reply_out=pltpu.VMEM(blocks, BF16),
        reply_in=pltpu.VMEM(blocks, BF16),
        mirror_rows=pltpu.VMEM((2,) + rows, BF16),
        sums_out=pltpu.VMEM((2,) + rows, BF16),
        sums_in=pltpu.VMEM((2,) + rows, BF16),
        taken=pltpu.VMEM(slot_rows, BF16),
        slope=pltpu.VMEM(slot_hidden, BF16),
        act=pltpu.VMEM(slot_hidden, BF16),
        expert_out=pltpu.VMEM(slot_rows, BF16),
        gated=pltpu.VMEM(slot_rows, BF16),
        gate=pltpu.VMEM((micro, z.slots, 1), F32),
        gate_slope=pltpu.VMEM((micro, z.slots, 1), F32),
        grad_gap=pltpu.VMEM((micro, z.slots, 1), F32),
        grad_out=pltpu.VMEM(slot_rows, BF16),
        grad_hidden=pltpu.VMEM(slot_hidden, BF16),
        dense=pltpu.VMEM((z.dense_rows, LANES), BF16),
        total=pltpu.VMEM((z.dense_rows, LANES), BF16),
        partial=pltpu.VMEM((z.dense_rows, LANES), BF16),
        load_sem=dma((5,)),
        save_sem=dma((2 + z.blocks - z.misc_blocks,)),
        info_send=dma(()),
        info_recv=dma(()),
        rows_send=dma((2, micro, z.flights)),
        rows_recv=dma((2, micro, z.flights)),
        reply_send=dma((2, micro, z.flights)),
        reply_recv=dma((2, micro, z.flights)),
        mirror_send=dma((2, micro)),
        mirror_recv=dma((2, micro)),
        sums_send=dma((2, micro)),
        sums_recv=dma((2, micro)),
        memory_send=dma((2 * micro,)),
        memory_recv=dma((2 * micro,)),
        sum_send=dma((z.parts, 2 * z.bits)),
        sum_recv=dma((z.parts, 2 * z.bits)),
    )
    names = [*inputs, *outputs, *scratch]

    def body(*refs):
        kernel_body(z, names, *refs)

    return pl.pallas_call(
        body,
        name="layer_step",
        out_shape=[jax.ShapeDtypeStruct(shape, dtype) for shape, dtype, _ in outputs.values()],
        in_specs=[spec for _, spec in inputs.values()],
        out_specs=[spec for _, _, spec in outputs.values()],
        scratch_shapes=list(scratch.values()),
        compiler_params=pltpu.CompilerParams(
            collective_id=0, has_side_effects=True, vmem_limit_bytes=vmem_bytes(scratch.values())
        ),
    )(*[value for value, _ in inputs.values()])


def widen_body(count, *refs):
    total = (len(refs) - 2) // 4
    sources, targets, came, made = [refs[i * total : (i + 1) * total] for i in range(4)]
    come_sem, go_sem = refs[4 * total :]
    loads = [pltpu.make_async_copy(sources[i], came[i], come_sem.at[i]) for i in range(total)]
    for copy in loads:
        copy.start()
    for i in range(total):
        loads[i].wait()
        if i >= count:
            pltpu.make_async_copy(came[i], targets[i], go_sem.at[i]).start()
            continue
        rows, lanes = came[i].shape
        step_rows = 1 << (min(rows, 128 * 1024 // lanes).bit_length() - 1)

        def step(index, _):
            at = pl.ds(pl.multiple_of(index * step_rows, step_rows), step_rows)
            made[i][at] = came[i][at].astype(F32)
            pltpu.make_async_copy(made[i].at[at], targets[i].at[at], go_sem.at[i]).start()
            return 0

        lax.fori_loop(0, rows // step_rows, step, 0)
    for i in range(total):
        left = made[i] if i < count else came[i]
        pltpu.make_async_copy(left, targets[i], go_sem.at[i]).wait()


def widen(narrow, passed):
    values = [*narrow, *passed]
    count = len(narrow)
    types = [F32] * count + [value.dtype for value in passed]
    hbm = pl.BlockSpec(memory_space=pltpu.HBM)
    dma = pltpu.SemaphoreType.DMA((len(values),))
    blank = pltpu.VMEM((8, LANES), F32)
    return pl.pallas_call(
        lambda *refs: widen_body(count, *refs),
        name="widen",
        out_shape=[jax.ShapeDtypeStruct(v.shape, t) for v, t in zip(values, types)],
        in_specs=[hbm] * len(values),
        out_specs=[hbm] * len(values),
        scratch_shapes=[pltpu.VMEM(value.shape, value.dtype) for value in values]
        + [pltpu.VMEM(value.shape, F32) for value in narrow]
        + [blank] * len(passed)
        + [dma, dma],
        compiler_params=pltpu.CompilerParams(vmem_limit_bytes=62 * 1024 * 1024),
    )(*values)


def shards(
    inputs,
    cotangent,
    segments,
    tasks,
    table,
    capacity,
    gains,
    w_qkv,
    w_out,
    w_cross,
    w_router,
    w_up,
    w_down,
):
    experts = lax.axis_size("expert")
    z = Sizes(inputs, w_qkv, w_cross, w_router, w_up, table, experts)
    model = z.model
    arrays = SimpleNamespace(
        segments=segments[0],
        tasks=tasks[0, :, :, 0],
        table=table[0].T,
        capacity=capacity,
        inputs=inputs[0],
        cotangent=cotangent[0],
        gains=gains.reshape(1, 3 * model),
        w_router=w_router[0].T,
        w_qkv=w_qkv[0],
        w_out=w_out[0],
        w_cross=w_cross[0],
        w_up=w_up[0, 0],
        w_down=w_down[0, 0],
    )
    *passed, qkv_grad, out_grad, cross_grad, up_grad, down_grad = run_kernel(z, arrays)
    narrow = (out_grad, cross_grad, qkv_grad, up_grad, down_grad)
    out_grad, cross_grad, qkv_grad, up_grad, down_grad, *passed = widen(narrow, passed)
    out, inputs_grad, gains_grad, router_grad = passed
    return (
        out[None],
        inputs_grad[None],
        gains_grad.reshape(1, 3, model),
        qkv_grad[None],
        out_grad[None],
        cross_grad[None],
        router_grad.T[None],
        up_grad[None, None],
        down_grad[None, None],
    )


def solution(mesh):
    in_specs = (
        P("section", None, "expert", None),
        P("section", None, "expert", None),
        P("section", None, "expert"),
        P("section", None, "expert", None),
        P("section", None, None),
        P("section"),
        P("section", None, None),
        P("section", None, None),
        P("section", None, None),
        P("section", None, None),
        P("section", None, None),
        P("section", "expert", None, None),
        P("section", "expert", None, None),
    )
    out_specs = (
        P("section", None, "expert", None),
        P("section", None, "expert", None),
        P("section", None, None),
        P("section", None, None),
        P("section", None, None),
        P("section", None, None),
        P("section", None, None),
        P("section", "expert", None, None),
        P("section", "expert", None, None),
    )
    return jax.shard_map(shards, mesh=mesh, in_specs=in_specs, out_specs=out_specs, check_vma=False)
```
